32 devices in a mesh: expert: 8 (over y, x, core), wshard: 4 (over z).
Axes of the slice: x: 2, y: 2, z: 4, core: 2. Of those that a mesh axis runs over, the one named last changes fastest.
Arguments:
- tokens: bfloat16 [4096, 2048], P(('expert', 'wshard')), may hold values from -6 to 6
- attention_norm: float32 [2048], P(('expert', 'wshard')), may hold values from 0.5 to 1.5
- query_weight: float32 [2048, 3072], P(('expert', 'wshard')), may hold values from -0.1875 to 0.1875
- latent_down: float32 [2048, 576], P(('expert', 'wshard')), may hold values from -0.125 to 0.125
- latent_norm: float32 [512], P(('expert', 'wshard')), may hold values from 0.5 to 1.5
- latent_up: float32 [512, 4096], P(('expert', 'wshard')), may hold values from -0.25 to 0.25
- output_weight: float32 [2048, 2048], P(('expert', 'wshard')), may hold values from -1 to 1
- post_norm: float32 [2048], P(('expert', 'wshard')), may hold values from 0.5 to 1.5
- shared_gate: float32 [2048, 2816], P(('expert', 'wshard')), may hold values from -0.125 to 0.125
- shared_up: float32 [2048, 2816], P(('expert', 'wshard')), may hold values from -0.125 to 0.125
- shared_down: float32 [2816, 2048], P(('expert', 'wshard')), may hold values from -0.109375 to 0.109375
- router_weight: float32 [2048, 16], P(('expert', 'wshard')), may hold values from -0.0625 to 0.0625
- expert_gate: bfloat16 [16, 2048, 1408], P('expert', None, 'wshard'), may hold values from -0.125 to 0.125
- expert_up: bfloat16 [16, 2048, 1408], P('expert', None, 'wshard'), may hold values from -0.125 to 0.125
- expert_down: bfloat16 [16, 1408, 2048], P('expert', 'wshard'), may hold values from -1 to 1
- image_piece_index: int32 [4096], P(('expert', 'wshard')), may hold values from 0 to 16, as said below
- routes: int32 [4096, 6], P(('expert', 'wshard')), may hold values from 0 to 15, all different within a row
- cotangent: bfloat16 [4096, 2048], P(('expert', 'wshard')), may hold values from -6 to 6
Outputs:
- layer_out: bfloat16 [4096, 2048], P(('expert', 'wshard'))
- tokens_grad: float32 [4096, 2048], P(('expert', 'wshard'))
- attention_norm_grad: float32 [2048], P(('expert', 'wshard'))
- query_weight_grad: float32 [2048, 3072], P(('expert', 'wshard'))
- latent_down_grad: float32 [2048, 576], P(('expert', 'wshard'))
- latent_norm_grad: float32 [512], P(('expert', 'wshard'))
- latent_up_grad: float32 [512, 4096], P(('expert', 'wshard'))
- output_weight_grad: float32 [2048, 2048], P(('expert', 'wshard'))
- post_norm_grad: float32 [2048], P(('expert', 'wshard'))
- shared_gate_grad: float32 [2048, 2816], P(('expert', 'wshard'))
- shared_up_grad: float32 [2048, 2816], P(('expert', 'wshard'))
- shared_down_grad: float32 [2816, 2048], P(('expert', 'wshard'))
- router_weight_grad: float32 [2048, 16], P(('expert', 'wshard'))
- expert_gate_grad: float32 [16, 2048, 1408], P('expert', None, 'wshard')
- expert_up_grad: float32 [16, 2048, 1408], P('expert', None, 'wshard')
- expert_down_grad: float32 [16, 1408, 2048], P('expert', 'wshard')
The draws below stay inside these ranges and needn't reach their ends.
Inputs may be any that keep to these rules, and one draw needn't show every extreme that they name: `image_piece_index`: tokens come in aligned blocks of 256; all tokens of a block carry the same id, 0 for text or 1 + the block's index among all tokens for an image piece; the last block is an image piece. `routes`: each row names 6 different experts.
All inputs are finite; a program needn't handle non-finite values.
Results may differ from the reference program's by a relative error of at most 0.022.
Values may be sent and summed in bfloat16 or wider, within the bound.
No kernel may reach another device: no remote copies, remote signals or barrier semaphores. Data moves between devices by JAX's collectives and lax.ppermute only.
A program may use at most 576 MiB of HBM per device.

```python
import jax
import jax.numpy as jnp
from jax import lax

D = 2048
H = 16
DN = 128
DR = 64
DV = 128
KVR = 512
FFE = 1408
TOPK = 6
TOK_DEV = 128
PIECE = 256
FFS = 2816
EXPERTS = 16
TOKENS = 4096
SEQ = 1024
CAP = 64


def draw_image_piece_index(key, part):
    block_count = TOKENS // PIECE
    chosen = jax.random.randint(key, (block_count,), 0, 5)
    block_ids = jnp.arange(block_count, dtype=jnp.int32)
    is_image = (chosen < 2) | (block_ids == block_count - 1)
    labels = jnp.where(is_image, block_ids + 1, 0).astype(jnp.int32)
    return jnp.repeat(labels, PIECE).astype(jnp.int32)


def level_of(stream_key, dims, split, least, largest):
    loudness, own = 1.0, jax.random.fold_in(stream_key, 6)
    for dim, blocks in split:
        steps = jnp.exp(jax.random.uniform(jax.random.fold_in(own, dim), (blocks,), jnp.float32, least / len(split), largest / len(split)))
        loudness = loudness * jnp.repeat(steps, dims[dim] // blocks).reshape([-1 if axis == dim else 1 for axis in range(len(dims))])
    return loudness


def choose_distinct(key, rows, number_of, top, lift):
    sequence = jax.random.permutation(jax.random.fold_in(key, 1), number_of)
    favour = sequence
    for power in range(3):
        favour = favour * favour // number_of
    favour = favour * lift // number_of
    lots = jax.random.randint(jax.random.fold_in(key, 2), (rows, number_of), 0, 4096) + favour
    holders = jax.random.permutation(jax.random.fold_in(key, 3), rows)[jnp.arange(number_of) % rows]
    lots = jnp.where(jnp.arange(rows)[:, None] == holders[None, :], 1 << 14, lots)
    priority = lots * number_of + jnp.arange(number_of)
    return lax.top_k(priority.astype(jnp.int32), top)[1].astype(jnp.int32)


def bell_draw(own_key, dims, deviation, bound, cuts=(), held_as=jnp.bfloat16):
    values = jax.random.normal(own_key, dims, jnp.float32) * deviation
    if len(cuts) > 0:
        values = level_of(own_key, dims, cuts, -0.22, 0.18) * values
    return jnp.clip(values, min=-bound, max=bound).astype(held_as)


def setup_inputs(seed: int = 0) -> dict:
    seeds = jax.random.split(jax.random.key(seed), 19)
    tokens = bell_draw(seeds[0], (TOKENS, D), 1.0, 6.0, ((0, 32),))
    attention_norm = jnp.clip(1.0 + 0.1 * jax.random.normal(seeds[1], (D,), jnp.float32), 0.5, 1.5)
    query_weight = bell_draw(seeds[2], (D, H * (DN + DR)), (D // 2) ** -0.5, 0.1875, ((0, 32),), jnp.float32)
    latent_down = bell_draw(seeds[3], (D, KVR + DR), D ** -0.5, 0.125, ((0, 32),), jnp.float32)
    latent_norm = jnp.clip(1.0 + 0.1 * jax.random.normal(seeds[4], (KVR,), jnp.float32), 0.5, 1.5)
    latent_up = bell_draw(seeds[5], (KVR, H * (DN + DV)), KVR ** -0.5, 0.25, ((0, 32),), jnp.float32)
    output_weight = bell_draw(seeds[6], (H * DV, D), (H * DV // 64) ** -0.5, 1.0, ((0, 32),), jnp.float32)
    post_norm = jnp.clip(1.0 + 0.1 * jax.random.normal(seeds[7], (D,), jnp.float32), 0.5, 1.5)
    shared_gate = bell_draw(seeds[8], (D, FFS), D ** -0.5, 0.125, ((0, 32),), jnp.float32)
    shared_up = bell_draw(seeds[9], (D, FFS), D ** -0.5, 0.125, ((0, 32),), jnp.float32)
    shared_down = bell_draw(seeds[10], (FFS, D), FFS ** -0.5, 0.109375, ((0, 32),), jnp.float32)
    router_weight = bell_draw(seeds[11], (D, EXPERTS), (4 * D) ** -0.5, 0.0625, ((0, 32),), jnp.float32)
    expert_gate = bell_draw(seeds[12], (EXPERTS, D, FFE), D ** -0.5, 0.125, ((0, 8), (2, 4)))
    expert_up = bell_draw(seeds[13], (EXPERTS, D, FFE), D ** -0.5, 0.125, ((0, 8), (2, 4)))
    expert_down = bell_draw(seeds[14], (EXPERTS, FFE, D), (max(1, FFE * TOPK // (EXPERTS * EXPERTS))) ** -0.5, 1.0, ((0, 8), (1, 4)))
    image_piece_index = draw_image_piece_index(jax.random.fold_in(seeds[18], 71), 0)
    routes = choose_distinct(seeds[16], TOKENS, EXPERTS, TOPK, 3072)
    cotangent = bell_draw(seeds[17], (TOKENS, D), 1.0, 6.0, ((0, 32),))
    return {"tokens": tokens, "attention_norm": attention_norm, "query_weight": query_weight, "latent_down": latent_down, "latent_norm": latent_norm, "latent_up": latent_up, "output_weight": output_weight, "post_norm": post_norm, "shared_gate": shared_gate, "shared_up": shared_up, "shared_down": shared_down, "router_weight": router_weight, "expert_gate": expert_gate, "expert_up": expert_up, "expert_down": expert_down, "image_piece_index": image_piece_index, "routes": routes, "cotangent": cotangent}


EPSILON = 1e-06
ROPE_BASE = 10000.0
NEGATIVE = -1e+30
HIGHEST = lax.Precision.HIGHEST

@jax.custom_vjp
def low(v):
    return lax.optimization_barrier(v.astype(jnp.bfloat16)).astype(jnp.float32)

@jax.custom_vjp
def low_back(v):
    return v

def low_keep(v):
    return (low(v), None)

def low_pass(kept, grad):
    return (grad,)

def back_keep(v):
    return (v, None)

def back_low(kept, grad):
    return (low(grad),)
low.defvjp(low_keep, low_pass)
low_back.defvjp(back_keep, back_low)

def rms_scale(values, norm_gain):
    mean_square = lax.optimization_barrier(jnp.mean(values * values, axis=-1, keepdims=True))
    return values * lax.rsqrt(mean_square + EPSILON) * norm_gain

def rope_tables(positions, width):
    half_width = width // 2
    frequency = ROPE_BASE ** (-2.0 * jnp.arange(half_width, dtype=jnp.float32) / width)
    angles = positions.astype(jnp.float32)[:, None] * frequency[None, :]
    return (jnp.cos(angles), jnp.sin(angles))

def rotate(values, cosine, sine_table):
    half_width = values.shape[-1] // 2
    first_half = values[..., :half_width]
    second_half = values[..., half_width:]
    return jnp.concatenate([first_half * cosine - second_half * sine_table, second_half * cosine + first_half * sine_table], axis=-1)

def swiglu(gate_part, up_part):
    return jax.nn.silu(gate_part) * up_part

def slot_tables(routes):
    block_count = TOKENS // TOK_DEV
    pair_count = TOK_DEV * TOPK
    dump_slot = EXPERTS * CAP
    blocks = routes.reshape(block_count, pair_count)
    expert_ids = jnp.arange(EXPERTS, dtype=jnp.int32)

    def one_block(block_routes, block_index):
        onehot = (block_routes[:, None] == expert_ids[None, :]).astype(jnp.int32)
        before = jnp.cumsum(onehot, axis=0) - onehot
        pair_rank = lax.optimization_barrier(jnp.sum(before * onehot, axis=1))
        pair_kept = pair_rank < CAP
        slot_index = jnp.where(pair_kept, block_routes * CAP + pair_rank, dump_slot).astype(jnp.int32)
        pair_token = (block_index * TOK_DEV + jnp.arange(pair_count, dtype=jnp.int32) // TOPK).astype(jnp.int32)
        token_slot_table = jnp.zeros((dump_slot + 1,), jnp.int32).at[slot_index].set(pair_token)
        slot_fill_table = jnp.zeros((dump_slot + 1,), jnp.int32).at[slot_index].set(1)
        return (token_slot_table[:dump_slot], slot_fill_table[:dump_slot])
    token_slot_table, slot_fill_table = jax.vmap(one_block)(blocks, jnp.arange(block_count, dtype=jnp.int32))
    token_slot_table = token_slot_table.reshape(block_count, EXPERTS, CAP).transpose(1, 0, 2)
    slot_fill_table = slot_fill_table.reshape(block_count, EXPERTS, CAP).transpose(1, 0, 2)
    return (token_slot_table, slot_fill_table)

def attention(query_rows, key_nope, key_rope, value_rows, image_piece_index):
    seq_count = TOKENS // SEQ
    score_scale = (DN + DR) ** (-0.5)

    def one_sequence(carry_unused, inputs):
        seq_query, seq_nope, seq_rope, seq_value, seq_piece = inputs
        scores = jnp.einsum('thd,uhd->htu', seq_query[..., :DN], seq_nope, precision=HIGHEST)
        scores = scores + jnp.einsum('thd,ud->htu', seq_query[..., DN:], seq_rope, precision=HIGHEST)
        scores = low_back(scores * score_scale)
        position = jnp.arange(SEQ, dtype=jnp.int32)
        allowed = (position[None, :] <= position[:, None]) | (seq_piece[None, :] == seq_piece[:, None]) & (seq_piece[:, None] > 0)
        scores = jnp.where(allowed[None], scores, NEGATIVE)
        weights_attn = jax.nn.softmax(scores, axis=-1)
        mixed_heads = jnp.einsum('htu,uhd->thd', low(weights_attn), seq_value, precision=HIGHEST)
        return (carry_unused, low(low_back(mixed_heads)).reshape(SEQ, H * DV))
    inputs = (query_rows.reshape(seq_count, SEQ, H, DN + DR), key_nope.reshape(seq_count, SEQ, H, DN), key_rope.reshape(seq_count, SEQ, DR), value_rows.reshape(seq_count, SEQ, H, DV), image_piece_index.reshape(seq_count, SEQ))
    _, heads_out = lax.scan(jax.checkpoint(one_sequence), jnp.zeros((), jnp.float32), inputs)
    return heads_out.reshape(TOKENS, H * DV)

def routed(normed_second, router_probs, expert_gate, expert_up, expert_down, token_slot_table, slot_fill_table):
    expert_ids = jnp.arange(EXPERTS, dtype=jnp.int32)

    def one_expert(pieces):
        gate_matrix, up_matrix, down_matrix, token_rows, fill_rows, expert_id = pieces
        present = fill_rows > 0
        slot_rows = low_back(jnp.where(present[..., None], normed_second[token_rows], 0.0))
        gate_part = low_back(jnp.einsum('bcd,df->bcf', slot_rows, gate_matrix, precision=HIGHEST))
        up_part = low_back(jnp.einsum('bcd,df->bcf', slot_rows, up_matrix, precision=HIGHEST))
        activation = low(swiglu(gate_part, up_part))
        slot_out = low_back(low(jnp.einsum('bcf,fd->bcd', activation, down_matrix, precision=HIGHEST)))
        slot_gate = jnp.where(present, router_probs[token_rows, expert_id], 0.0)
        return slot_gate[..., None] * slot_out
    weighted = lax.map(jax.checkpoint(one_expert), (expert_gate, expert_up, expert_down, token_slot_table, slot_fill_table, expert_ids))
    routed_sum = jnp.zeros((TOKENS, D), jnp.float32)
    return routed_sum.at[token_slot_table.reshape(-1)].add(weighted.reshape(-1, D))

def forward_pass(tokens, attention_norm, query_weight, latent_down, latent_norm, latent_up, output_weight, post_norm, shared_gate, shared_up, shared_down, router_weight, expert_gate, expert_up, expert_down, image_piece_index, token_slot_table, slot_fill_table):
    positions = jnp.arange(TOKENS, dtype=jnp.int32) % SEQ
    cosine, sine_table = rope_tables(positions, DR)
    normed_first = low(rms_scale(tokens, low(attention_norm)))
    query_raw = low_back(jnp.dot(normed_first, low(query_weight), precision=HIGHEST)).reshape(TOKENS, H, DN + DR)
    down_raw = low_back(jnp.dot(normed_first, low(latent_down), precision=HIGHEST))
    query_rows = low(jnp.concatenate([query_raw[..., :DN], rotate(query_raw[..., DN:], cosine[:, None, :], sine_table[:, None, :])], axis=-1))
    latent = low(rms_scale(down_raw[:, :KVR], low(latent_norm)))
    key_rope = low(rotate(down_raw[:, KVR:], cosine, sine_table))
    expanded = low(low_back(jnp.dot(latent, low(latent_up), precision=HIGHEST))).reshape(TOKENS, H, DN + DV)
    heads_out = attention(query_rows, expanded[..., :DN], key_rope, expanded[..., DN:], image_piece_index)
    residual = tokens + low_back(jnp.dot(heads_out, low(output_weight), precision=HIGHEST))
    normed_second = low(rms_scale(residual, low(post_norm)))
    shared_gate_part = low_back(jnp.dot(normed_second, low(shared_gate), precision=HIGHEST))
    shared_up_part = low_back(jnp.dot(normed_second, low(shared_up), precision=HIGHEST))
    shared_out = jnp.dot(low(swiglu(shared_gate_part, shared_up_part)), low(shared_down), precision=HIGHEST)
    logits = low_back(jnp.dot(normed_second, low(router_weight), precision=HIGHEST))
    router_probs = jax.nn.softmax(logits, axis=-1)
    routed_out = routed(normed_second, router_probs, expert_gate, expert_up, expert_down, token_slot_table, slot_fill_table)
    return residual + shared_out + routed_out

def reference(tokens, attention_norm, query_weight, latent_down, latent_norm, latent_up, output_weight, post_norm, shared_gate, shared_up, shared_down, router_weight, expert_gate, expert_up, expert_down, image_piece_index, routes, cotangent):
    token_slot_table, slot_fill_table = slot_tables(routes)

    def decoder_layer(tokens_input, attention_input, query_input, down_input, latent_input, up_input, output_input, post_input, shared_gate_input, shared_up_input, shared_down_input, router_input, expert_gate_input, expert_up_input, expert_down_input):
        return forward_pass(tokens_input, attention_input, query_input, down_input, latent_input, up_input, output_input, post_input, shared_gate_input, shared_up_input, shared_down_input, router_input, expert_gate_input, expert_up_input, expert_down_input, image_piece_index, token_slot_table, slot_fill_table)
    result, pull = jax.vjp(decoder_layer, tokens.astype(jnp.float32), attention_norm, query_weight, latent_down, latent_norm, latent_up, output_weight, post_norm, shared_gate, shared_up, shared_down, router_weight, expert_gate.astype(jnp.float32), expert_up.astype(jnp.float32), expert_down.astype(jnp.float32))
    grads = pull(cotangent.astype(jnp.float32))
    return (result.astype(jnp.bfloat16), grads[0], grads[1], grads[2], grads[3], grads[4], grads[5], grads[6], grads[7], grads[8], grads[9], grads[10], grads[11], grads[12], grads[13], grads[14])
```

```python
import functools

import jax
import jax.numpy as jnp
from jax import lax
from jax.experimental import pallas as pl
from jax.experimental.pallas import tpu as pltpu
from jax.sharding import Mesh, PartitionSpec as P

D = 2048
H = 16
DN = 128
DR = 64
DV = 128
KVR = 512
TOPK = 6
PIECE = 256
EPSILON = 1e-06
ROPE_BASE = 10000.0
NEGATIVE = -1e30
BF = jnp.bfloat16
F32 = jnp.float32
EVERY = ("c", "k", "z")
COLUMN = ("k", "z")


def swap(block, axis, distance):
    n = lax.axis_size(axis)
    return lax.ppermute(block, axis, [(i, i ^ distance) for i in range(n)])


def lanes(n):
    return -(-n // 128) * 128


def widen(block, extra):
    room = lanes(extra.shape[1]) - extra.shape[1]
    return jnp.concatenate([block, jnp.pad(extra.astype(BF), ((0, 0), (0, room)))], axis=1)


def dot(a, b, dims):
    return lax.dot_general(a, b, (dims, ((), ())), preferred_element_type=F32)


def mm(a, b):
    return dot(a, b, ((1,), (0,)))


def mm_nt(a, b):
    return dot(a, b, ((1,), (1,)))


def mm_tn(a, b):
    return dot(a, b, ((0,), (0,)))


def gather_column(unit):
    z_size = lax.axis_size("z")
    mine = jnp.concatenate([unit] + [swap(unit, "z", d) for d in range(1, z_size)], axis=0)
    return mine


def gather_every(unit):
    mine = gather_column(unit)
    groups = [mine] + [swap(mine, "c", d) for d in range(1, lax.axis_size("c"))]
    return [(g, swap(g, "k", 1)) for g in groups]


def scatter_column(part, rows):
    z_size = lax.axis_size("z")
    half = z_size * rows
    summed = part[:half].astype(F32) + swap(part[half:].astype(BF), "k", 1).astype(F32)
    return scatter_z(summed, rows)


def scatter_z(summed, rows):
    total = summed[:rows]
    for d in range(1, lax.axis_size("z")):
        total = total + swap(summed[d * rows : (d + 1) * rows].astype(BF), "z", d).astype(F32)
    return total


def scatter_every(parts, rows):
    total = None
    half = lax.axis_size("z") * rows
    for d in reversed(range(len(parts))):
        part = parts[d]
        summed = part[:half].astype(F32) + swap(part[half:].astype(BF), "k", 1).astype(F32)
        if d:
            summed = swap(summed.astype(BF), "c", d).astype(F32)
        total = summed if total is None else total + summed
    return scatter_z(total, rows)


def pick(array, index):
    return lax.dynamic_index_in_dim(array, index, axis=0, keepdims=False)


def scatter_weight(part):
    c_size, k_size, z_size = (lax.axis_size(a) for a in EVERY)
    c, k, z = (lax.axis_index(a) for a in EVERY)
    rows = part.shape[0] // (c_size * k_size * z_size)
    n = part.shape[1]
    grid = part.reshape(c_size, k_size, z_size * rows, n)
    away = lax.dynamic_index_in_dim(grid, k ^ 1, axis=1, keepdims=False).astype(BF)
    kept = lax.dynamic_index_in_dim(grid, k, axis=1, keepdims=False).astype(F32)
    summed = kept + swap(away, "k", 1).astype(F32)
    total = pick(summed, c)
    for d in range(1, c_size):
        total = total + swap(pick(summed, c ^ d).astype(BF), "c", d).astype(F32)
    total = total.reshape(z_size, rows, n)
    out = pick(total, z)
    for d in range(1, z_size):
        out = out + swap(pick(total, z ^ d).astype(BF), "z", d).astype(F32)
    return out


def rms_parts(values):
    return lax.rsqrt(jnp.mean(values * values, axis=-1, keepdims=True) + EPSILON)


def rms_back(values, scale, gain, grad):
    weighted = grad * gain
    inner = jnp.mean(weighted * values, axis=-1, keepdims=True)
    return scale * (weighted - values * (scale * scale * inner)), grad * values * scale


def rotate(values, cosine, sine, sign):
    half = values.shape[-1] // 2
    a, b = values[..., :half], values[..., half:]
    return jnp.concatenate([a * cosine - sign * b * sine, b * cosine + sign * a * sine], axis=-1)


def expert_kernel(
    local_experts,
    capacity,
    rows,
    experts,
    first,
    place_ref,
    sec_a,
    sec_b,
    cot_a,
    cot_b,
    gate_hbm,
    up_hbm,
    down_hbm,
    sin_hbm,
    sdn_hbm,
    *rest,
):
    rest = rest if first else rest[5:]
    (x_out, c_out, aw_out, gg_out, ug_out, out_out, in_out, sg_out, sd_out) = rest[:9]
    (sec_v, cot_v, gate_v, up_v, down_v, sin_v, sdn_v, x_v, c_v, y_v, z_v, aw_v, gg_v, ug_v) = rest[9:23]
    (choose_v, prob_v, sact_v, slow_v, sgp_v, sdp_v, sem_in, sem_out) = rest[23:31]
    half = sec_a.shape[0]
    blocks = 2 * half // rows
    per = blocks * capacity
    wpad = sdn_v.shape[0]
    base = place_ref[1] * per

    def copy(src, dst, sem, i):
        made = pltpu.make_async_copy(src, dst, sem.at[i])
        made.start()
        return made

    in_sec = [
        copy(sec_a, sec_v.at[pl.ds(0, half)], sem_in, 0),
        copy(sec_b, sec_v.at[pl.ds(half, half)], sem_in, 1),
    ]
    in_cot = [
        copy(cot_a, cot_v.at[pl.ds(0, half)], sem_in, 2),
        copy(cot_b, cot_v.at[pl.ds(half, half)], sem_in, 3),
    ]
    in_gate = copy(gate_hbm, gate_v, sem_in, 4)
    in_up = copy(up_hbm, up_v, sem_in, 5)
    in_down = copy(down_hbm, down_v, sem_in, 6)
    in_sin = copy(sin_hbm, sin_v, sem_in, 7)
    in_sdn = copy(sdn_hbm, sdn_v, sem_in, 8)
    for one in in_cot:
        one.wait()

    first_expert = place_ref[0]
    tail = cot_v.shape[1] - D
    row_i = lax.broadcasted_iota(jnp.int32, (rows, rows), 0)
    col_i = lax.broadcasted_iota(jnp.int32, (rows, rows), 1)
    earlier = (col_i < row_i).astype(BF)
    lane = lax.broadcasted_iota(jnp.int32, (rows, tail), 1)
    slot = lax.broadcasted_iota(jnp.int32, (rows, local_experts * capacity), 1).astype(F32)
    for one in in_sec:
        one.wait()
    sec_tail = sec_v.shape[1] - D
    tail_lane = lax.broadcasted_iota(jnp.int32, (capacity, sec_tail), 1)

    def gather(b, carry):
        at = pl.ds(pl.multiple_of(b * rows, rows), rows)
        named = cot_v[at, D:]
        rank = mm(earlier, named)
        code = jnp.where((named.astype(F32) > 0) & (rank < capacity), rank, -1e6)
        chosen = jnp.zeros(slot.shape, F32)
        for e in range(local_experts):
            own = jnp.sum(jnp.where(lane == first_expert + e, code, 0.0), axis=1, keepdims=True)
            chosen = jnp.where(own + e * capacity == slot, 1.0, chosen)
        choose = chosen.astype(BF)
        choose_v[at, :] = choose
        picked = mm_tn(choose, sec_v[at, :])
        cots = mm_tn(choose, cot_v[at, :D])
        for e in range(local_experts):
            mine = slice(e * capacity, (e + 1) * capacity)
            to = pl.ds(pl.multiple_of(e * per + b * capacity, capacity), capacity)
            x_v[to, :] = picked[mine, :D].astype(BF)
            c_v[to, :] = cots[mine].astype(BF)
            which = first_expert + e
            hits = (tail_lane == which) | (tail_lane == which + experts)
            prob = jnp.sum(jnp.where(hits, picked[mine, D:], 0.0), axis=1, keepdims=True)
            prob_v[to, :] = jnp.broadcast_to(prob, (capacity, 128))
        return carry

    lax.fori_loop(0, blocks, gather, 0)
    outs = []
    for e in range(local_experts):
        mine = pl.ds(e * per, per)
        outs.append(copy(x_v.at[mine], x_out.at[e, pl.ds(base, per)], sem_out, 2 * e))
        outs.append(copy(c_v.at[mine], c_out.at[e, pl.ds(base, per)], sem_out, 2 * e + 1))
    used = 2 * local_experts

    in_sin.wait()
    in_sdn.wait()
    shared = mm(sec_v[:, :D], sin_v[...])
    s_gate, s_up = shared[:, :wpad], shared[:, wpad:]
    s_sigma = jax.nn.sigmoid(s_gate)
    s_silu = s_gate * s_sigma
    s_grad = mm_nt(cot_v[:, :D], sdn_v[...])
    sact_v[...] = (s_silu * s_up).astype(BF)
    slow_v[:, :wpad] = (s_grad * s_up * (s_sigma * (1.0 + s_gate * (1.0 - s_sigma)))).astype(BF)
    slow_v[:, wpad:] = (s_grad * s_silu).astype(BF)
    sgp_v[...] = mm_tn(slow_v[...], sec_v[:, :D])
    sdp_v[...] = mm_tn(sact_v[...], cot_v[:, :D])
    outs.append(copy(sgp_v, sg_out, sem_out, used))
    outs.append(copy(sdp_v, sd_out, sem_out, used + 1))
    used += 2

    in_gate.wait()
    in_up.wait()
    in_down.wait()
    in_tail = z_v.shape[2] - D
    pair_lane = lax.broadcasted_iota(jnp.int32, (per, in_tail), 1)
    for e in range(local_experts):
        mine = pl.ds(e * per, per)
        x_e, c_e = x_v[mine, :], c_v[mine, :]
        gate = mm(x_e, gate_v[e])
        up = mm(x_e, up_v[e])
        pull = mm_nt(c_e, down_v[e])
        prob = prob_v[mine, :1]
        sigma = jax.nn.sigmoid(gate)
        silu = gate * sigma
        act = silu * up
        pair = jnp.sum(pull * act, axis=1, keepdims=True)
        pull = pull * prob
        gg_v[e] = (pull * up * (sigma * (1.0 + gate * (1.0 - sigma)))).astype(BF)
        ug_v[e] = (pull * silu).astype(BF)
        aw_v[e] = (act * prob).astype(BF)
        outs.append(copy(aw_v.at[e], aw_out.at[e, pl.ds(base, per)], sem_out, used))
        outs.append(copy(gg_v.at[e], gg_out.at[e, pl.ds(base, per)], sem_out, used + 1))
        outs.append(copy(ug_v.at[e], ug_out.at[e, pl.ds(base, per)], sem_out, used + 2))
        used += 3
        y = mm(aw_v[e], down_v[e]).astype(BF)
        y_v[:, e * capacity : (e + 1) * capacity, :] = y.reshape(blocks, capacity, D)
        zed = (mm_nt(gg_v[e], gate_v[e]) + mm_nt(ug_v[e], up_v[e])).astype(BF)
        z_v[:, e * capacity : (e + 1) * capacity, :D] = zed.reshape(blocks, capacity, D)
        pairs = jnp.where(pair_lane == first_expert + e, pair, 0.0).astype(BF)
        z_v[:, e * capacity : (e + 1) * capacity, D:] = pairs.reshape(blocks, capacity, in_tail)

    def scatter(b, carry):
        at = pl.ds(pl.multiple_of(b * rows, rows), rows)
        choose = choose_v[at, :]
        cot_v[at, :D] = (mm(choose, y_v[b]) + mm(sact_v[at, :], sdn_v[...])).astype(BF)
        back = mm(choose, z_v[b])
        sec_v[at, :D] = (back[:, :D] + mm_nt(slow_v[at, :], sin_v[...])).astype(BF)
        sec_v[at, D:] = back[:, D:].astype(BF)
        return carry

    lax.fori_loop(0, blocks, scatter, 0)
    outs.append(copy(sec_v, in_out, sem_out, used))
    outs.append(copy(cot_v.at[:, pl.ds(0, D)], out_out, sem_out, used + 1))
    for one in outs:
        one.wait()


def expert_group(place, sec, cot, weights, kept, capacity, rows, experts, groups):
    gate, up, down, sin, sdn = weights
    local_experts, _, hidden = gate.shape
    half = sec[0].shape[0]
    tokens = 2 * half
    blocks = tokens // rows
    per = blocks * capacity
    slots = per * groups
    wpad = sdn.shape[0]
    in_width = D + lanes(experts)
    big = (local_experts, slots)
    shapes = [
        jax.ShapeDtypeStruct((*big, D), BF),
        jax.ShapeDtypeStruct((*big, D), BF),
        jax.ShapeDtypeStruct((*big, hidden), BF),
        jax.ShapeDtypeStruct((*big, hidden), BF),
        jax.ShapeDtypeStruct((*big, hidden), BF),
        jax.ShapeDtypeStruct((tokens, D), BF),
        jax.ShapeDtypeStruct((tokens, in_width), BF),
        jax.ShapeDtypeStruct((2 * wpad, D), F32),
        jax.ShapeDtypeStruct((wpad, D), F32),
    ]
    first = kept is None
    operands = [place, *sec, *cot, gate, up, down, sin, sdn] + ([] if first else list(kept))
    any_space = pl.BlockSpec(memory_space=pl.ANY)
    smem = pl.BlockSpec(memory_space=pltpu.SMEM)
    flops = 2 * tokens * D * (6 * wpad + 8 * local_experts * capacity) + 12 * local_experts * per * D * hidden
    return pl.pallas_call(
        functools.partial(expert_kernel, local_experts, capacity, rows, experts, first),
        out_shape=shapes,
        in_specs=[smem] + [any_space] * (len(operands) - 1),
        out_specs=[any_space] * len(shapes),
        scratch_shapes=[
            pltpu.VMEM((tokens, sec[0].shape[1]), BF),
            pltpu.VMEM((tokens, cot[0].shape[1]), BF),
            pltpu.VMEM(gate.shape, BF),
            pltpu.VMEM(up.shape, BF),
            pltpu.VMEM(down.shape, BF),
            pltpu.VMEM(sin.shape, BF),
            pltpu.VMEM(sdn.shape, BF),
            pltpu.VMEM((local_experts * per, D), BF),
            pltpu.VMEM((local_experts * per, D), BF),
            pltpu.VMEM((blocks, local_experts * capacity, D), BF),
            pltpu.VMEM((blocks, local_experts * capacity, in_width), BF),
            pltpu.VMEM((local_experts, per, hidden), BF),
            pltpu.VMEM((local_experts, per, hidden), BF),
            pltpu.VMEM((local_experts, per, hidden), BF),
            pltpu.VMEM((tokens, local_experts * capacity), BF),
            pltpu.VMEM((local_experts * per, 128), F32),
            pltpu.VMEM((tokens, wpad), BF),
            pltpu.VMEM((tokens, 2 * wpad), BF),
            pltpu.VMEM((2 * wpad, D), F32),
            pltpu.VMEM((wpad, D), F32),
            pltpu.SemaphoreType.DMA((9,)),
            pltpu.SemaphoreType.DMA((5 * local_experts + 4,)),
        ],
        input_output_aliases={} if first else {10 + i: i for i in range(5)},
        compiler_params=pltpu.CompilerParams(vmem_limit_bytes=63 * 1024 * 1024),
        cost_estimate=pl.CostEstimate(flops=flops, bytes_accessed=38 << 20, transcendentals=0),
    )(*operands)


def on_device(
    tokens,
    attention_norm,
    query_weight,
    latent_down,
    latent_norm,
    latent_up,
    output_weight,
    post_norm,
    shared_gate,
    shared_up,
    shared_down,
    router_weight,
    expert_gate,
    expert_up,
    expert_down,
    image_piece_index,
    routes,
    cotangent,
):
    rows = tokens.shape[0]
    c_size, k_size, z_size = (lax.axis_size(a) for a in EVERY)
    c, k, z = (lax.axis_index(a) for a in EVERY)
    column_size = k_size * z_size
    device_count = c_size * column_size
    local_experts = expert_gate.shape[0]
    experts = router_weight.shape[1]
    capacity = rows * TOPK * 4 // (3 * experts)
    length = column_size * rows
    heads = H // column_size
    width = shared_down.shape[0]
    score_scale = (DN + DR) ** (-0.5)
    weight_rows = query_weight.shape[0]
    up_rows = latent_up.shape[0]

    expert_ids = jnp.arange(experts, dtype=jnp.int32)
    named = jnp.any(routes[:, :, None] == expert_ids[None, None, :], axis=1)
    flag = (image_piece_index > 0).astype(BF)[:, None]
    mine = gather_column(widen(tokens, flag))
    sequence = jnp.concatenate([mine, swap(mine, "k", 1)], axis=0)
    cot_groups = gather_every(widen(cotangent, named))

    small = jnp.concatenate(
        [
            latent_down,
            router_weight,
            attention_norm[:, None],
            post_norm[:, None],
            jnp.pad(latent_norm, (0, weight_rows - latent_norm.shape[0]))[:, None],
        ],
        axis=1,
    ).astype(BF)
    small_width = small.shape[1]
    small = jnp.pad(small, ((0, 0), (0, lanes(small_width) - small_width)))
    full_small = lax.all_gather(small, EVERY, axis=0, tiled=True)
    down_width = KVR + DR
    full_down = full_small[:, :down_width]
    full_router = full_small[:, down_width : down_width + experts]
    attn_gain = full_small[:, down_width + experts].astype(F32)
    post_gain = full_small[:, down_width + experts + 1].astype(F32)
    latent_gain = (
        full_small[:, down_width + experts + 2]
        .reshape(device_count, weight_rows)[:, : latent_norm.shape[0]]
        .reshape(KVR)
        .astype(F32)
    )
    q_width = heads * (DN + DR)
    kv_width = heads * (DN + DV)
    q_out = query_weight.astype(BF).reshape(weight_rows, column_size, q_width).transpose(1, 0, 2)
    q_out = jnp.pad(q_out, ((0, 0), (0, 0), (0, kv_width - q_width)))
    up_out = latent_up.astype(BF).reshape(up_rows, column_size, kv_width).transpose(1, 0, 2)
    head_pack = jnp.concatenate([q_out, up_out], axis=1)
    head_pack = lax.all_to_all(head_pack, COLUMN, split_axis=0, concat_axis=0, tiled=True)
    head_pack = lax.all_gather(head_pack, "c", axis=0, tiled=False)
    head_query = head_pack[:, :, :weight_rows, :q_width].reshape(D, q_width)
    head_up = head_pack[:, :, weight_rows:].reshape(KVR, kv_width)
    full_out = lax.all_gather(output_weight.astype(BF), EVERY, axis=0, tiled=True)
    shared_pack = jnp.concatenate(
        [
            shared_gate.astype(BF).reshape(weight_rows, device_count, width),
            shared_up.astype(BF).reshape(weight_rows, device_count, width),
        ],
        axis=2,
    ).transpose(1, 0, 2)
    shared_in = lax.all_to_all(shared_pack, EVERY, split_axis=0, concat_axis=0, tiled=True)
    shared_in = shared_in.reshape(D, 2 * width)
    room = ((0, 0), (0, lanes(width) - width))
    shared_in = jnp.concatenate(
        [jnp.pad(shared_in[:, :width], room), jnp.pad(shared_in[:, width:], room)], axis=1
    )
    shared_low = shared_down.astype(BF)

    step = jnp.arange(rows, dtype=jnp.int32)
    places = jnp.concatenate(
        [
            ((k ^ dk) * z_size + (z ^ dz)) * rows + step
            for dk in range(k_size)
            for dz in range(z_size)
        ]
    )
    image = sequence[:, D] > 0
    allowed = (places[None, :] <= places[:, None]) | (
        (places[None, :] // PIECE == places[:, None] // PIECE) & image[:, None]
    )
    frequency = ROPE_BASE ** (-2.0 * jnp.arange(DR // 2, dtype=F32) / DR)
    angles = places.astype(F32)[:, None] * frequency[None, :]
    cosine, sine = jnp.cos(angles), jnp.sin(angles)

    values = sequence[:, :D].astype(F32)
    first_scale = rms_parts(values)
    first_low = (values * first_scale * attn_gain).astype(BF)
    query_raw = mm(first_low, head_query).reshape(length, heads, DN + DR)
    down_raw = mm(first_low, full_down)
    query_nope = query_raw[..., :DN].astype(BF)
    query_rope = rotate(query_raw[..., DN:], cosine[:, None], sine[:, None], 1.0).astype(BF)
    latent_raw = down_raw[:, :KVR]
    latent_scale = rms_parts(latent_raw)
    latent_low = (latent_raw * latent_scale * latent_gain).astype(BF)
    key_rope = rotate(down_raw[:, KVR:], cosine, sine, 1.0).astype(BF)
    expanded = mm(latent_low, head_up).astype(BF).reshape(length, heads, DN + DV)
    key_nope = expanded[..., :DN]
    value_rows = expanded[..., DN:]
    scores = jnp.einsum("thd,uhd->htu", query_nope, key_nope, preferred_element_type=F32)
    scores = scores + jnp.einsum("thd,ud->htu", query_rope, key_rope, preferred_element_type=F32)
    scores = jnp.where(allowed[None], scores * score_scale, NEGATIVE)
    weights_attn = jax.nn.softmax(scores, axis=-1)
    probs_low = weights_attn.astype(BF)
    heads_out = jnp.einsum("htu,uhd->thd", probs_low, value_rows, preferred_element_type=F32)
    heads_out = heads_out.astype(BF).reshape(length, heads * DV)

    def place_order(array):
        blocks = array.reshape(k_size, z_size, rows, array.shape[1])
        return jnp.concatenate(
            [
                lax.dynamic_slice(
                    blocks, (k ^ (j // z_size), z ^ (j % z_size), 0, 0), (1, 1, rows, array.shape[1])
                ).reshape(rows, array.shape[1])
                for j in range(column_size)
            ],
            axis=0,
        )

    def own_order(array):
        return place_order(array)

    def heads_to_tokens(array):
        moved = lax.all_to_all(
            place_order(array).reshape(column_size, rows, array.shape[1]),
            COLUMN,
            split_axis=0,
            concat_axis=0,
            tiled=True,
        )
        return moved.transpose(1, 0, 2).reshape(rows, column_size * array.shape[1])

    def tokens_to_heads(array):
        n = array.shape[1] // column_size
        moved = lax.all_to_all(
            array.reshape(rows, column_size, n).transpose(1, 0, 2),
            COLUMN,
            split_axis=0,
            concat_axis=0,
            tiled=True,
        )
        return own_order(moved.reshape(length, n))

    heads_low = heads_to_tokens(heads_out)
    residual = tokens.astype(F32) + mm(heads_low, full_out)
    second_scale = rms_parts(residual)
    second_low = (residual * second_scale * post_gain).astype(BF)
    router_probs = jax.nn.softmax(mm(second_low, full_router), axis=-1)

    probs_high = router_probs.astype(BF)
    probs_rest = (router_probs - probs_high.astype(F32)).astype(BF)
    second_groups = gather_every(
        widen(second_low, jnp.concatenate([probs_high, probs_rest], axis=1))
    )
    wpad = lanes(width)
    place = jnp.stack([(c * k_size + k) * local_experts, jnp.zeros((), jnp.int32)]).astype(jnp.int32)
    shared_rows = jnp.pad(shared_low, ((0, wpad - width), (0, 0)))
    weights = (expert_gate, expert_up, expert_down, shared_in, shared_rows)
    kept, out_parts, in_parts, sg_parts, sd_parts = None, [], [], [], []
    for d in range(c_size):
        results = expert_group(
            place.at[1].set(d), second_groups[d], cot_groups[d], weights, kept, capacity, rows, experts, c_size
        )
        kept = results[:5]
        out_parts.append(results[5])
        in_parts.append(results[6])
        sg_parts.append(results[7])
        sd_parts.append(results[8])
    expert_in, cot_in, act_weighted, gate_grad, up_grad = kept
    ein = lambda spec, a, b: jnp.einsum(spec, a, b, preferred_element_type=F32)
    expert_down_grad = ein("esf,esd->efd", act_weighted, cot_in)
    expert_gate_grad = ein("esd,esf->edf", expert_in, gate_grad)
    expert_up_grad = ein("esd,esf->edf", expert_in, up_grad)
    shared_in_grad = sum(sg_parts[1:], sg_parts[0])
    shared_in_grad = jnp.concatenate(
        [shared_in_grad[:width], shared_in_grad[wpad : wpad + width]], axis=0
    ).astype(BF)
    shared_down_grad = sum(sd_parts[1:], sd_parts[0])[:width]

    second_sum = scatter_every(in_parts, rows)
    out_sum = scatter_every(out_parts, rows)
    layer_out = (residual + out_sum).astype(BF)

    probs_grad = second_sum[:, D : D + experts]
    logits_grad = (
        router_probs * (probs_grad - jnp.sum(router_probs * probs_grad, axis=-1, keepdims=True))
    ).astype(BF)
    router_grad = mm_tn(second_low, logits_grad)
    second_grad = second_sum[:, :D] + mm_nt(logits_grad, full_router)
    norm_part, post_terms = rms_back(residual, second_scale, post_gain, second_grad)
    residual_grad = cotangent.astype(F32) + norm_part
    attn_grad_low = residual_grad.astype(BF)
    output_grad = mm_tn(heads_low, attn_grad_low)
    heads_grad = tokens_to_heads(mm_nt(attn_grad_low, full_out).astype(BF))
    heads_grad = heads_grad.reshape(length, heads, DV)

    value_grad = ein("htu,thd->uhd", probs_low, heads_grad)
    dprob = ein("thd,uhd->htu", heads_grad, value_rows)
    score_grad = (
        weights_attn * (dprob - jnp.sum(weights_attn * dprob, axis=-1, keepdims=True))
    ).astype(BF)
    query_nope_grad = ein("htu,uhd->thd", score_grad, key_nope) * score_scale
    query_rope_grad = ein("htu,ud->thd", score_grad, key_rope) * score_scale
    key_nope_grad = ein("htu,thd->uhd", score_grad, query_nope) * score_scale
    key_rope_grad = ein("htu,thd->ud", score_grad, query_rope) * score_scale
    expanded_grad = jnp.concatenate([key_nope_grad, value_grad], axis=-1)
    expanded_grad = expanded_grad.reshape(length, kv_width).astype(BF)
    head_up_grad = mm_tn(latent_low, expanded_grad)
    latent_part = mm_nt(expanded_grad, head_up)
    latent_part = jnp.concatenate(
        [latent_part, key_rope_grad, jnp.zeros((length, lanes(down_width) - down_width), F32)], axis=1
    )
    latent_sum = scatter_column(latent_part, rows)
    latent_raw_grad, latent_terms = rms_back(
        latent_raw[:rows], latent_scale[:rows], latent_gain, latent_sum[:, :KVR]
    )
    rope_raw_grad = rotate(latent_sum[:, KVR:down_width], cosine[:rows], sine[:rows], -1.0)
    down_grad_low = jnp.concatenate([latent_raw_grad, rope_raw_grad], axis=-1).astype(BF)
    query_rope_raw = rotate(query_rope_grad, cosine[:, None], sine[:, None], -1.0)
    query_grad_low = jnp.concatenate([query_nope_grad, query_rope_raw], axis=-1)
    query_grad_low = query_grad_low.reshape(length, q_width).astype(BF)
    head_query_grad = mm_tn(first_low, query_grad_low)
    latent_down_grad = mm_tn(first_low[:rows], down_grad_low)
    first_part = mm_nt(query_grad_low, head_query)
    first_own = mm_nt(down_grad_low, full_down)
    first_grad = scatter_column(first_part, rows) + first_own
    first_norm_grad, attn_terms = rms_back(values[:rows], first_scale[:rows], attn_gain, first_grad)
    tokens_grad = residual_grad + first_norm_grad

    small_grad = jnp.concatenate(
        [
            latent_down_grad,
            router_grad,
            jnp.sum(attn_terms, axis=0)[:, None],
            jnp.sum(post_terms, axis=0)[:, None],
            jnp.pad(
                jnp.sum(latent_terms, axis=0).reshape(device_count, latent_norm.shape[0]),
                ((0, 0), (0, weight_rows - latent_norm.shape[0])),
            ).reshape(D, 1),
            jnp.zeros((D, lanes(small_width) - small_width), F32),
        ],
        axis=1,
    )
    own_small = scatter_weight(small_grad)
    own_output = scatter_weight(output_grad)
    head_grad = jnp.concatenate(
        [
            jnp.pad(
                head_query_grad.reshape(c_size, column_size, weight_rows, q_width),
                ((0, 0), (0, 0), (0, 0), (0, kv_width - q_width)),
            ),
            head_up_grad.reshape(c_size, column_size, up_rows, kv_width),
        ],
        axis=2,
    )
    head_sum = pick(head_grad, c)
    for d in range(1, c_size):
        head_sum = head_sum + swap(pick(head_grad, c ^ d).astype(BF), "c", d).astype(F32)
    head_sum = lax.all_to_all(head_sum.astype(BF), COLUMN, split_axis=0, concat_axis=0, tiled=True)
    own_query = head_sum[:, :weight_rows, :q_width].transpose(1, 0, 2).reshape(weight_rows, -1)
    own_up = head_sum[:, weight_rows:].transpose(1, 0, 2).reshape(up_rows, -1)
    shared_back = lax.all_to_all(
        shared_in_grad.reshape(2 * width, device_count, weight_rows).transpose(1, 2, 0),
        EVERY,
        split_axis=0,
        concat_axis=0,
        tiled=True,
    ).transpose(1, 0, 2)
    own_gate = shared_back[:, :, :width].reshape(weight_rows, -1)
    own_shared_up = shared_back[:, :, width:].reshape(weight_rows, -1)
    return (
        layer_out,
        tokens_grad,
        own_small[:, down_width + experts],
        own_query.astype(F32),
        own_small[:, :down_width],
        own_small[: latent_norm.shape[0], down_width + experts + 2],
        own_up.astype(F32),
        own_output,
        own_small[:, down_width + experts + 1],
        own_gate.astype(F32),
        own_shared_up.astype(F32),
        shared_down_grad,
        own_small[:, down_width : down_width + experts],
        expert_gate_grad,
        expert_up_grad,
        expert_down_grad,
    )


def solution(mesh):
    expert_size, z_size = mesh.devices.shape
    fine = Mesh(mesh.devices.reshape(expert_size // 2, 2, z_size), EVERY)
    row, flat = P(EVERY, None), P(EVERY)
    wide, tall = P(("c", "k"), None, "z"), P(("c", "k"), "z", None)
    return jax.shard_map(
        on_device,
        mesh=fine,
        in_specs=(row, flat, row, row, flat, row, row, flat, row, row, row, row)
        + (wide, wide, tall, flat, row, row),
        out_specs=(row, row, flat, row, row, flat, row, row, flat, row, row, row, row)
        + (wide, wide, tall),
        check_vma=False,
    )
```

```python
import functools

import jax
import jax.numpy as jnp
from jax import lax
from jax.experimental import pallas as pl
from jax.experimental.pallas import tpu as pltpu
from jax.sharding import Mesh, PartitionSpec as P

D = 2048
H = 16
DN = 128
DR = 64
DV = 128
KVR = 512
TOPK = 6
PIECE = 256
EPSILON = 1e-06
ROPE_BASE = 10000.0
NEGATIVE = -1e30
BF = jnp.bfloat16
F32 = jnp.float32
EVERY = ("c", "k", "z")
COLUMN = ("k", "z")


def swap(block, axis, distance):
    n = lax.axis_size(axis)
    return lax.ppermute(block, axis, [(i, i ^ distance) for i in range(n)])


def lanes(n):
    return -(-n // 128) * 128


def widen(block, extra):
    room = lanes(extra.shape[1]) - extra.shape[1]
    return jnp.concatenate([block, jnp.pad(extra.astype(BF), ((0, 0), (0, room)))], axis=1)


def dot(a, b, dims):
    return lax.dot_general(a, b, (dims, ((), ())), preferred_element_type=F32)


def mm(a, b):
    return dot(a, b, ((1,), (0,)))


def mm_nt(a, b):
    return dot(a, b, ((1,), (1,)))


def mm_tn(a, b):
    return dot(a, b, ((0,), (0,)))


def after(array, *others):
    return lax.optimization_barrier((array, *others))[0]


def after_all(arrays, *others):
    return lax.optimization_barrier((tuple(arrays), *others))[0]


def put(buffer, block, index):
    return lax.dynamic_update_slice_in_dim(buffer, block[None], index, axis=0)


def gather_z(unit):
    return [unit] + [swap(unit, "z", d) for d in range(1, lax.axis_size("z"))]


def in_order(blocks, index):
    whole = jnp.zeros((len(blocks), *blocks[0].shape), blocks[0].dtype)
    for d, block in enumerate(blocks):
        whole = put(whole, block, index ^ d)
    return whole


def gather_weight(unit):
    c_size, k_size, _ = (lax.axis_size(a) for a in EVERY)
    c, k, z = (lax.axis_index(a) for a in EVERY)
    mine = in_order(gather_z(unit), z)
    planes = [mine] + [swap(mine, "c", d) for d in range(1, c_size)]
    own = in_order(planes, c)
    other = swap(own, "k", 1)
    halves = in_order([own, other], k)
    return halves.transpose(1, 0, 2, 3, 4), planes[1:]


def scatter_z(blocks):
    total = blocks[0]
    for d in range(1, len(blocks)):
        total = total + swap(blocks[d].astype(BF), "z", d).astype(F32)
    return total


def scatter_column(part, rows):
    z_size = lax.axis_size("z")
    k, z = lax.axis_index("k"), lax.axis_index("z")
    grid = part.reshape(2, z_size, rows, part.shape[1])
    summed = pick(grid, k) + swap(pick(grid, k ^ 1).astype(BF), "k", 1).astype(F32)
    return scatter_z([pick(summed, z ^ d) for d in range(z_size)])


def core_sum(own, other, distance):
    summed = own.astype(F32) + swap(other, "k", 1).astype(F32)
    return summed.astype(BF) if distance else summed


def plane_sum(sums, *others):
    moved = [swap(block, "c", d) for d, block in enumerate(sums) if d]
    if others:
        moved = after_all(moved, *others)
    total = sums[0]
    for block in moved:
        total = total + block.astype(F32)
    return total, moved


def z_units(total, rows):
    return [total[d * rows : (d + 1) * rows] for d in range(lax.axis_size("z"))]


def pick(array, index):
    return lax.dynamic_index_in_dim(array, index, axis=0, keepdims=False)


def core_pieces(part):
    c_size, k_size, z_size = (lax.axis_size(a) for a in EVERY)
    c, k = lax.axis_index("c"), lax.axis_index("k")
    grid = part.reshape(c_size, k_size, part.shape[0] // (c_size * k_size), part.shape[1])
    got = swap(lax.dynamic_index_in_dim(grid, k ^ 1, axis=1, keepdims=False), "k", 1)
    kept = lax.dynamic_index_in_dim(grid, k, axis=1, keepdims=False)
    pieces = []
    for d in range(c_size):
        piece = pick(kept, c ^ d).astype(F32) + pick(got, c ^ d).astype(F32)
        pieces.append(piece.astype(BF) if d else piece)
    return pieces


def pieces_sum(pieces, *others):
    total, _ = plane_sum(pieces, *others)
    return z_sum(total)


def z_sum(total):
    z_size, z = lax.axis_size("z"), lax.axis_index("z")
    total = total.reshape(z_size, total.shape[0] // z_size, total.shape[1])
    return scatter_z([pick(total, z ^ d) for d in range(z_size)])


def scatter_weight(part):
    return pieces_sum(core_pieces(part))


def rms_parts(values):
    return lax.rsqrt(jnp.mean(values * values, axis=-1, keepdims=True) + EPSILON)


def rms_back(values, scale, gain, grad):
    weighted = grad * gain
    inner = jnp.mean(weighted * values, axis=-1, keepdims=True)
    return scale * (weighted - values * (scale * scale * inner)), grad * values * scale


def rotate(values, cosine, sine, sign):
    half = values.shape[-1] // 2
    a, b = values[..., :half], values[..., half:]
    return jnp.concatenate([a * cosine - sign * b * sine, b * cosine + sign * a * sine], axis=-1)


def expert_kernel(
    local_experts,
    capacity,
    rows,
    experts,
    first,
    place_ref,
    sec_a,
    sec_b,
    cot_a,
    cot_b,
    gate_hbm,
    up_hbm,
    down_hbm,
    sin_hbm,
    sdn_hbm,
    *rest,
):
    rest = rest if first else rest[5:]
    (x_out, c_out, aw_out, gg_out, ug_out, out_a, out_b, in_a, in_b, sg_out, sd_out) = rest[:11]
    (sec_v, cot_v, gate_v, up_v, down_v, sin_v, sdn_v, x_v, c_v, y_v, z_v, aw_v, gg_v, ug_v) = rest[11:25]
    (choose_v, prob_v, sact_v, slow_v, sgp_v, sdp_v, sem_in, sem_out, sem_block) = rest[25:34]
    half = sec_a.shape[0]
    blocks = 2 * half // rows
    per = blocks * capacity
    wpad = sdn_v.shape[0]
    base = place_ref[1] * per

    def copy(src, dst, sem, i):
        made = pltpu.make_async_copy(src, dst, sem.at[i])
        made.start()
        return made

    in_sec = [
        copy(sec_a, sec_v.at[pl.ds(0, half)], sem_in, 0),
        copy(sec_b, sec_v.at[pl.ds(half, half)], sem_in, 1),
    ]
    in_cot = [
        copy(cot_a, cot_v.at[pl.ds(0, half)], sem_in, 2),
        copy(cot_b, cot_v.at[pl.ds(half, half)], sem_in, 3),
    ]
    for one in in_cot:
        one.wait()

    first_expert = place_ref[0]
    tail = cot_v.shape[1] - D
    row_i = lax.broadcasted_iota(jnp.int32, (rows, rows), 0)
    col_i = lax.broadcasted_iota(jnp.int32, (rows, rows), 1)
    earlier = (col_i < row_i).astype(BF)
    lane = lax.broadcasted_iota(jnp.int32, (rows, tail), 1)
    slot = lax.broadcasted_iota(jnp.int32, (rows, local_experts * capacity), 1).astype(F32)
    for one in in_sec:
        one.wait()
    in_sin = copy(sin_hbm, sin_v, sem_in, 7)
    in_sdn = copy(sdn_hbm, sdn_v, sem_in, 8)
    in_gate = copy(gate_hbm, gate_v, sem_in, 4)
    in_up = copy(up_hbm, up_v, sem_in, 5)
    in_down = copy(down_hbm, down_v, sem_in, 6)
    sec_tail = sec_v.shape[1] - D
    tail_lane = lax.broadcasted_iota(jnp.int32, (capacity, sec_tail), 1)

    def gather(b, carry):
        at = pl.ds(pl.multiple_of(b * rows, rows), rows)
        named = cot_v[at, D:]
        rank = mm(earlier, named)
        code = jnp.where((named.astype(F32) > 0) & (rank < capacity), rank, -1e6)
        chosen = jnp.zeros(slot.shape, F32)
        for e in range(local_experts):
            own = jnp.sum(jnp.where(lane == first_expert + e, code, 0.0), axis=1, keepdims=True)
            chosen = jnp.where(own + e * capacity == slot, 1.0, chosen)
        choose = chosen.astype(BF)
        choose_v[at, :] = choose
        picked = mm_tn(choose, sec_v[at, :])
        cots = mm_tn(choose, cot_v[at, :D])
        for e in range(local_experts):
            mine = slice(e * capacity, (e + 1) * capacity)
            to = pl.ds(pl.multiple_of(e * per + b * capacity, capacity), capacity)
            x_v[to, :] = picked[mine, :D].astype(BF)
            c_v[to, :] = cots[mine].astype(BF)
            which = first_expert + e
            hits = (tail_lane == which) | (tail_lane == which + experts)
            prob = jnp.sum(jnp.where(hits, picked[mine, D:], 0.0), axis=1, keepdims=True)
            prob_v[to, :] = jnp.broadcast_to(prob, (capacity, 128))
        return carry

    lax.fori_loop(0, blocks, gather, 0)
    outs = []
    for e in range(local_experts):
        mine = pl.ds(e * per, per)
        outs.append(copy(x_v.at[mine], x_out.at[e, pl.ds(base, per)], sem_out, 2 * e))
        outs.append(copy(c_v.at[mine], c_out.at[e, pl.ds(base, per)], sem_out, 2 * e + 1))
    used = 2 * local_experts

    in_sin.wait()
    in_sdn.wait()
    shared = mm(sec_v[:, :D], sin_v[...])
    s_gate, s_up = shared[:, :wpad], shared[:, wpad:]
    s_sigma = jax.nn.sigmoid(s_gate)
    s_silu = s_gate * s_sigma
    s_grad = mm_nt(cot_v[:, :D], sdn_v[...])
    sact_v[...] = (s_silu * s_up).astype(BF)
    slow_v[:, :wpad] = (s_grad * s_up * (s_sigma * (1.0 + s_gate * (1.0 - s_sigma)))).astype(BF)
    slow_v[:, wpad:] = (s_grad * s_silu).astype(BF)
    sgp_v[...] = mm_tn(slow_v[...], sec_v[:, :D])
    sdp_v[...] = mm_tn(sact_v[...], cot_v[:, :D])
    cot_v[:, :D] = mm(sact_v[...], sdn_v[...]).astype(BF)
    sec_v[:, :D] = mm_nt(slow_v[...], sin_v[...]).astype(BF)
    outs.append(copy(sgp_v, sg_out, sem_out, used))
    outs.append(copy(sdp_v, sd_out, sem_out, used + 1))
    used += 2

    in_gate.wait()
    in_up.wait()
    in_down.wait()
    in_tail = z_v.shape[2] - D
    pair_lane = lax.broadcasted_iota(jnp.int32, (per, in_tail), 1)
    for e in range(local_experts):
        mine = pl.ds(e * per, per)
        x_e, c_e = x_v[mine, :], c_v[mine, :]
        gate = mm_nt(x_e, gate_v[e])
        up = mm_nt(x_e, up_v[e])
        pull = mm_nt(c_e, down_v[e])
        prob = prob_v[mine, :1]
        sigma = jax.nn.sigmoid(gate)
        silu = gate * sigma
        act = silu * up
        pair = jnp.sum(pull * act, axis=1, keepdims=True)
        pull = pull * prob
        gg_v[e] = (pull * up * (sigma * (1.0 + gate * (1.0 - sigma)))).astype(BF)
        ug_v[e] = (pull * silu).astype(BF)
        aw_v[e] = (act * prob).astype(BF)
        outs.append(copy(aw_v.at[e], aw_out.at[e, pl.ds(base, per)], sem_out, used))
        outs.append(copy(gg_v.at[e], gg_out.at[e, pl.ds(base, per)], sem_out, used + 1))
        outs.append(copy(ug_v.at[e], ug_out.at[e, pl.ds(base, per)], sem_out, used + 2))
        used += 3
        y = mm(aw_v[e], down_v[e]).astype(BF)
        y_v[:, e * capacity : (e + 1) * capacity, :] = y.reshape(blocks, capacity, D)
        zed = (mm(gg_v[e], gate_v[e]) + mm(ug_v[e], up_v[e])).astype(BF)
        z_v[:, e * capacity : (e + 1) * capacity, :D] = zed.reshape(blocks, capacity, D)
        pairs = jnp.where(pair_lane == first_expert + e, pair, 0.0).astype(BF)
        z_v[:, e * capacity : (e + 1) * capacity, D:] = pairs.reshape(blocks, capacity, in_tail)

    def block_copies(b):
        moves = []
        for i, (to_in, to_out) in enumerate(((in_a, out_a), (in_b, out_b))):
            at = pl.ds(pl.multiple_of(b * rows, rows), rows)
            from_at = pl.ds(pl.multiple_of(i * half + b * rows, rows), rows)
            moves.append(pltpu.make_async_copy(sec_v.at[from_at], to_in.at[at], sem_block.at[i, 0, b]))
            moves.append(
                pltpu.make_async_copy(cot_v.at[from_at, pl.ds(0, D)], to_out.at[at], sem_block.at[i, 1, b])
            )
        return moves

    def scatter(b, carry):
        for i in range(2):
            at = pl.ds(pl.multiple_of(i * half + b * rows, rows), rows)
            choose = choose_v[at, :]
            which = i * (half // rows) + b
            cot_v[at, :D] = (mm(choose, y_v[which]) + cot_v[at, :D].astype(F32)).astype(BF)
            back = mm(choose, z_v[which])
            sec_v[at, :D] = (back[:, :D] + sec_v[at, :D].astype(F32)).astype(BF)
            sec_v[at, D:] = back[:, D:].astype(BF)
        for move in block_copies(b):
            move.start()
        return carry

    lax.fori_loop(0, half // rows, scatter, 0)
    for b in range(half // rows):
        for move in block_copies(b):
            move.wait()
    for one in outs:
        one.wait()


def expert_group(place, sec, cot, weights, kept, capacity, rows, experts, groups):
    gate, up, down, sin, sdn = weights
    local_experts, hidden, _ = gate.shape
    half = sec[0].shape[0]
    tokens = 2 * half
    blocks = tokens // rows
    per = blocks * capacity
    slots = per * groups
    wpad = sdn.shape[0]
    in_width = D + lanes(experts)
    big = (local_experts, slots)
    shapes = [
        jax.ShapeDtypeStruct((*big, D), BF),
        jax.ShapeDtypeStruct((*big, D), BF),
        jax.ShapeDtypeStruct((*big, hidden), BF),
        jax.ShapeDtypeStruct((*big, hidden), BF),
        jax.ShapeDtypeStruct((*big, hidden), BF),
        jax.ShapeDtypeStruct((half, D), BF),
        jax.ShapeDtypeStruct((half, D), BF),
        jax.ShapeDtypeStruct((half, in_width), BF),
        jax.ShapeDtypeStruct((half, in_width), BF),
        jax.ShapeDtypeStruct((2 * wpad, D), F32),
        jax.ShapeDtypeStruct((wpad, D), F32),
    ]
    first = kept is None
    operands = [place, *sec, *cot, gate, up, down, sin, sdn] + ([] if first else list(kept))
    any_space = pl.BlockSpec(memory_space=pl.ANY)
    smem = pl.BlockSpec(memory_space=pltpu.SMEM)
    return pl.pallas_call(
        functools.partial(expert_kernel, local_experts, capacity, rows, experts, first),
        out_shape=shapes,
        in_specs=[smem] + [any_space] * (len(operands) - 1),
        out_specs=[any_space] * len(shapes),
        scratch_shapes=[
            pltpu.VMEM((tokens, sec[0].shape[1]), BF),
            pltpu.VMEM((tokens, cot[0].shape[1]), BF),
            pltpu.VMEM(gate.shape, BF),
            pltpu.VMEM(up.shape, BF),
            pltpu.VMEM(down.shape, BF),
            pltpu.VMEM(sin.shape, BF),
            pltpu.VMEM(sdn.shape, BF),
            pltpu.VMEM((local_experts * per, D), BF),
            pltpu.VMEM((local_experts * per, D), BF),
            pltpu.VMEM((blocks, local_experts * capacity, D), BF),
            pltpu.VMEM((blocks, local_experts * capacity, in_width), BF),
            pltpu.VMEM((local_experts, per, hidden), BF),
            pltpu.VMEM((local_experts, per, hidden), BF),
            pltpu.VMEM((local_experts, per, hidden), BF),
            pltpu.VMEM((tokens, local_experts * capacity), BF),
            pltpu.VMEM((local_experts * per, 128), F32),
            pltpu.VMEM((tokens, wpad), BF),
            pltpu.VMEM((tokens, 2 * wpad), BF),
            pltpu.VMEM((2 * wpad, D), F32),
            pltpu.VMEM((wpad, D), F32),
            pltpu.SemaphoreType.DMA((9,)),
            pltpu.SemaphoreType.DMA((5 * local_experts + 2,)),
            pltpu.SemaphoreType.DMA((2, 2, half // rows)),
        ],
        input_output_aliases={} if first else {10 + i: i for i in range(5)},
        compiler_params=pltpu.CompilerParams(vmem_limit_bytes=63 * 1024 * 1024),
        cost_estimate=pl.CostEstimate(flops=1 << 20, bytes_accessed=1 << 16, transcendentals=0),
    )(*operands)


def turn(values, cosine, sine):
    lane = lax.broadcasted_iota(jnp.int32, values.shape, 1)
    partner = jnp.where(
        lane % DR < DR // 2, pltpu.roll(values, 2 * DR - DR // 2, 1), pltpu.roll(values, DR // 2, 1)
    )
    return values * cosine + partner * sine


def score_block(i, block, image, scores):
    row = lax.broadcasted_iota(jnp.int32, scores.shape, 0) + i * block
    column = lax.broadcasted_iota(jnp.int32, scores.shape, 1)
    allowed = (column <= row) | ((column >= i * block) & image)
    return jnp.where(allowed, scores * ((DN + DR) ** (-0.5)), NEGATIVE)


def head_part(values, h):
    lane = lax.broadcasted_iota(jnp.int32, values.shape, 1)
    return jnp.where(lane // DR == h, values.astype(F32), 0.0).astype(BF)


def attend_kernel(
    heads, rows, place, seq, gain, lgain, wq, wd, wup, cos, sin, out, first, q_out, lat_out, kr_out, ex_out, own_out, down_v
):
    block = PIECE
    nope = heads * DN
    for i in range(seq.shape[0] // block):
        at = slice(i * block, (i + 1) * block)
        values = seq[at, :D].astype(F32)
        low = (values * rms_parts(values) * gain[...]).astype(BF)
        first[at, :] = low
        q = mm(low, wq[...])
        down = mm(low, wd[...])
        down_v[at, :] = down
        latent = down[:, :KVR]
        lat = (latent * rms_parts(latent) * lgain[...]).astype(BF)
        lat_out[at, :] = lat
        ex_out[at, :] = mm(lat, wup[...]).astype(BF)
        turned = turn(down[:, KVR : KVR + 2 * DR], cos[at, :], sin[at, :])
        lane = lax.broadcasted_iota(jnp.int32, turned.shape, 1)
        turned = jnp.where(lane < DR, turned, 0.0)
        kr_out[at, :] = (turned + pltpu.roll(turned, DR, 1)).astype(BF)
        q_rope = turn(q[:, nope:], cos[at, :], sin[at, :]).astype(BF)
        q_out[at, :nope] = q[:, :nope].astype(BF)
        q_out[at, nope:] = q_rope
        image = seq[at, D : D + 128][:, :1].astype(F32) > 0
        n = (i + 1) * block
        for h in range(heads):
            mine = slice(h * (DN + DV), h * (DN + DV) + DN)
            scores = mm_nt(q_out[at, h * DN : (h + 1) * DN], ex_out[:n, mine])
            scores = scores + mm_nt(head_part(q_rope, h), kr_out[:n, :])
            scores = score_block(i, block, image, scores)
            weight = jnp.exp(scores - jnp.max(scores, axis=1, keepdims=True))
            weight = weight / jnp.sum(weight, axis=1, keepdims=True)
            value = ex_out[:n, h * (DN + DV) + DN : (h + 1) * (DN + DV)]
            out[at, h * DV : (h + 1) * DV] = mm(weight.astype(BF), value).astype(BF)
    own_out[...] = down_v[pl.ds(pl.multiple_of(place[0] * rows, rows), rows), :]


def attend(place, seq, gain, lgain, wq, wd, wup, cos, sin, heads, rows):
    length = seq.shape[0]
    shapes = [
        jax.ShapeDtypeStruct((length, heads * DV), BF),
        jax.ShapeDtypeStruct((length, D), BF),
        jax.ShapeDtypeStruct((length, wq.shape[1]), BF),
        jax.ShapeDtypeStruct((length, KVR), BF),
        jax.ShapeDtypeStruct((length, 2 * DR), BF),
        jax.ShapeDtypeStruct((length, wup.shape[1]), BF),
        jax.ShapeDtypeStruct((rows, wd.shape[1]), F32),
    ]
    vmem = pl.BlockSpec(memory_space=pltpu.VMEM)
    return pl.pallas_call(
        functools.partial(attend_kernel, heads, rows),
        out_shape=shapes,
        in_specs=[pl.BlockSpec(memory_space=pltpu.SMEM)] + [vmem] * 8,
        out_specs=[vmem] * len(shapes),
        scratch_shapes=[pltpu.VMEM((length, wd.shape[1]), F32)],
        compiler_params=pltpu.CompilerParams(vmem_limit_bytes=56 * 1024 * 1024),
        cost_estimate=pl.CostEstimate(flops=1 << 20, bytes_accessed=1 << 16, transcendentals=0),
    )(place, seq, gain, lgain, wq, wd, wup, cos, sin)


def attend_back_kernel(
    heads, place, grad, flags, first, q, kr, ex, lat, wq, wup, cos, sin,
    gain_out, first_keep, first_send, lat_keep, lat_send, pack_out,
    dk_v, dv_v, dr_v, qg_v, eg_v,
):
    block = PIECE
    nope = heads * DN
    length = first.shape[0]
    half = length // 2
    scale = (DN + DR) ** (-0.5)
    dk_v[...] = jnp.zeros_like(dk_v)
    dv_v[...] = jnp.zeros_like(dv_v)
    dr_v[...] = jnp.zeros_like(dr_v)
    for i in range(length // block):
        at = slice(i * block, (i + 1) * block)
        n = (i + 1) * block
        image = flags[at, :1].astype(F32) > 0
        rope_grad = jnp.zeros((block, 2 * DR), F32)
        for h in range(heads):
            mine = slice(h * (DN + DV), h * (DN + DV) + DN)
            value = ex[:n, h * (DN + DV) + DN : (h + 1) * (DN + DV)]
            q_nope = q[at, h * DN : (h + 1) * DN]
            q_rope = head_part(q[at, nope:], h)
            scores = mm_nt(q_nope, ex[:n, mine]) + mm_nt(q_rope, kr[:n, :])
            scores = score_block(i, block, image, scores)
            weight = jnp.exp(scores - jnp.max(scores, axis=1, keepdims=True))
            weight = weight / jnp.sum(weight, axis=1, keepdims=True)
            upstream = grad[at, h * DV : (h + 1) * DV]
            dprob = mm_nt(upstream, value)
            dv_v[:n, h * DV : (h + 1) * DV] += mm_tn(weight.astype(BF), upstream)
            inner = jnp.sum(weight * dprob, axis=1, keepdims=True)
            back = (weight * (dprob - inner)).astype(BF)
            qg_v[at, h * DN : (h + 1) * DN] = (mm(back, ex[:n, mine]) * scale).astype(BF)
            turned = mm(back, kr[:n, :])
            lane = lax.broadcasted_iota(jnp.int32, turned.shape, 1)
            rope_grad = jnp.where(lane // DR == h, turned * scale, rope_grad)
            dk_v[:n, h * DN : (h + 1) * DN] += mm_tn(back, q_nope)
            dr_v[:n, :] += mm_tn(back, q_rope)
        qg_v[at, nope:] = turn(rope_grad, cos[at, :], -sin[at, :]).astype(BF)
    for h in range(heads):
        mine = slice(h * (DN + DV), h * (DN + DV) + DN)
        eg_v[:, mine] = (dk_v[:, h * DN : (h + 1) * DN] * scale).astype(BF)
        eg_v[:, h * (DN + DV) + DN : (h + 1) * (DN + DV)] = dv_v[:, h * DV : (h + 1) * DV].astype(BF)
    key_rope = dr_v[...]
    key_rope = (key_rope + pltpu.roll(key_rope, DR, 1)) * scale
    dr_v[...] = key_rope
    keep = pl.ds(pl.multiple_of(place[1] * half, half), half)
    send = pl.ds(pl.multiple_of((1 - place[1]) * half, half), half)
    total = jnp.zeros((1, D), F32)
    for at, to_lat, to_first in ((send, lat_send, first_send), (keep, lat_keep, first_keep)):
        to_lat[:, :KVR] = mm_nt(eg_v[at, :], wup[...]).astype(BF)
        to_lat[:, KVR:] = dr_v[at, :].astype(BF)
        part = mm_nt(qg_v[at, :], wq[...])
        to_first[...] = part.astype(BF)
        total = total + jnp.sum(part * first[at, :].astype(F32), axis=0, keepdims=True)
    gain_out[...] = total
    owners, pack_rows, _ = pack_out.shape
    wide = wq.shape[1]
    q_rows = D // owners
    pack_out[:, :q_rows, :wide] = mm_tn(first[...], qg_v[...]).astype(BF).reshape(owners, q_rows, wide)
    pack_out[:, :q_rows, wide:] = jnp.zeros((owners, q_rows, pack_out.shape[2] - wide), BF)
    pack_out[:, q_rows:, :] = mm_tn(lat[...], eg_v[...]).astype(BF).reshape(owners, pack_rows - q_rows, -1)


def attend_back(place, grad, flags, first, q, kr, ex, lat, wq, wup, cos, sin, heads, owners):
    length = first.shape[0]
    half = length // 2
    wide = KVR + 2 * DR
    shapes = [
        jax.ShapeDtypeStruct((1, D), F32),
        jax.ShapeDtypeStruct((half, D), BF),
        jax.ShapeDtypeStruct((half, D), BF),
        jax.ShapeDtypeStruct((half, wide), BF),
        jax.ShapeDtypeStruct((half, wide), BF),
        jax.ShapeDtypeStruct((owners, (D + KVR) // owners, wup.shape[1]), BF),
    ]
    vmem = pl.BlockSpec(memory_space=pltpu.VMEM)
    return pl.pallas_call(
        functools.partial(attend_back_kernel, heads),
        out_shape=shapes,
        in_specs=[pl.BlockSpec(memory_space=pltpu.SMEM)] + [vmem] * 11,
        out_specs=[vmem] * len(shapes),
        scratch_shapes=[
            pltpu.VMEM((length, heads * DN), F32),
            pltpu.VMEM((length, heads * DV), F32),
            pltpu.VMEM((length, 2 * DR), F32),
            pltpu.VMEM((length, q.shape[1]), BF),
            pltpu.VMEM((length, ex.shape[1]), BF),
        ],
        compiler_params=pltpu.CompilerParams(vmem_limit_bytes=56 * 1024 * 1024),
        cost_estimate=pl.CostEstimate(flops=1 << 20, bytes_accessed=1 << 16, transcendentals=0),
    )(place, grad, flags, first, q, kr, ex, lat, wq, wup, cos, sin)


def on_device(
    tokens,
    attention_norm,
    query_weight,
    latent_down,
    latent_norm,
    latent_up,
    output_weight,
    post_norm,
    shared_gate,
    shared_up,
    shared_down,
    router_weight,
    expert_gate,
    expert_up,
    expert_down,
    image_piece_index,
    routes,
    cotangent,
):
    rows = tokens.shape[0]
    c_size, k_size, z_size = (lax.axis_size(a) for a in EVERY)
    c, k, z = (lax.axis_index(a) for a in EVERY)
    column_size = k_size * z_size
    device_count = c_size * column_size
    local_experts = expert_gate.shape[0]
    experts = router_weight.shape[1]
    capacity = rows * TOPK * 4 // (3 * experts)
    length = column_size * rows
    heads = H // column_size
    width = shared_down.shape[0]
    score_scale = (DN + DR) ** (-0.5)
    weight_rows = query_weight.shape[0]
    up_rows = latent_up.shape[0]

    paired = H == 4 * c_size and heads == 2 and column_size == 8

    def by_owner(array, n):
        if paired:
            array = array.reshape(-1, 2, 2, 4, n).transpose(0, 3, 1, 2, 4)
        return array.reshape(-1, column_size, heads * n)

    def by_head(array, n):
        if paired:
            array = array.reshape(-1, 4, 2, 2, n).transpose(0, 2, 3, 1, 4)
        return array.reshape(-1, H * n)

    flag = (image_piece_index > 0).astype(BF)[:, None]
    expert_ids = jnp.arange(experts, dtype=jnp.int32)
    named = jnp.any(routes[:, :, None] == expert_ids[None, None, :], axis=1)

    out_mine = in_order(gather_z(output_weight.astype(BF)), z)
    extra = -(-weight_rows // 8) * 8 + 8 - weight_rows
    down_width = KVR + DR
    small_width = lanes(max(down_width + experts + 8, weight_rows))
    gains = jnp.stack(
        [attention_norm, post_norm, jnp.pad(latent_norm, (0, weight_rows - latent_norm.shape[0]))]
    )
    small = jnp.concatenate([latent_down, router_weight], axis=1).astype(BF)
    small = jnp.pad(small, ((0, 0), (0, small_width - small.shape[1])))
    gains = jnp.pad(gains.astype(BF), ((0, extra - 3), (0, small_width - weight_rows)))
    small = jnp.concatenate([small, gains], axis=0)
    q_width = heads * (DN + DR)
    kv_width = heads * (DN + DV)
    q_out = by_owner(query_weight.astype(BF), DN + DR).transpose(1, 0, 2)
    q_out = q_out.reshape(column_size, weight_rows, heads, DN + DR)
    q_out = jnp.concatenate(
        [q_out[..., :DN].reshape(column_size, weight_rows, -1), q_out[..., DN:].reshape(column_size, weight_rows, -1)],
        axis=2,
    )
    q_out = jnp.pad(q_out, ((0, 0), (0, 0), (0, kv_width - q_width)))
    up_out = by_owner(latent_up.astype(BF), DN + DV).transpose(1, 0, 2)
    head_pack = jnp.concatenate([q_out, up_out], axis=1)
    head_pack = lax.all_to_all(head_pack, COLUMN, split_axis=0, concat_axis=0, tiled=True)
    token_units = gather_z(after(widen(tokens, flag), head_pack))
    cot_units = gather_z(after(widen(cotangent, named), *token_units[1:]))
    head_pack = [head_pack] + [swap(head_pack, "c", d) for d in range(1, c_size)]
    small, small_recv = gather_weight(small)
    mine = in_order(after_all(token_units, *head_pack[1:], *small_recv), z)
    sequence = in_order([mine, swap(mine, "k", 1)], k).reshape(length, -1)
    small = small.reshape(device_count, weight_rows + extra, small_width)
    full_small = small[:, :weight_rows].reshape(D, small_width)
    full_router = full_small[:, down_width : down_width + experts]
    full_gains = small[:, weight_rows : weight_rows + 3, :weight_rows].astype(F32)
    attn_gain = full_gains[:, 0].reshape(D)
    post_gain = full_gains[:, 1].reshape(D)
    latent_gain = full_gains[:, 2, : latent_norm.shape[0]].reshape(KVR)
    out_mine = after(out_mine, *head_pack[1:])
    out_planes = [out_mine] + [swap(out_mine, "c", d) for d in range(1, c_size)]
    head_pack = in_order(head_pack, c)
    head_query = head_pack[:, :, :weight_rows, :q_width].reshape(D, q_width)
    head_up = head_pack[:, :, weight_rows:].reshape(KVR, kv_width)
    shared_pack = jnp.concatenate(
        [
            shared_gate.astype(BF).reshape(weight_rows, device_count, width),
            shared_up.astype(BF).reshape(weight_rows, device_count, width),
        ],
        axis=2,
    ).transpose(1, 0, 2)
    shared_in = lax.all_to_all(after(shared_pack, *token_units[1:]), EVERY, split_axis=0, concat_axis=0, tiled=True)
    shared_low = shared_down.astype(BF)

    places = jnp.arange(length, dtype=F32)
    frequency = ROPE_BASE ** (-2.0 * jnp.arange(DR // 2, dtype=F32) / DR)
    angles = places[:, None] * frequency[None, :]
    cosine, sine = jnp.cos(angles), jnp.sin(angles)
    cosine_wide = jnp.tile(cosine, (1, 4))
    sine_wide = jnp.tile(jnp.concatenate([-sine, sine], axis=1), (1, 2))
    here = k * z_size + z

    def own_rows(array):
        return lax.dynamic_slice_in_dim(array, here * rows, rows, axis=0)

    spot = jnp.stack([here, k]).astype(jnp.int32)
    heads_out, first_low, query_low, latent_low, rope_low, expanded, down_raw = attend(
        spot, sequence, attn_gain[None], latent_gain[None], head_query, full_small, head_up,
        cosine_wide, sine_wide, heads, rows,
    )
    own_values = tokens.astype(F32)
    own_scale = rms_parts(own_values)
    own_first_low = (own_values * own_scale * attn_gain).astype(BF)
    latent_raw = down_raw[:, :KVR]
    latent_scale = rms_parts(latent_raw)

    def heads_to_tokens(array):
        n = array.shape[1]
        moved = lax.all_to_all(
            array.reshape(column_size, rows, n), COLUMN, split_axis=0, concat_axis=0, tiled=True
        )
        return by_head(moved.transpose(1, 0, 2), n // heads)

    def tokens_to_heads(array):
        n = array.shape[1] // H
        moved = lax.all_to_all(
            by_owner(array, n).transpose(1, 0, 2), COLUMN, split_axis=0, concat_axis=0, tiled=True
        )
        return moved.reshape(length, heads * n)

    shared_in, *cot_units = after_all([shared_in, *cot_units], heads_out)
    cot_own = jnp.concatenate(cot_units, axis=0)
    shared_in = shared_in.reshape(D, 2 * width)
    room = ((0, 0), (0, lanes(width) - width))
    shared_in = jnp.concatenate(
        [jnp.pad(shared_in[:, :width], room), jnp.pad(shared_in[:, width:], room)], axis=1
    )
    out_planes = in_order(after_all(out_planes, heads_out, cot_own), c)
    full_out = in_order([out_planes, swap(out_planes, "k", 1)], k)
    full_out = full_out.transpose(1, 0, 2, 3, 4).reshape(D, D)

    def plane_groups(own):
        near = [swap(own, "c", d) for d in range(1, c_size - 1)]
        return [own, *near, swap(after(own, *near), "c", c_size - 1)]

    cot_groups = plane_groups(cot_own)
    heads_low = after(
        heads_to_tokens(after(heads_out, cot_own, shared_in)), full_out, *cot_groups[1:-1]
    )
    residual = tokens.astype(F32) + mm(heads_low, full_out)
    second_scale = rms_parts(residual)
    second_low = (residual * second_scale * post_gain).astype(BF)
    router_probs = jax.nn.softmax(mm(second_low, full_router), axis=-1)

    probs_high = router_probs.astype(BF)
    probs_rest = (router_probs - probs_high.astype(F32)).astype(BF)
    second_own = jnp.concatenate(
        gather_z(widen(second_low, jnp.concatenate([probs_high, probs_rest], axis=1))), axis=0
    )
    second_own = after(second_own, cot_groups[-1])
    second_groups = plane_groups(second_own)
    pair = lambda group: (group, swap(group, "k", 1))
    cot_groups = [pair(g) for g in cot_groups]
    wpad = lanes(width)
    place = jnp.stack([(c * k_size + k) * local_experts, jnp.zeros((), jnp.int32)]).astype(jnp.int32)
    shared_rows = jnp.pad(shared_low, ((0, wpad - width), (0, 0)))
    weights = (
        jnp.swapaxes(expert_gate, 1, 2),
        jnp.swapaxes(expert_up, 1, 2),
        expert_down,
        shared_in,
        shared_rows,
    )
    kept, sg_parts, sd_parts, sums, out_sums, marks = None, [], [], [], [], []
    arrived = []
    for d in range(c_size):
        where = place.at[1].set(d)
        group = second_groups[d]
        if d:
            group = after(group, marks[max(d - 2, 0)])
        if d > 1:
            where = after(where, out_sums[d - 2], sums[d - 1])
        results = list(
            expert_group(
                where, pair(group), cot_groups[d], weights, kept, capacity, rows, experts, c_size
            )
        )
        kept = results[:5]
        marks.append(results[10])
        if d == c_size - 1:
            results[8] = after(results[8], *arrived)
        sums.append(core_sum(*results[7:9], d))
        if d:
            arrived.append(swap(sums[d], "c", d))
        if d == c_size - 1:
            kept = after_all(kept, *arrived[:-1])
            results[6] = after(results[6], arrived[-1])
        out_sums.append(core_sum(*results[5:7], d))
        sg_parts.append(results[9])
        sd_parts.append(results[10])
    plane = functools.reduce(lambda total, block: total + block.astype(F32), arrived, sums[0])
    expert_in, cot_in, act_weighted, gate_grad, up_grad = kept
    ein = lambda spec, a, b: jnp.einsum(spec, a, b, preferred_element_type=F32)
    expert_down_grad = ein("esf,esd->efd", act_weighted, cot_in)
    expert_gate_grad = jnp.swapaxes(ein("esf,esd->efd", gate_grad, expert_in), 1, 2)
    expert_up_grad = jnp.swapaxes(ein("esf,esd->efd", up_grad, expert_in), 1, 2)
    plane = after(plane, expert_down_grad, expert_gate_grad, expert_up_grad)
    second_sum = scatter_z(z_units(plane, rows))
    out_near = [swap(after(out_sums[d], *arrived), "c", d) for d in range(1, c_size - 1)]
    second_sum = after(second_sum, *out_near, out_sums[-1])
    out_far = swap(after(out_sums[-1], *out_near), "c", c_size - 1)
    probs_grad = second_sum[:, D : D + experts]
    logits_grad = (
        router_probs * (probs_grad - jnp.sum(router_probs * probs_grad, axis=-1, keepdims=True))
    ).astype(BF)
    second_grad = second_sum[:, :D] + mm_nt(logits_grad, full_router)
    norm_part, post_terms = rms_back(residual, second_scale, post_gain, second_grad)
    residual_grad = cotangent.astype(F32) + norm_part
    attn_grad_low = residual_grad.astype(BF)
    heads_grad = tokens_to_heads(mm_nt(attn_grad_low, full_out).astype(BF))
    output_pieces = core_pieces(mm_tn(heads_low, attn_grad_low).astype(BF))

    gain_part, first_keep, first_send, latent_keep, latent_send, head_grad = attend_back(
        after(spot, *output_pieces), heads_grad, sequence[:, D:], first_low, query_low,
        rope_low, expanded, latent_low, head_query, head_up, cosine_wide, sine_wide, heads, device_count,
    )
    def column_sum(keep, send):
        summed = keep.astype(F32) + swap(send, "k", 1).astype(F32)
        summed = summed.reshape(z_size, rows, keep.shape[1])
        return scatter_z([pick(summed, z ^ d) for d in range(z_size)])

    latent_sum = column_sum(latent_keep, after(latent_send, out_far))
    out_plane = functools.reduce(
        lambda total, block: total + block.astype(F32),
        after_all([*out_near, out_far], latent_sum),
        out_sums[0],
    )
    out_units = z_units(out_plane, rows)
    out_units = out_units[:1] + [swap(unit.astype(BF), "z", d) for d, unit in enumerate(out_units) if d]
    first_keep = after(first_keep, latent_sum)
    shared_in_grad = sum(sg_parts[1:], sg_parts[0])
    shared_in_grad = jnp.concatenate(
        [shared_in_grad[:width], shared_in_grad[wpad : wpad + width]], axis=0
    ).astype(BF)
    shared_down_grad = sum(sd_parts[1:], sd_parts[0])[:width]
    shared_back = shared_in_grad.reshape(2 * width, c_size, column_size, weight_rows).transpose(2, 1, 3, 0)
    shared_back = lax.all_to_all(
        after(shared_back, latent_keep), COLUMN, split_axis=0, concat_axis=0, tiled=True
    )
    latent_raw_grad, latent_terms = rms_back(
        latent_raw, latent_scale, latent_gain, latent_sum[:, :KVR]
    )
    rope_raw_grad = rotate(
        latent_sum[:, KVR:down_width], own_rows(cosine), own_rows(sine), -1.0
    )
    down_grad_low = jnp.concatenate([latent_raw_grad, rope_raw_grad], axis=-1).astype(BF)
    first_own = mm_nt(down_grad_low, full_small[:, :down_width])
    attn_gain_grad = gain_part[0] / attn_gain + jnp.sum(
        first_own * (own_values * own_scale), axis=0
    )
    gain_grads = jnp.stack(
        [
            attn_gain_grad,
            jnp.sum(post_terms, axis=0),
            jnp.pad(
                jnp.sum(latent_terms, axis=0).reshape(device_count, latent_norm.shape[0]),
                ((0, 0), (0, weight_rows - latent_norm.shape[0])),
            ).reshape(D),
        ]
    )
    first_gain = down_width + experts
    small_right = jnp.zeros((2 * rows + 8, small_width), BF)
    small_right = small_right.at[:rows, :down_width].set(down_grad_low)
    small_right = small_right.at[rows : 2 * rows, down_width:first_gain].set(logits_grad)
    ones = (jnp.arange(8)[:, None] == jnp.arange(small_width)[None, :] - first_gain).astype(BF)
    small_right = small_right.at[2 * rows :].set(ones)
    small_left = jnp.concatenate(
        [own_first_low, second_low, jnp.pad(gain_grads, ((0, 5), (0, 0))).astype(BF)], axis=0
    )
    output_moved = [swap(block, "c", d) for d, block in enumerate(output_pieces) if d]
    small_left = after(small_left, *output_moved)
    small_pieces = core_pieces(mm_tn(small_left, small_right).astype(BF))
    head_grad = head_grad.reshape(c_size, column_size, weight_rows + up_rows, kv_width)
    head_moved = [swap(pick(head_grad, c ^ d), "c", d) for d in range(1, c_size)]
    small_plane, _ = plane_sum(small_pieces, *head_moved)
    output_plane = functools.reduce(
        lambda total, block: total + block.astype(F32),
        after_all(output_moved, small_plane),
        output_pieces[0],
    )
    shared_back = after(shared_back, small_plane)
    shared_back = in_order(
        [
            swap(lax.dynamic_index_in_dim(shared_back, c ^ d, axis=1, keepdims=False), "c", d)
            if d
            else lax.dynamic_index_in_dim(shared_back, c, axis=1, keepdims=False)
            for d in range(c_size)
        ],
        c,
    ).reshape(device_count, weight_rows, 2 * width).transpose(1, 0, 2)
    first_grad = after(column_sum(first_keep, first_send), small_plane) + first_own
    out_sum = functools.reduce(
        lambda total, block: total + block.astype(F32), after_all(out_units[1:], first_grad), out_units[0]
    )
    layer_out = (residual + out_sum).astype(BF)
    first_norm_grad, _ = rms_back(own_values, own_scale, attn_gain, first_grad)
    tokens_grad = residual_grad + first_norm_grad
    own_small = z_sum(small_plane)
    own_output = z_sum(output_plane)
    head_sum = pick(head_grad, c).astype(F32)
    for block in after_all(head_moved, small_plane):
        head_sum = head_sum + block.astype(F32)
    head_sum = lax.all_to_all(head_sum.astype(BF), COLUMN, split_axis=0, concat_axis=0, tiled=True)
    own_query = head_sum[:, :weight_rows, :q_width].transpose(1, 0, 2)
    own_query = jnp.concatenate(
        [
            own_query[..., : heads * DN].reshape(weight_rows, column_size, heads, DN),
            own_query[..., heads * DN :].reshape(weight_rows, column_size, heads, DR),
        ],
        axis=3,
    )
    own_query = by_head(own_query.reshape(weight_rows, column_size, q_width), DN + DR)
    own_up = by_head(head_sum[:, weight_rows:].transpose(1, 0, 2), DN + DV)
    own_gate = shared_back[:, :, :width].reshape(weight_rows, -1)
    own_shared_up = shared_back[:, :, width:].reshape(weight_rows, -1)
    return (
        layer_out,
        tokens_grad,
        own_small[:, first_gain],
        own_query.astype(F32),
        own_small[:, :down_width],
        own_small[: latent_norm.shape[0], first_gain + 2],
        own_up.astype(F32),
        own_output,
        own_small[:, first_gain + 1],
        own_gate.astype(F32),
        own_shared_up.astype(F32),
        shared_down_grad,
        own_small[:, down_width:first_gain],
        expert_gate_grad,
        expert_up_grad,
        expert_down_grad,
    )


def solution(mesh):
    expert_size, z_size = mesh.devices.shape
    fine = Mesh(mesh.devices.reshape(expert_size // 2, 2, z_size), EVERY)
    row, flat = P(EVERY, None), P(EVERY)
    wide, tall = P(("c", "k"), None, "z"), P(("c", "k"), "z", None)
    return jax.shard_map(
        on_device,
        mesh=fine,
        in_specs=(row, flat, row, row, flat, row, row, flat, row, row, row, row)
        + (wide, wide, tall, flat, row, row),
        out_specs=(row, row, flat, row, row, flat, row, row, flat, row, row, row, row)
        + (wide, wide, tall),
        check_vma=False,
    )
```

```python
import functools

import jax
import jax.numpy as jnp
from jax import lax
from jax.experimental import pallas as pl
from jax.experimental.pallas import tpu as pltpu
from jax.sharding import Mesh, PartitionSpec as P

D = 2048
H = 16
DN = 128
DR = 64
DV = 128
KVR = 512
TOPK = 6
PIECE = 256
EPSILON = 1e-06
ROPE_BASE = 10000.0
NEGATIVE = -1e30
BF = jnp.bfloat16
F32 = jnp.float32
EVERY = ("c", "k", "z")
COLUMN = ("k", "z")


def swap(block, axis, distance):
    n = lax.axis_size(axis)
    return lax.ppermute(block, axis, [(i, i ^ distance) for i in range(n)])


def lanes(n):
    return -(-n // 128) * 128


def widen(block, extra):
    room = lanes(extra.shape[1]) - extra.shape[1]
    return jnp.concatenate([block, jnp.pad(extra.astype(BF), ((0, 0), (0, room)))], axis=1)


def dot(a, b, dims):
    return lax.dot_general(a, b, (dims, ((), ())), preferred_element_type=F32)


def mm(a, b):
    return dot(a, b, ((1,), (0,)))


def mm_nt(a, b):
    return dot(a, b, ((1,), (1,)))


def mm_tn(a, b):
    return dot(a, b, ((0,), (0,)))


def after(array, *others):
    return lax.optimization_barrier((array, *others))[0]


def after_all(arrays, *others):
    return lax.optimization_barrier((tuple(arrays), *others))[0]


def put(buffer, block, index):
    return lax.dynamic_update_slice_in_dim(buffer, block[None], index, axis=0)


def gather_z(unit):
    return [unit] + [swap(unit, "z", d) for d in range(1, lax.axis_size("z"))]


def in_order(blocks, index):
    whole = jnp.zeros((len(blocks), *blocks[0].shape), blocks[0].dtype)
    for d, block in enumerate(blocks):
        whole = put(whole, block, index ^ d)
    return whole


def gather_weight(unit):
    c_size, k_size, _ = (lax.axis_size(a) for a in EVERY)
    c, k, z = (lax.axis_index(a) for a in EVERY)
    mine = in_order(gather_z(unit), z)
    planes = [mine] + [swap(mine, "c", d) for d in range(1, c_size)]
    own = in_order(planes, c)
    other = swap(own, "k", 1)
    halves = in_order([own, other], k)
    return halves.transpose(1, 0, 2, 3, 4), planes[1:]


def scatter_z(blocks):
    total = blocks[0]
    for d in range(1, len(blocks)):
        total = total + swap(blocks[d].astype(BF), "z", d).astype(F32)
    return total


def scatter_column(part, rows):
    z_size = lax.axis_size("z")
    k, z = lax.axis_index("k"), lax.axis_index("z")
    grid = part.reshape(2, z_size, rows, part.shape[1])
    summed = pick(grid, k) + swap(pick(grid, k ^ 1).astype(BF), "k", 1).astype(F32)
    return scatter_z([pick(summed, z ^ d) for d in range(z_size)])


def core_sum(own, other, distance):
    summed = own.astype(F32) + swap(other, "k", 1).astype(F32)
    return summed.astype(BF) if distance else summed


def plane_sum(sums, *others):
    moved = [swap(block, "c", d) for d, block in enumerate(sums) if d]
    if others:
        moved = after_all(moved, *others)
    total = sums[0]
    for block in moved:
        total = total + block.astype(F32)
    return total, moved


def z_units(total, rows):
    return [total[d * rows : (d + 1) * rows] for d in range(lax.axis_size("z"))]


def pick(array, index):
    return lax.dynamic_index_in_dim(array, index, axis=0, keepdims=False)


def core_pieces(part):
    c_size, k_size, z_size = (lax.axis_size(a) for a in EVERY)
    c, k = lax.axis_index("c"), lax.axis_index("k")
    grid = part.reshape(c_size, k_size, part.shape[0] // (c_size * k_size), part.shape[1])
    got = swap(lax.dynamic_index_in_dim(grid, k ^ 1, axis=1, keepdims=False), "k", 1)
    kept = lax.dynamic_index_in_dim(grid, k, axis=1, keepdims=False)
    pieces = []
    for d in range(c_size):
        piece = pick(kept, c ^ d).astype(F32) + pick(got, c ^ d).astype(F32)
        pieces.append(piece.astype(BF) if d else piece)
    return pieces


def pieces_sum(pieces, *others):
    total, _ = plane_sum(pieces, *others)
    return z_sum(total)


def z_sum(total):
    z_size, z = lax.axis_size("z"), lax.axis_index("z")
    total = total.reshape(z_size, total.shape[0] // z_size, total.shape[1])
    return scatter_z([pick(total, z ^ d) for d in range(z_size)])


def scatter_weight(part):
    return pieces_sum(core_pieces(part))


def rms_parts(values):
    return lax.rsqrt(jnp.mean(values * values, axis=-1, keepdims=True) + EPSILON)


def rms_back(values, scale, gain, grad):
    weighted = grad * gain
    inner = jnp.mean(weighted * values, axis=-1, keepdims=True)
    return scale * (weighted - values * (scale * scale * inner)), grad * values * scale


def rotate(values, cosine, sine, sign):
    half = values.shape[-1] // 2
    a, b = values[..., :half], values[..., half:]
    return jnp.concatenate([a * cosine - sign * b * sine, b * cosine + sign * a * sine], axis=-1)


def expert_kernel(
    local_experts,
    capacity,
    rows,
    experts,
    first,
    place_ref,
    sec_a,
    sec_b,
    cot_a,
    cot_b,
    gate_hbm,
    up_hbm,
    down_hbm,
    sin_hbm,
    sdn_hbm,
    *rest,
):
    rest = rest if first else rest[5:]
    (x_out, c_out, aw_out, gg_out, ug_out, out_a, out_b, in_a, in_b, sg_out, sd_out) = rest[:11]
    (sec_v, cot_v, gate_v, up_v, down_v, sin_v, sdn_v, x_v, c_v, y_v, z_v, aw_v, gg_v, ug_v) = rest[11:25]
    (choose_v, prob_v, sact_v, slow_v, sgp_v, sdp_v, sem_in, sem_out, sem_block) = rest[25:34]
    half = sec_a.shape[0]
    blocks = 2 * half // rows
    per = blocks * capacity
    wpad = sdn_v.shape[0]
    base = place_ref[1] * per

    def copy(src, dst, sem, i):
        made = pltpu.make_async_copy(src, dst, sem.at[i])
        made.start()
        return made

    in_sec = [
        copy(sec_a, sec_v.at[pl.ds(0, half)], sem_in, 0),
        copy(sec_b, sec_v.at[pl.ds(half, half)], sem_in, 1),
    ]
    in_cot = [
        copy(cot_a, cot_v.at[pl.ds(0, half)], sem_in, 2),
        copy(cot_b, cot_v.at[pl.ds(half, half)], sem_in, 3),
    ]
    for one in in_cot:
        one.wait()

    first_expert = place_ref[0]
    tail = cot_v.shape[1] - D
    row_i = lax.broadcasted_iota(jnp.int32, (rows, rows), 0)
    col_i = lax.broadcasted_iota(jnp.int32, (rows, rows), 1)
    earlier = (col_i < row_i).astype(BF)
    lane = lax.broadcasted_iota(jnp.int32, (rows, tail), 1)
    slot = lax.broadcasted_iota(jnp.int32, (rows, local_experts * capacity), 1).astype(F32)
    for one in in_sec:
        one.wait()
    in_sin = copy(sin_hbm, sin_v, sem_in, 7)
    in_sdn = copy(sdn_hbm, sdn_v, sem_in, 8)
    in_gate = copy(gate_hbm, gate_v, sem_in, 4)
    in_up = copy(up_hbm, up_v, sem_in, 5)
    in_down = copy(down_hbm, down_v, sem_in, 6)
    sec_tail = sec_v.shape[1] - D
    tail_lane = lax.broadcasted_iota(jnp.int32, (capacity, sec_tail), 1)

    def gather(b, carry):
        at = pl.ds(pl.multiple_of(b * rows, rows), rows)
        named = cot_v[at, D:]
        rank = mm(earlier, named)
        code = jnp.where((named.astype(F32) > 0) & (rank < capacity), rank, -1e6)
        chosen = jnp.zeros(slot.shape, F32)
        for e in range(local_experts):
            own = jnp.sum(jnp.where(lane == first_expert + e, code, 0.0), axis=1, keepdims=True)
            chosen = jnp.where(own + e * capacity == slot, 1.0, chosen)
        choose = chosen.astype(BF)
        choose_v[at, :] = choose
        picked = mm_tn(choose, sec_v[at, :])
        cots = mm_tn(choose, cot_v[at, :D])
        for e in range(local_experts):
            mine = slice(e * capacity, (e + 1) * capacity)
            to = pl.ds(pl.multiple_of(e * per + b * capacity, capacity), capacity)
            x_v[to, :] = picked[mine, :D].astype(BF)
            c_v[to, :] = cots[mine].astype(BF)
            which = first_expert + e
            hits = (tail_lane == which) | (tail_lane == which + experts)
            prob = jnp.sum(jnp.where(hits, picked[mine, D:], 0.0), axis=1, keepdims=True)
            prob_v[to, :] = jnp.broadcast_to(prob, (capacity, 128))
        return carry

    lax.fori_loop(0, blocks, gather, 0)
    outs = []
    for e in range(local_experts):
        mine = pl.ds(e * per, per)
        outs.append(copy(x_v.at[mine], x_out.at[e, pl.ds(base, per)], sem_out, 2 * e))
        outs.append(copy(c_v.at[mine], c_out.at[e, pl.ds(base, per)], sem_out, 2 * e + 1))
    used = 2 * local_experts

    in_sin.wait()
    in_sdn.wait()
    shared = mm(sec_v[:, :D], sin_v[...])
    s_gate, s_up = shared[:, :wpad], shared[:, wpad:]
    s_sigma = jax.nn.sigmoid(s_gate)
    s_silu = s_gate * s_sigma
    s_grad = mm_nt(cot_v[:, :D], sdn_v[...])
    sact_v[...] = (s_silu * s_up).astype(BF)
    slow_v[:, :wpad] = (s_grad * s_up * (s_sigma * (1.0 + s_gate * (1.0 - s_sigma)))).astype(BF)
    slow_v[:, wpad:] = (s_grad * s_silu).astype(BF)
    sgp_v[...] = mm_tn(slow_v[...], sec_v[:, :D])
    sdp_v[...] = mm_tn(sact_v[...], cot_v[:, :D])
    cot_v[:, :D] = mm(sact_v[...], sdn_v[...]).astype(BF)
    sec_v[:, :D] = mm_nt(slow_v[...], sin_v[...]).astype(BF)
    outs.append(copy(sgp_v, sg_out, sem_out, used))
    outs.append(copy(sdp_v, sd_out, sem_out, used + 1))
    used += 2

    in_gate.wait()
    in_up.wait()
    in_down.wait()
    in_tail = z_v.shape[2] - D
    pair_lane = lax.broadcasted_iota(jnp.int32, (per, in_tail), 1)
    for e in range(local_experts):
        mine = pl.ds(e * per, per)
        x_e, c_e = x_v[mine, :], c_v[mine, :]
        gate = mm_nt(x_e, gate_v[e])
        up = mm_nt(x_e, up_v[e])
        pull = mm_nt(c_e, down_v[e])
        prob = prob_v[mine, :1]
        sigma = jax.nn.sigmoid(gate)
        silu = gate * sigma
        act = silu * up
        pair = jnp.sum(pull * act, axis=1, keepdims=True)
        pull = pull * prob
        gg_v[e] = (pull * up * (sigma * (1.0 + gate * (1.0 - sigma)))).astype(BF)
        ug_v[e] = (pull * silu).astype(BF)
        aw_v[e] = (act * prob).astype(BF)
        outs.append(copy(aw_v.at[e], aw_out.at[e, pl.ds(base, per)], sem_out, used))
        outs.append(copy(gg_v.at[e], gg_out.at[e, pl.ds(base, per)], sem_out, used + 1))
        outs.append(copy(ug_v.at[e], ug_out.at[e, pl.ds(base, per)], sem_out, used + 2))
        used += 3
        y = mm(aw_v[e], down_v[e]).astype(BF)
        y_v[:, e * capacity : (e + 1) * capacity, :] = y.reshape(blocks, capacity, D)
        zed = (mm(gg_v[e], gate_v[e]) + mm(ug_v[e], up_v[e])).astype(BF)
        z_v[:, e * capacity : (e + 1) * capacity, :D] = zed.reshape(blocks, capacity, D)
        pairs = jnp.where(pair_lane == first_expert + e, pair, 0.0).astype(BF)
        z_v[:, e * capacity : (e + 1) * capacity, D:] = pairs.reshape(blocks, capacity, in_tail)

    def block_copies(b):
        moves = []
        for i, (to_in, to_out) in enumerate(((in_a, out_a), (in_b, out_b))):
            at = pl.ds(pl.multiple_of(b * rows, rows), rows)
            from_at = pl.ds(pl.multiple_of(i * half + b * rows, rows), rows)
            moves.append(pltpu.make_async_copy(sec_v.at[from_at], to_in.at[at], sem_block.at[i, 0, b]))
            moves.append(
                pltpu.make_async_copy(cot_v.at[from_at, pl.ds(0, D)], to_out.at[at], sem_block.at[i, 1, b])
            )
        return moves

    def scatter(b, carry):
        for i in range(2):
            at = pl.ds(pl.multiple_of(i * half + b * rows, rows), rows)
            choose = choose_v[at, :]
            which = i * (half // rows) + b
            cot_v[at, :D] = (mm(choose, y_v[which]) + cot_v[at, :D].astype(F32)).astype(BF)
            back = mm(choose, z_v[which])
            sec_v[at, :D] = (back[:, :D] + sec_v[at, :D].astype(F32)).astype(BF)
            sec_v[at, D:] = back[:, D:].astype(BF)
        for move in block_copies(b):
            move.start()
        return carry

    lax.fori_loop(0, half // rows, scatter, 0)
    for b in range(half // rows):
        for move in block_copies(b):
            move.wait()
    for one in outs:
        one.wait()


def expert_group(place, sec, cot, weights, kept, capacity, rows, experts, groups):
    gate, up, down, sin, sdn = weights
    local_experts, hidden, _ = gate.shape
    half = sec[0].shape[0]
    tokens = 2 * half
    blocks = tokens // rows
    per = blocks * capacity
    slots = per * groups
    wpad = sdn.shape[0]
    in_width = D + lanes(experts)
    big = (local_experts, slots)
    shapes = [
        jax.ShapeDtypeStruct((*big, D), BF),
        jax.ShapeDtypeStruct((*big, D), BF),
        jax.ShapeDtypeStruct((*big, hidden), BF),
        jax.ShapeDtypeStruct((*big, hidden), BF),
        jax.ShapeDtypeStruct((*big, hidden), BF),
        jax.ShapeDtypeStruct((half, D), BF),
        jax.ShapeDtypeStruct((half, D), BF),
        jax.ShapeDtypeStruct((half, in_width), BF),
        jax.ShapeDtypeStruct((half, in_width), BF),
        jax.ShapeDtypeStruct((2 * wpad, D), F32),
        jax.ShapeDtypeStruct((wpad, D), F32),
    ]
    first = kept is None
    operands = [place, *sec, *cot, gate, up, down, sin, sdn] + ([] if first else list(kept))
    any_space = pl.BlockSpec(memory_space=pl.ANY)
    smem = pl.BlockSpec(memory_space=pltpu.SMEM)
    return pl.pallas_call(
        functools.partial(expert_kernel, local_experts, capacity, rows, experts, first),
        out_shape=shapes,
        in_specs=[smem] + [any_space] * (len(operands) - 1),
        out_specs=[any_space] * len(shapes),
        scratch_shapes=[
            pltpu.VMEM((tokens, sec[0].shape[1]), BF),
            pltpu.VMEM((tokens, cot[0].shape[1]), BF),
            pltpu.VMEM(gate.shape, BF),
            pltpu.VMEM(up.shape, BF),
            pltpu.VMEM(down.shape, BF),
            pltpu.VMEM(sin.shape, BF),
            pltpu.VMEM(sdn.shape, BF),
            pltpu.VMEM((local_experts * per, D), BF),
            pltpu.VMEM((local_experts * per, D), BF),
            pltpu.VMEM((blocks, local_experts * capacity, D), BF),
            pltpu.VMEM((blocks, local_experts * capacity, in_width), BF),
            pltpu.VMEM((local_experts, per, hidden), BF),
            pltpu.VMEM((local_experts, per, hidden), BF),
            pltpu.VMEM((local_experts, per, hidden), BF),
            pltpu.VMEM((tokens, local_experts * capacity), BF),
            pltpu.VMEM((local_experts * per, 128), F32),
            pltpu.VMEM((tokens, wpad), BF),
            pltpu.VMEM((tokens, 2 * wpad), BF),
            pltpu.VMEM((2 * wpad, D), F32),
            pltpu.VMEM((wpad, D), F32),
            pltpu.SemaphoreType.DMA((9,)),
            pltpu.SemaphoreType.DMA((5 * local_experts + 2,)),
            pltpu.SemaphoreType.DMA((2, 2, half // rows)),
        ],
        input_output_aliases={} if first else {10 + i: i for i in range(5)},
        compiler_params=pltpu.CompilerParams(vmem_limit_bytes=63 * 1024 * 1024),
        cost_estimate=pl.CostEstimate(flops=1 << 20, bytes_accessed=1 << 16, transcendentals=0),
    )(*operands)


def turn(values, cosine, sine):
    lane = lax.broadcasted_iota(jnp.int32, values.shape, 1)
    partner = jnp.where(
        lane % DR < DR // 2, pltpu.roll(values, 2 * DR - DR // 2, 1), pltpu.roll(values, DR // 2, 1)
    )
    return values * cosine + partner * sine


def score_block(i, block, image, scores):
    row = lax.broadcasted_iota(jnp.int32, scores.shape, 0) + i * block
    column = lax.broadcasted_iota(jnp.int32, scores.shape, 1)
    allowed = (column <= row) | ((column >= i * block) & image)
    return jnp.where(allowed, scores * ((DN + DR) ** (-0.5)), NEGATIVE)


def head_part(values, h):
    lane = lax.broadcasted_iota(jnp.int32, values.shape, 1)
    return jnp.where(lane // DR == h, values.astype(F32), 0.0).astype(BF)


def attend_kernel(
    heads, rows, place, seq, gain, lgain, wq, wd, wup, cos, sin, out, first, q_out, lat_out, kr_out, ex_out, own_out, down_v
):
    block = PIECE
    nope = heads * DN
    for i in range(seq.shape[0] // block):
        at = slice(i * block, (i + 1) * block)
        values = seq[at, :D].astype(F32)
        low = (values * rms_parts(values) * gain[...]).astype(BF)
        first[at, :] = low
        q = mm(low, wq[...])
        down = mm(low, wd[...])
        down_v[at, :] = down
        latent = down[:, :KVR]
        lat = (latent * rms_parts(latent) * lgain[...]).astype(BF)
        lat_out[at, :] = lat
        ex_out[at, :] = mm(lat, wup[...]).astype(BF)
        turned = turn(down[:, KVR : KVR + 2 * DR], cos[at, :], sin[at, :])
        lane = lax.broadcasted_iota(jnp.int32, turned.shape, 1)
        turned = jnp.where(lane < DR, turned, 0.0)
        kr_out[at, :] = (turned + pltpu.roll(turned, DR, 1)).astype(BF)
        q_rope = turn(q[:, nope:], cos[at, :], sin[at, :]).astype(BF)
        q_out[at, :nope] = q[:, :nope].astype(BF)
        q_out[at, nope:] = q_rope
        image = seq[at, D : D + 128][:, :1].astype(F32) > 0
        n = (i + 1) * block
        for h in range(heads):
            mine = slice(h * (DN + DV), h * (DN + DV) + DN)
            scores = mm_nt(q_out[at, h * DN : (h + 1) * DN], ex_out[:n, mine])
            scores = scores + mm_nt(head_part(q_rope, h), kr_out[:n, :])
            scores = score_block(i, block, image, scores)
            weight = jnp.exp(scores - jnp.max(scores, axis=1, keepdims=True))
            weight = weight / jnp.sum(weight, axis=1, keepdims=True)
            value = ex_out[:n, h * (DN + DV) + DN : (h + 1) * (DN + DV)]
            out[at, h * DV : (h + 1) * DV] = mm(weight.astype(BF), value).astype(BF)
    own_out[...] = down_v[pl.ds(pl.multiple_of(place[0] * rows, rows), rows), :]


def attend(place, seq, gain, lgain, wq, wd, wup, cos, sin, heads, rows):
    length = seq.shape[0]
    shapes = [
        jax.ShapeDtypeStruct((length, heads * DV), BF),
        jax.ShapeDtypeStruct((length, D), BF),
        jax.ShapeDtypeStruct((length, wq.shape[1]), BF),
        jax.ShapeDtypeStruct((length, KVR), BF),
        jax.ShapeDtypeStruct((length, 2 * DR), BF),
        jax.ShapeDtypeStruct((length, wup.shape[1]), BF),
        jax.ShapeDtypeStruct((rows, wd.shape[1]), F32),
    ]
    vmem = pl.BlockSpec(memory_space=pltpu.VMEM)
    return pl.pallas_call(
        functools.partial(attend_kernel, heads, rows),
        out_shape=shapes,
        in_specs=[pl.BlockSpec(memory_space=pltpu.SMEM)] + [vmem] * 8,
        out_specs=[vmem] * len(shapes),
        scratch_shapes=[pltpu.VMEM((length, wd.shape[1]), F32)],
        compiler_params=pltpu.CompilerParams(vmem_limit_bytes=56 * 1024 * 1024),
        cost_estimate=pl.CostEstimate(flops=1 << 20, bytes_accessed=1 << 16, transcendentals=0),
    )(place, seq, gain, lgain, wq, wd, wup, cos, sin)


def attend_back_kernel(
    heads, place, grad, flags, first, q, kr, ex, lat, wq, wup, cos, sin,
    gain_out, first_keep, first_send, lat_keep, lat_send, pack_out,
    dk_v, dv_v, dr_v, qg_v, eg_v,
):
    block = PIECE
    nope = heads * DN
    length = first.shape[0]
    half = length // 2
    scale = (DN + DR) ** (-0.5)
    dk_v[...] = jnp.zeros_like(dk_v)
    dv_v[...] = jnp.zeros_like(dv_v)
    dr_v[...] = jnp.zeros_like(dr_v)
    for i in range(length // block):
        at = slice(i * block, (i + 1) * block)
        n = (i + 1) * block
        image = flags[at, :1].astype(F32) > 0
        rope_grad = jnp.zeros((block, 2 * DR), F32)
        for h in range(heads):
            mine = slice(h * (DN + DV), h * (DN + DV) + DN)
            value = ex[:n, h * (DN + DV) + DN : (h + 1) * (DN + DV)]
            q_nope = q[at, h * DN : (h + 1) * DN]
            q_rope = head_part(q[at, nope:], h)
            scores = mm_nt(q_nope, ex[:n, mine]) + mm_nt(q_rope, kr[:n, :])
            scores = score_block(i, block, image, scores)
            weight = jnp.exp(scores - jnp.max(scores, axis=1, keepdims=True))
            weight = weight / jnp.sum(weight, axis=1, keepdims=True)
            upstream = grad[at, h * DV : (h + 1) * DV]
            dprob = mm_nt(upstream, value)
            dv_v[:n, h * DV : (h + 1) * DV] += mm_tn(weight.astype(BF), upstream)
            inner = jnp.sum(weight * dprob, axis=1, keepdims=True)
            back = (weight * (dprob - inner)).astype(BF)
            qg_v[at, h * DN : (h + 1) * DN] = (mm(back, ex[:n, mine]) * scale).astype(BF)
            turned = mm(back, kr[:n, :])
            lane = lax.broadcasted_iota(jnp.int32, turned.shape, 1)
            rope_grad = jnp.where(lane // DR == h, turned * scale, rope_grad)
            dk_v[:n, h * DN : (h + 1) * DN] += mm_tn(back, q_nope)
            dr_v[:n, :] += mm_tn(back, q_rope)
        qg_v[at, nope:] = turn(rope_grad, cos[at, :], -sin[at, :]).astype(BF)
    for h in range(heads):
        mine = slice(h * (DN + DV), h * (DN + DV) + DN)
        eg_v[:, mine] = (dk_v[:, h * DN : (h + 1) * DN] * scale).astype(BF)
        eg_v[:, h * (DN + DV) + DN : (h + 1) * (DN + DV)] = dv_v[:, h * DV : (h + 1) * DV].astype(BF)
    key_rope = dr_v[...]
    key_rope = (key_rope + pltpu.roll(key_rope, DR, 1)) * scale
    dr_v[...] = key_rope
    keep = pl.ds(pl.multiple_of(place[1] * half, half), half)
    send = pl.ds(pl.multiple_of((1 - place[1]) * half, half), half)
    total = jnp.zeros((1, D), F32)
    for at, to_lat, to_first in ((send, lat_send, first_send), (keep, lat_keep, first_keep)):
        to_lat[:, :KVR] = mm_nt(eg_v[at, :], wup[...]).astype(BF)
        to_lat[:, KVR:] = dr_v[at, :].astype(BF)
        part = mm_nt(qg_v[at, :], wq[...])
        to_first[...] = part.astype(BF)
        total = total + jnp.sum(part * first[at, :].astype(F32), axis=0, keepdims=True)
    gain_out[...] = total
    owners, pack_rows, _ = pack_out.shape
    wide = wq.shape[1]
    q_rows = D // owners
    pack_out[:, :q_rows, :wide] = mm_tn(first[...], qg_v[...]).astype(BF).reshape(owners, q_rows, wide)
    pack_out[:, :q_rows, wide:] = jnp.zeros((owners, q_rows, pack_out.shape[2] - wide), BF)
    pack_out[:, q_rows:, :] = mm_tn(lat[...], eg_v[...]).astype(BF).reshape(owners, pack_rows - q_rows, -1)


def attend_back(place, grad, flags, first, q, kr, ex, lat, wq, wup, cos, sin, heads, owners):
    length = first.shape[0]
    half = length // 2
    wide = KVR + 2 * DR
    shapes = [
        jax.ShapeDtypeStruct((1, D), F32),
        jax.ShapeDtypeStruct((half, D), BF),
        jax.ShapeDtypeStruct((half, D), BF),
        jax.ShapeDtypeStruct((half, wide), BF),
        jax.ShapeDtypeStruct((half, wide), BF),
        jax.ShapeDtypeStruct((owners, (D + KVR) // owners, wup.shape[1]), BF),
    ]
    vmem = pl.BlockSpec(memory_space=pltpu.VMEM)
    return pl.pallas_call(
        functools.partial(attend_back_kernel, heads),
        out_shape=shapes,
        in_specs=[pl.BlockSpec(memory_space=pltpu.SMEM)] + [vmem] * 11,
        out_specs=[vmem] * len(shapes),
        scratch_shapes=[
            pltpu.VMEM((length, heads * DN), F32),
            pltpu.VMEM((length, heads * DV), F32),
            pltpu.VMEM((length, 2 * DR), F32),
            pltpu.VMEM((length, q.shape[1]), BF),
            pltpu.VMEM((length, ex.shape[1]), BF),
        ],
        compiler_params=pltpu.CompilerParams(vmem_limit_bytes=56 * 1024 * 1024),
        cost_estimate=pl.CostEstimate(flops=1 << 20, bytes_accessed=1 << 16, transcendentals=0),
    )(place, grad, flags, first, q, kr, ex, lat, wq, wup, cos, sin)


def on_device(
    tokens,
    attention_norm,
    query_weight,
    latent_down,
    latent_norm,
    latent_up,
    output_weight,
    post_norm,
    shared_gate,
    shared_up,
    shared_down,
    router_weight,
    expert_gate,
    expert_up,
    expert_down,
    image_piece_index,
    routes,
    cotangent,
):
    rows = tokens.shape[0]
    c_size, k_size, z_size = (lax.axis_size(a) for a in EVERY)
    c, k, z = (lax.axis_index(a) for a in EVERY)
    column_size = k_size * z_size
    device_count = c_size * column_size
    local_experts = expert_gate.shape[0]
    experts = router_weight.shape[1]
    capacity = rows * TOPK * 4 // (3 * experts)
    length = column_size * rows
    heads = H // column_size
    width = shared_down.shape[0]
    score_scale = (DN + DR) ** (-0.5)
    weight_rows = query_weight.shape[0]
    up_rows = latent_up.shape[0]

    paired = H == 4 * c_size and heads == 2 and column_size == 8

    def by_owner(array, n):
        if paired:
            array = array.reshape(-1, 2, 2, 4, n).transpose(0, 3, 1, 2, 4)
        return array.reshape(-1, column_size, heads * n)

    def by_head(array, n):
        if paired:
            array = array.reshape(-1, 4, 2, 2, n).transpose(0, 2, 3, 1, 4)
        return array.reshape(-1, H * n)

    flag = (image_piece_index > 0).astype(BF)[:, None]
    expert_ids = jnp.arange(experts, dtype=jnp.int32)
    named = jnp.any(routes[:, :, None] == expert_ids[None, None, :], axis=1)

    out_mine = in_order(gather_z(output_weight.astype(BF)), z)
    extra = -(-weight_rows // 8) * 8 + 8 - weight_rows
    down_width = KVR + DR
    small_width = lanes(max(down_width + experts + 8, weight_rows))
    gains = jnp.stack(
        [attention_norm, post_norm, jnp.pad(latent_norm, (0, weight_rows - latent_norm.shape[0]))]
    )
    small = jnp.concatenate([latent_down, router_weight], axis=1).astype(BF)
    small = jnp.pad(small, ((0, 0), (0, small_width - small.shape[1])))
    gains = jnp.pad(gains.astype(BF), ((0, extra - 3), (0, small_width - weight_rows)))
    small = jnp.concatenate([small, gains], axis=0)
    q_width = heads * (DN + DR)
    kv_width = heads * (DN + DV)
    q_out = by_owner(query_weight.astype(BF), DN + DR).transpose(1, 0, 2)
    q_out = q_out.reshape(column_size, weight_rows, heads, DN + DR)
    q_out = jnp.concatenate(
        [q_out[..., :DN].reshape(column_size, weight_rows, -1), q_out[..., DN:].reshape(column_size, weight_rows, -1)],
        axis=2,
    )
    q_out = jnp.pad(q_out, ((0, 0), (0, 0), (0, kv_width - q_width)))
    up_out = by_owner(latent_up.astype(BF), DN + DV).transpose(1, 0, 2)
    head_pack = jnp.concatenate([q_out, up_out], axis=1)
    head_pack = lax.all_to_all(head_pack, COLUMN, split_axis=0, concat_axis=0, tiled=True)
    token_units = gather_z(after(widen(tokens, flag), head_pack))
    cot_units = gather_z(after(widen(cotangent, named), *token_units[1:]))
    head_pack = [head_pack] + [swap(head_pack, "c", d) for d in range(1, c_size)]
    small, small_recv = gather_weight(small)
    mine = in_order(after_all(token_units, *head_pack[1:], *small_recv), z)
    sequence = in_order([mine, swap(mine, "k", 1)], k).reshape(length, -1)
    small = small.reshape(device_count, weight_rows + extra, small_width)
    full_small = small[:, :weight_rows].reshape(D, small_width)
    full_router = full_small[:, down_width : down_width + experts]
    full_gains = small[:, weight_rows : weight_rows + 3, :weight_rows].astype(F32)
    attn_gain = full_gains[:, 0].reshape(D)
    post_gain = full_gains[:, 1].reshape(D)
    latent_gain = full_gains[:, 2, : latent_norm.shape[0]].reshape(KVR)
    out_mine = after(out_mine, *head_pack[1:])
    out_planes = [out_mine] + [swap(out_mine, "c", d) for d in range(1, c_size)]
    head_pack = in_order(head_pack, c)
    head_query = head_pack[:, :, :weight_rows, :q_width].reshape(D, q_width)
    head_up = head_pack[:, :, weight_rows:].reshape(KVR, kv_width)
    shared_pack = jnp.concatenate(
        [
            shared_gate.astype(BF).reshape(weight_rows, device_count, width),
            shared_up.astype(BF).reshape(weight_rows, device_count, width),
        ],
        axis=2,
    ).transpose(1, 0, 2)
    shared_in = lax.all_to_all(after(shared_pack, *token_units[1:]), EVERY, split_axis=0, concat_axis=0, tiled=True)
    shared_low = shared_down.astype(BF)

    places = jnp.arange(length, dtype=F32)
    frequency = ROPE_BASE ** (-2.0 * jnp.arange(DR // 2, dtype=F32) / DR)
    angles = places[:, None] * frequency[None, :]
    cosine, sine = jnp.cos(angles), jnp.sin(angles)
    cosine_wide = jnp.tile(cosine, (1, 4))
    sine_wide = jnp.tile(jnp.concatenate([-sine, sine], axis=1), (1, 2))
    here = k * z_size + z

    def own_rows(array):
        return lax.dynamic_slice_in_dim(array, here * rows, rows, axis=0)

    spot = jnp.stack([here, k]).astype(jnp.int32)
    heads_out, first_low, query_low, latent_low, rope_low, expanded, down_raw = attend(
        spot, sequence, attn_gain[None], latent_gain[None], head_query, full_small, head_up,
        cosine_wide, sine_wide, heads, rows,
    )
    own_values = tokens.astype(F32)
    own_scale = rms_parts(own_values)
    own_first_low = (own_values * own_scale * attn_gain).astype(BF)
    latent_raw = down_raw[:, :KVR]
    latent_scale = rms_parts(latent_raw)

    def heads_to_tokens(array):
        n = array.shape[1]
        moved = lax.all_to_all(
            array.reshape(column_size, rows, n), COLUMN, split_axis=0, concat_axis=0, tiled=True
        )
        return by_head(moved.transpose(1, 0, 2), n // heads)

    def tokens_to_heads(array):
        n = array.shape[1] // H
        moved = lax.all_to_all(
            by_owner(array, n).transpose(1, 0, 2), COLUMN, split_axis=0, concat_axis=0, tiled=True
        )
        return moved.reshape(length, heads * n)

    shared_in, *cot_units = after_all([shared_in, *cot_units], heads_out)
    cot_own = jnp.concatenate(cot_units, axis=0)
    shared_in = shared_in.reshape(D, 2 * width)
    room = ((0, 0), (0, lanes(width) - width))
    shared_in = jnp.concatenate(
        [jnp.pad(shared_in[:, :width], room), jnp.pad(shared_in[:, width:], room)], axis=1
    )
    out_planes = in_order(after_all(out_planes, heads_out, cot_own), c)
    full_out = in_order([out_planes, swap(out_planes, "k", 1)], k)
    full_out = full_out.transpose(1, 0, 2, 3, 4).reshape(D, D)

    def plane_groups(own):
        near = [swap(own, "c", d) for d in range(1, c_size - 1)]
        return [own, *near, swap(after(own, *near), "c", c_size - 1)]

    cot_groups = [cot_own] + [swap(cot_own, "c", d) for d in range(1, c_size)]
    heads_low = after(heads_to_tokens(after(heads_out, cot_own, shared_in)), full_out)
    residual = tokens.astype(F32) + mm(heads_low, full_out)
    second_scale = rms_parts(residual)
    second_low = (residual * second_scale * post_gain).astype(BF)
    router_probs = jax.nn.softmax(mm(second_low, full_router), axis=-1)

    probs_high = router_probs.astype(BF)
    probs_rest = (router_probs - probs_high.astype(F32)).astype(BF)
    second_own = jnp.concatenate(
        gather_z(widen(second_low, jnp.concatenate([probs_high, probs_rest], axis=1))), axis=0
    )
    second_own = after(second_own, *cot_groups[1:])
    second_groups = plane_groups(second_own)
    pair = lambda group: (group, swap(group, "k", 1))
    cot_groups = [pair(g) for g in cot_groups]
    wpad = lanes(width)
    place = jnp.stack([(c * k_size + k) * local_experts, jnp.zeros((), jnp.int32)]).astype(jnp.int32)
    shared_rows = jnp.pad(shared_low, ((0, wpad - width), (0, 0)))
    weights = (
        jnp.swapaxes(expert_gate, 1, 2),
        jnp.swapaxes(expert_up, 1, 2),
        expert_down,
        shared_in,
        shared_rows,
    )
    kept, sg_parts, sd_parts, sums, out_sums, marks = None, [], [], [], [], []
    arrived = []
    for d in range(c_size):
        where = place.at[1].set(d)
        group = second_groups[d]
        if d == 1:
            group, *second_groups[2:-1] = after_all([group, *second_groups[2:-1]], marks[0])
        if d == c_size - 2:
            second_groups[-1] = after(second_groups[-1], marks[d - 1])
            where = after(where, second_groups[-1])
        if d > 1:
            where = after(where, out_sums[d - 2], sums[d - 1])
        results = list(
            expert_group(
                where, pair(group), cot_groups[d], weights, kept, capacity, rows, experts, c_size
            )
        )
        kept = results[:5]
        marks.append(results[10])
        if d == c_size - 1:
            results[8] = after(results[8], *arrived)
        sums.append(core_sum(*results[7:9], d))
        if d:
            arrived.append(swap(sums[d], "c", d))
        if d == c_size - 1:
            kept = after_all(kept, *arrived[:-1])
            results[6] = after(results[6], arrived[-1])
        out_sums.append(core_sum(*results[5:7], d))
        sg_parts.append(results[9])
        sd_parts.append(results[10])
    plane = functools.reduce(lambda total, block: total + block.astype(F32), arrived, sums[0])
    expert_in, cot_in, act_weighted, gate_grad, up_grad = kept
    ein = lambda spec, a, b: jnp.einsum(spec, a, b, preferred_element_type=F32)
    expert_down_grad = ein("esf,esd->efd", act_weighted, cot_in)
    expert_gate_grad = jnp.swapaxes(ein("esf,esd->efd", gate_grad, expert_in), 1, 2)
    expert_up_grad = jnp.swapaxes(ein("esf,esd->efd", up_grad, expert_in), 1, 2)
    plane = after(plane, expert_down_grad, expert_gate_grad, expert_up_grad)
    second_sum = scatter_z(z_units(plane, rows))
    out_near = [swap(after(out_sums[d], *arrived), "c", d) for d in range(1, c_size - 1)]
    second_sum = after(second_sum, *out_near, out_sums[-1])
    out_far = swap(after(out_sums[-1], *out_near), "c", c_size - 1)
    probs_grad = second_sum[:, D : D + experts]
    logits_grad = (
        router_probs * (probs_grad - jnp.sum(router_probs * probs_grad, axis=-1, keepdims=True))
    ).astype(BF)
    second_grad = second_sum[:, :D] + mm_nt(logits_grad, full_router)
    norm_part, post_terms = rms_back(residual, second_scale, post_gain, second_grad)
    residual_grad = cotangent.astype(F32) + norm_part
    attn_grad_low = residual_grad.astype(BF)
    heads_grad = tokens_to_heads(mm_nt(attn_grad_low, full_out).astype(BF))
    output_pieces = core_pieces(mm_tn(heads_low, attn_grad_low).astype(BF))

    gain_part, first_keep, first_send, latent_keep, latent_send, head_grad = attend_back(
        after(spot, *output_pieces), heads_grad, sequence[:, D:], first_low, query_low,
        rope_low, expanded, latent_low, head_query, head_up, cosine_wide, sine_wide, heads, device_count,
    )
    def column_sum(keep, send):
        summed = keep.astype(F32) + swap(send, "k", 1).astype(F32)
        summed = summed.reshape(z_size, rows, keep.shape[1])
        return scatter_z([pick(summed, z ^ d) for d in range(z_size)])

    latent_sum = column_sum(latent_keep, after(latent_send, out_far))
    shared_in_grad = sum(sg_parts[1:], sg_parts[0])
    shared_in_grad = jnp.concatenate(
        [shared_in_grad[:width], shared_in_grad[wpad : wpad + width]], axis=0
    ).astype(BF)
    shared_down_grad = sum(sd_parts[1:], sd_parts[0])[:width]
    shared_back = shared_in_grad.reshape(2 * width, c_size, column_size, weight_rows).transpose(2, 1, 3, 0)
    shared_back = lax.all_to_all(
        after(shared_back, latent_keep), COLUMN, split_axis=0, concat_axis=0, tiled=True
    )
    latent_raw_grad, latent_terms = rms_back(
        latent_raw, latent_scale, latent_gain, latent_sum[:, :KVR]
    )
    rope_raw_grad = rotate(
        latent_sum[:, KVR:down_width], own_rows(cosine), own_rows(sine), -1.0
    )
    down_grad_low = jnp.concatenate([latent_raw_grad, rope_raw_grad], axis=-1).astype(BF)
    first_own = mm_nt(down_grad_low, full_small[:, :down_width])
    attn_gain_grad = gain_part[0] / attn_gain + jnp.sum(
        first_own * (own_values * own_scale), axis=0
    )
    gain_grads = jnp.stack(
        [
            attn_gain_grad,
            jnp.sum(post_terms, axis=0),
            jnp.pad(
                jnp.sum(latent_terms, axis=0).reshape(device_count, latent_norm.shape[0]),
                ((0, 0), (0, weight_rows - latent_norm.shape[0])),
            ).reshape(D),
        ]
    )
    first_gain = down_width + experts
    small_right = jnp.zeros((2 * rows + 8, small_width), BF)
    small_right = small_right.at[:rows, :down_width].set(down_grad_low)
    small_right = small_right.at[rows : 2 * rows, down_width:first_gain].set(logits_grad)
    ones = (jnp.arange(8)[:, None] == jnp.arange(small_width)[None, :] - first_gain).astype(BF)
    small_right = small_right.at[2 * rows :].set(ones)
    small_left = jnp.concatenate(
        [own_first_low, second_low, jnp.pad(gain_grads, ((0, 5), (0, 0))).astype(BF)], axis=0
    )
    output_near = [swap(output_pieces[d], "c", d) for d in range(1, c_size - 1)]
    small_pieces = core_pieces(mm_tn(small_left, small_right).astype(BF))
    first_sum = column_sum(first_keep, first_send)
    first_sum, *small_pieces = after_all([first_sum, *small_pieces], *output_near)
    out_plane = functools.reduce(
        lambda total, block: total + block.astype(F32),
        after_all([*out_near, out_far], first_sum),
        out_sums[0],
    )
    out_units = z_units(out_plane, rows)
    out_units = out_units[:1] + [swap(unit.astype(BF), "z", d) for d, unit in enumerate(out_units) if d]
    output_moved = [
        *output_near, swap(after(output_pieces[-1], *output_near), "c", c_size - 1)
    ]
    head_grad = head_grad.reshape(c_size, column_size, weight_rows + up_rows, kv_width)
    head_moved = [swap(pick(head_grad, c ^ d), "c", d) for d in range(1, c_size)]
    small_plane, _ = plane_sum(small_pieces, *head_moved)
    output_plane = functools.reduce(
        lambda total, block: total + block.astype(F32),
        after_all(output_moved, small_plane),
        output_pieces[0],
    )
    shared_back = after(shared_back, small_plane)
    shared_moved = [
        swap(lax.dynamic_index_in_dim(shared_back, c ^ d, axis=1, keepdims=False), "c", d)
        for d in range(1, c_size)
    ]
    first_grad = first_sum + first_own
    out_sum = functools.reduce(
        lambda total, block: total + block.astype(F32), after_all(out_units[1:], first_grad), out_units[0]
    )
    layer_out = (residual + out_sum).astype(BF)
    first_norm_grad, _ = rms_back(own_values, own_scale, attn_gain, first_grad)
    tokens_grad = residual_grad + first_norm_grad
    own_both = z_sum(jnp.concatenate([output_plane, small_plane], axis=1))
    own_output, own_small = own_both[:, :D], own_both[:, D:]
    shared_back = in_order(
        [
            lax.dynamic_index_in_dim(shared_back, c, axis=1, keepdims=False),
            *after_all(shared_moved, own_both),
        ],
        c,
    ).reshape(device_count, weight_rows, 2 * width).transpose(1, 0, 2)
    head_sum = pick(head_grad, c).astype(F32)
    for block in after_all(head_moved, small_plane):
        head_sum = head_sum + block.astype(F32)
    head_sum = lax.all_to_all(head_sum.astype(BF), COLUMN, split_axis=0, concat_axis=0, tiled=True)
    own_query = head_sum[:, :weight_rows, :q_width].transpose(1, 0, 2)
    own_query = jnp.concatenate(
        [
            own_query[..., : heads * DN].reshape(weight_rows, column_size, heads, DN),
            own_query[..., heads * DN :].reshape(weight_rows, column_size, heads, DR),
        ],
        axis=3,
    )
    own_query = by_head(own_query.reshape(weight_rows, column_size, q_width), DN + DR)
    own_up = by_head(head_sum[:, weight_rows:].transpose(1, 0, 2), DN + DV)
    own_gate = shared_back[:, :, :width].reshape(weight_rows, -1)
    own_shared_up = shared_back[:, :, width:].reshape(weight_rows, -1)
    return (
        layer_out,
        tokens_grad,
        own_small[:, first_gain],
        own_query.astype(F32),
        own_small[:, :down_width],
        own_small[: latent_norm.shape[0], first_gain + 2],
        own_up.astype(F32),
        own_output,
        own_small[:, first_gain + 1],
        own_gate.astype(F32),
        own_shared_up.astype(F32),
        shared_down_grad,
        own_small[:, down_width:first_gain],
        expert_gate_grad,
        expert_up_grad,
        expert_down_grad,
    )


def solution(mesh):
    expert_size, z_size = mesh.devices.shape
    fine = Mesh(mesh.devices.reshape(expert_size // 2, 2, z_size), EVERY)
    row, flat = P(EVERY, None), P(EVERY)
    wide, tall = P(("c", "k"), None, "z"), P(("c", "k"), "z", None)
    return jax.shard_map(
        on_device,
        mesh=fine,
        in_specs=(row, flat, row, row, flat, row, row, flat, row, row, row, row)
        + (wide, wide, tall, flat, row, row),
        out_specs=(row, row, flat, row, row, flat, row, row, flat, row, row, row, row)
        + (wide, wide, tall),
        check_vma=False,
    )
```

```python
import functools

import jax
import jax.numpy as jnp
from jax import lax
from jax.experimental import pallas as pl
from jax.experimental.pallas import tpu as pltpu
from jax.sharding import Mesh, PartitionSpec as P

D = 2048
H = 16
DN = 128
DR = 64
DV = 128
KVR = 512
TOPK = 6
PIECE = 256
EPSILON = 1e-06
ROPE_BASE = 10000.0
NEGATIVE = -1e30
BF = jnp.bfloat16
F32 = jnp.float32
EVERY = ("c", "k", "z")
COLUMN = ("k", "z")


def swap(block, axis, distance):
    n = lax.axis_size(axis)
    return lax.ppermute(block, axis, [(i, i ^ distance) for i in range(n)])


def lanes(n):
    return -(-n // 128) * 128


def widen(block, extra):
    room = lanes(extra.shape[1]) - extra.shape[1]
    return jnp.concatenate([block, jnp.pad(extra.astype(BF), ((0, 0), (0, room)))], axis=1)


def dot(a, b, dims):
    return lax.dot_general(a, b, (dims, ((), ())), preferred_element_type=F32)


def mm(a, b):
    return dot(a, b, ((1,), (0,)))


def mm_nt(a, b):
    return dot(a, b, ((1,), (1,)))


def mm_tn(a, b):
    return dot(a, b, ((0,), (0,)))


def after(array, *others):
    return lax.optimization_barrier((array, *others))[0]


def after_all(arrays, *others):
    return lax.optimization_barrier((tuple(arrays), *others))[0]


def put(buffer, block, index):
    return lax.dynamic_update_slice_in_dim(buffer, block[None], index, axis=0)


def gather_z(unit):
    return [unit] + [swap(unit, "z", d) for d in range(1, lax.axis_size("z"))]


def in_order(blocks, index):
    whole = jnp.zeros((len(blocks), *blocks[0].shape), blocks[0].dtype)
    for d, block in enumerate(blocks):
        whole = put(whole, block, index ^ d)
    return whole


def gather_weight(unit):
    c_size, k_size, _ = (lax.axis_size(a) for a in EVERY)
    c, k, z = (lax.axis_index(a) for a in EVERY)
    mine = in_order(gather_z(unit), z)
    planes = [mine] + [swap(mine, "c", d) for d in range(1, c_size)]
    own = in_order(planes, c)
    other = swap(own, "k", 1)
    halves = in_order([own, other], k)
    return halves.transpose(1, 0, 2, 3, 4), planes[1:]


def scatter_z(blocks):
    total = blocks[0]
    for d in range(1, len(blocks)):
        total = total + swap(blocks[d].astype(BF), "z", d).astype(F32)
    return total


def scatter_column(part, rows):
    z_size = lax.axis_size("z")
    k, z = lax.axis_index("k"), lax.axis_index("z")
    grid = part.reshape(2, z_size, rows, part.shape[1])
    summed = pick(grid, k) + swap(pick(grid, k ^ 1).astype(BF), "k", 1).astype(F32)
    return scatter_z([pick(summed, z ^ d) for d in range(z_size)])


def core_sum(own, other, distance):
    summed = own.astype(F32) + swap(other, "k", 1).astype(F32)
    return summed.astype(BF) if distance else summed


def plane_sum(sums, *others):
    moved = [swap(block, "c", d) for d, block in enumerate(sums) if d]
    if others:
        moved = after_all(moved, *others)
    total = sums[0]
    for block in moved:
        total = total + block.astype(F32)
    return total, moved


def z_units(total, rows):
    return [total[d * rows : (d + 1) * rows] for d in range(lax.axis_size("z"))]


def pick(array, index):
    return lax.dynamic_index_in_dim(array, index, axis=0, keepdims=False)


def core_pieces(part):
    c_size, k_size, z_size = (lax.axis_size(a) for a in EVERY)
    c, k = lax.axis_index("c"), lax.axis_index("k")
    grid = part.reshape(c_size, k_size, part.shape[0] // (c_size * k_size), part.shape[1])
    got = swap(lax.dynamic_index_in_dim(grid, k ^ 1, axis=1, keepdims=False), "k", 1)
    kept = lax.dynamic_index_in_dim(grid, k, axis=1, keepdims=False)
    pieces = []
    for d in range(c_size):
        piece = pick(kept, c ^ d).astype(F32) + pick(got, c ^ d).astype(F32)
        pieces.append(piece.astype(BF) if d else piece)
    return pieces


def pieces_sum(pieces, *others):
    total, _ = plane_sum(pieces, *others)
    return z_sum(total)


def z_sum(total):
    z_size, z = lax.axis_size("z"), lax.axis_index("z")
    total = total.reshape(z_size, total.shape[0] // z_size, total.shape[1])
    return scatter_z([pick(total, z ^ d) for d in range(z_size)])


def scatter_weight(part):
    return pieces_sum(core_pieces(part))


def rms_parts(values):
    return lax.rsqrt(jnp.mean(values * values, axis=-1, keepdims=True) + EPSILON)


def rms_back(values, scale, gain, grad):
    weighted = grad * gain
    inner = jnp.mean(weighted * values, axis=-1, keepdims=True)
    return scale * (weighted - values * (scale * scale * inner)), grad * values * scale


def rotate(values, cosine, sine, sign):
    half = values.shape[-1] // 2
    a, b = values[..., :half], values[..., half:]
    return jnp.concatenate([a * cosine - sign * b * sine, b * cosine + sign * a * sine], axis=-1)


def expert_kernel(
    local_experts,
    capacity,
    rows,
    experts,
    first,
    place_ref,
    sec_a,
    sec_b,
    cot_a,
    cot_b,
    gate_hbm,
    up_hbm,
    down_hbm,
    sin_hbm,
    sdn_hbm,
    *rest,
):
    rest = rest if first else rest[5:]
    (x_out, c_out, aw_out, gg_out, ug_out, out_a, out_b, in_a, in_b, sg_out, sd_out) = rest[:11]
    (sec_v, cot_v, gate_v, up_v, down_v, sin_v, sdn_v, x_v, c_v, y_v, z_v, aw_v, gg_v, ug_v) = rest[11:25]
    (choose_v, prob_v, sact_v, slow_v, sgp_v, sdp_v, sem_in, sem_out, sem_block) = rest[25:34]
    half = sec_a.shape[0]
    blocks = 2 * half // rows
    per = blocks * capacity
    wpad = sdn_v.shape[0]
    base = place_ref[1] * per

    def copy(src, dst, sem, i):
        made = pltpu.make_async_copy(src, dst, sem.at[i])
        made.start()
        return made

    near = [
        copy(sec_a, sec_v.at[pl.ds(0, half)], sem_in, 0),
        copy(cot_a, cot_v.at[pl.ds(0, half)], sem_in, 2),
    ]
    first_expert = place_ref[0]
    tail = cot_v.shape[1] - D
    row_i = lax.broadcasted_iota(jnp.int32, (rows, rows), 0)
    col_i = lax.broadcasted_iota(jnp.int32, (rows, rows), 1)
    earlier = (col_i < row_i).astype(BF)
    lane = lax.broadcasted_iota(jnp.int32, (rows, tail), 1)
    slot = lax.broadcasted_iota(jnp.int32, (rows, local_experts * capacity), 1).astype(F32)
    sec_tail = sec_v.shape[1] - D
    tail_lane = lax.broadcasted_iota(jnp.int32, (capacity, sec_tail), 1)

    def gather(b, carry):
        at = pl.ds(pl.multiple_of(b * rows, rows), rows)
        named = cot_v[at, D:]
        rank = mm(earlier, named)
        code = jnp.where((named.astype(F32) > 0) & (rank < capacity), rank, -1e6)
        chosen = jnp.zeros(slot.shape, F32)
        for e in range(local_experts):
            own = jnp.sum(jnp.where(lane == first_expert + e, code, 0.0), axis=1, keepdims=True)
            chosen = jnp.where(own + e * capacity == slot, 1.0, chosen)
        choose = chosen.astype(BF)
        choose_v[at, :] = choose
        picked = mm_tn(choose, sec_v[at, :])
        cots = mm_tn(choose, cot_v[at, :D])
        for e in range(local_experts):
            mine = slice(e * capacity, (e + 1) * capacity)
            to = pl.ds(pl.multiple_of(e * per + b * capacity, capacity), capacity)
            x_v[to, :] = picked[mine, :D].astype(BF)
            c_v[to, :] = cots[mine].astype(BF)
            which = first_expert + e
            hits = (tail_lane == which) | (tail_lane == which + experts)
            prob = jnp.sum(jnp.where(hits, picked[mine, D:], 0.0), axis=1, keepdims=True)
            prob_v[to, :] = jnp.broadcast_to(prob, (capacity, 128))
        return carry

    for one in near:
        one.wait()
    far = [
        copy(sec_b, sec_v.at[pl.ds(half, half)], sem_in, 1),
        copy(cot_b, cot_v.at[pl.ds(half, half)], sem_in, 3),
    ]
    in_sin = copy(sin_hbm, sin_v, sem_in, 7)
    in_sdn = copy(sdn_hbm, sdn_v, sem_in, 8)
    lax.fori_loop(0, blocks // 2, gather, 0, unroll=True)
    for one in far:
        one.wait()
    in_gate = copy(gate_hbm, gate_v, sem_in, 4)
    in_up = copy(up_hbm, up_v, sem_in, 5)
    in_down = copy(down_hbm, down_v, sem_in, 6)
    lax.fori_loop(blocks // 2, blocks, gather, 0, unroll=True)
    outs = []
    for e in range(local_experts):
        mine = pl.ds(e * per, per)
        outs.append(copy(x_v.at[mine], x_out.at[e, pl.ds(base, per)], sem_out, 2 * e))
        outs.append(copy(c_v.at[mine], c_out.at[e, pl.ds(base, per)], sem_out, 2 * e + 1))
    used = 2 * local_experts

    in_sin.wait()
    in_sdn.wait()
    shared = mm(sec_v[:, :D], sin_v[...])
    s_gate, s_up = shared[:, :wpad], shared[:, wpad:]
    s_sigma = jax.nn.sigmoid(s_gate)
    s_silu = s_gate * s_sigma
    s_grad = mm_nt(cot_v[:, :D], sdn_v[...])
    sact_v[...] = (s_silu * s_up).astype(BF)
    slow_v[:, :wpad] = (s_grad * s_up * (s_sigma * (1.0 + s_gate * (1.0 - s_sigma)))).astype(BF)
    slow_v[:, wpad:] = (s_grad * s_silu).astype(BF)
    sgp_v[...] = mm_tn(slow_v[...], sec_v[:, :D])
    sdp_v[...] = mm_tn(sact_v[...], cot_v[:, :D])
    cot_v[:, :D] = mm(sact_v[...], sdn_v[...]).astype(BF)
    sec_v[:, :D] = mm_nt(slow_v[...], sin_v[...]).astype(BF)
    outs.append(copy(sgp_v, sg_out, sem_out, used))
    outs.append(copy(sdp_v, sd_out, sem_out, used + 1))
    used += 2

    in_gate.wait()
    in_up.wait()
    in_down.wait()
    in_tail = z_v.shape[2] - D
    pair_lane = lax.broadcasted_iota(jnp.int32, (per, in_tail), 1)
    for e in range(local_experts):
        mine = pl.ds(e * per, per)
        x_e, c_e = x_v[mine, :], c_v[mine, :]
        gate = mm_nt(x_e, gate_v[e])
        up = mm_nt(x_e, up_v[e])
        pull = mm_nt(c_e, down_v[e])
        prob = prob_v[mine, :1]
        sigma = jax.nn.sigmoid(gate)
        silu = gate * sigma
        act = silu * up
        pair = jnp.sum(pull * act, axis=1, keepdims=True)
        pull = pull * prob
        gg_v[e] = (pull * up * (sigma * (1.0 + gate * (1.0 - sigma)))).astype(BF)
        ug_v[e] = (pull * silu).astype(BF)
        aw_v[e] = (act * prob).astype(BF)
        outs.append(copy(aw_v.at[e], aw_out.at[e, pl.ds(base, per)], sem_out, used))
        outs.append(copy(gg_v.at[e], gg_out.at[e, pl.ds(base, per)], sem_out, used + 1))
        outs.append(copy(ug_v.at[e], ug_out.at[e, pl.ds(base, per)], sem_out, used + 2))
        used += 3
        y = mm(aw_v[e], down_v[e]).astype(BF)
        y_v[:, e * capacity : (e + 1) * capacity, :] = y.reshape(blocks, capacity, D)
        zed = (mm(gg_v[e], gate_v[e]) + mm(ug_v[e], up_v[e])).astype(BF)
        z_v[:, e * capacity : (e + 1) * capacity, :D] = zed.reshape(blocks, capacity, D)
        pairs = jnp.where(pair_lane == first_expert + e, pair, 0.0).astype(BF)
        z_v[:, e * capacity : (e + 1) * capacity, D:] = pairs.reshape(blocks, capacity, in_tail)

    def block_copies(b):
        moves = []
        for i, (to_in, to_out) in enumerate(((in_a, out_a), (in_b, out_b))):
            at = pl.ds(pl.multiple_of(b * rows, rows), rows)
            from_at = pl.ds(pl.multiple_of(i * half + b * rows, rows), rows)
            moves.append(pltpu.make_async_copy(sec_v.at[from_at], to_in.at[at], sem_block.at[i, 0, b]))
            moves.append(
                pltpu.make_async_copy(cot_v.at[from_at, pl.ds(0, D)], to_out.at[at], sem_block.at[i, 1, b])
            )
        return moves

    def scatter(b, carry):
        for i in range(2):
            at = pl.ds(pl.multiple_of(i * half + b * rows, rows), rows)
            choose = choose_v[at, :]
            which = i * (half // rows) + b
            cot_v[at, :D] = (mm(choose, y_v[which]) + cot_v[at, :D].astype(F32)).astype(BF)
            back = mm(choose, z_v[which])
            sec_v[at, :D] = (back[:, :D] + sec_v[at, :D].astype(F32)).astype(BF)
            sec_v[at, D:] = back[:, D:].astype(BF)
        for move in block_copies(b):
            move.start()
        return carry

    lax.fori_loop(0, half // rows, scatter, 0, unroll=True)
    for b in range(half // rows):
        for move in block_copies(b):
            move.wait()
    for one in outs:
        one.wait()


def expert_group(place, sec, cot, weights, kept, capacity, rows, experts, groups):
    gate, up, down, sin, sdn = weights
    local_experts, hidden, _ = gate.shape
    half = sec[0].shape[0]
    tokens = 2 * half
    blocks = tokens // rows
    per = blocks * capacity
    slots = per * groups
    wpad = sdn.shape[0]
    in_width = D + lanes(experts)
    big = (local_experts, slots)
    shapes = [
        jax.ShapeDtypeStruct((*big, D), BF),
        jax.ShapeDtypeStruct((*big, D), BF),
        jax.ShapeDtypeStruct((*big, hidden), BF),
        jax.ShapeDtypeStruct((*big, hidden), BF),
        jax.ShapeDtypeStruct((*big, hidden), BF),
        jax.ShapeDtypeStruct((half, D), BF),
        jax.ShapeDtypeStruct((half, D), BF),
        jax.ShapeDtypeStruct((half, in_width), BF),
        jax.ShapeDtypeStruct((half, in_width), BF),
        jax.ShapeDtypeStruct((2 * wpad, D), F32),
        jax.ShapeDtypeStruct((wpad, D), F32),
    ]
    first = kept is None
    operands = [place, *sec, *cot, gate, up, down, sin, sdn] + ([] if first else list(kept))
    any_space = pl.BlockSpec(memory_space=pl.ANY)
    smem = pl.BlockSpec(memory_space=pltpu.SMEM)
    return pl.pallas_call(
        functools.partial(expert_kernel, local_experts, capacity, rows, experts, first),
        out_shape=shapes,
        in_specs=[smem] + [any_space] * (len(operands) - 1),
        out_specs=[any_space] * len(shapes),
        scratch_shapes=[
            pltpu.VMEM((tokens, sec[0].shape[1]), BF),
            pltpu.VMEM((tokens, cot[0].shape[1]), BF),
            pltpu.VMEM(gate.shape, BF),
            pltpu.VMEM(up.shape, BF),
            pltpu.VMEM(down.shape, BF),
            pltpu.VMEM(sin.shape, BF),
            pltpu.VMEM(sdn.shape, BF),
            pltpu.VMEM((local_experts * per, D), BF),
            pltpu.VMEM((local_experts * per, D), BF),
            pltpu.VMEM((blocks, local_experts * capacity, D), BF),
            pltpu.VMEM((blocks, local_experts * capacity, in_width), BF),
            pltpu.VMEM((local_experts, per, hidden), BF),
            pltpu.VMEM((local_experts, per, hidden), BF),
            pltpu.VMEM((local_experts, per, hidden), BF),
            pltpu.VMEM((tokens, local_experts * capacity), BF),
            pltpu.VMEM((local_experts * per, 128), F32),
            pltpu.VMEM((tokens, wpad), BF),
            pltpu.VMEM((tokens, 2 * wpad), BF),
            pltpu.VMEM((2 * wpad, D), F32),
            pltpu.VMEM((wpad, D), F32),
            pltpu.SemaphoreType.DMA((9,)),
            pltpu.SemaphoreType.DMA((5 * local_experts + 2,)),
            pltpu.SemaphoreType.DMA((2, 2, half // rows)),
        ],
        input_output_aliases={} if first else {10 + i: i for i in range(5)},
        compiler_params=pltpu.CompilerParams(vmem_limit_bytes=63 * 1024 * 1024),
        cost_estimate=pl.CostEstimate(flops=1 << 20, bytes_accessed=1 << 16, transcendentals=0),
    )(*operands)


def turn(values, cosine, sine):
    lane = lax.broadcasted_iota(jnp.int32, values.shape, 1)
    partner = jnp.where(
        lane % DR < DR // 2, pltpu.roll(values, 2 * DR - DR // 2, 1), pltpu.roll(values, DR // 2, 1)
    )
    return values * cosine + partner * sine


def score_block(i, block, image, scores):
    row = lax.broadcasted_iota(jnp.int32, scores.shape, 0) + i * block
    column = lax.broadcasted_iota(jnp.int32, scores.shape, 1)
    allowed = (column <= row) | ((column >= i * block) & image)
    return jnp.where(allowed, scores * ((DN + DR) ** (-0.5)), NEGATIVE)


def head_part(values, h):
    lane = lax.broadcasted_iota(jnp.int32, values.shape, 1)
    return jnp.where(lane // DR == h, values.astype(F32), 0.0).astype(BF)


def attend_kernel(
    heads, rows, place, seq, gain, lgain, wq, wd, wup, cos, sin, out, first, q_out, lat_out, kr_out, ex_out, own_out, down_v
):
    block = PIECE
    nope = heads * DN
    for i in range(seq.shape[0] // block):
        at = slice(i * block, (i + 1) * block)
        values = seq[at, :D].astype(F32)
        low = (values * rms_parts(values) * gain[...]).astype(BF)
        first[at, :] = low
        q = mm(low, wq[...])
        down = mm(low, wd[...])
        down_v[at, :] = down
        latent = down[:, :KVR]
        lat = (latent * rms_parts(latent) * lgain[...]).astype(BF)
        lat_out[at, :] = lat
        ex_out[at, :] = mm(lat, wup[...]).astype(BF)
        turned = turn(down[:, KVR : KVR + 2 * DR], cos[at, :], sin[at, :])
        lane = lax.broadcasted_iota(jnp.int32, turned.shape, 1)
        turned = jnp.where(lane < DR, turned, 0.0)
        kr_out[at, :] = (turned + pltpu.roll(turned, DR, 1)).astype(BF)
        q_rope = turn(q[:, nope:], cos[at, :], sin[at, :]).astype(BF)
        q_out[at, :nope] = q[:, :nope].astype(BF)
        q_out[at, nope:] = q_rope
        image = seq[at, D : D + 128][:, :1].astype(F32) > 0
        n = (i + 1) * block
        for h in range(heads):
            mine = slice(h * (DN + DV), h * (DN + DV) + DN)
            scores = mm_nt(q_out[at, h * DN : (h + 1) * DN], ex_out[:n, mine])
            scores = scores + mm_nt(head_part(q_rope, h), kr_out[:n, :])
            scores = score_block(i, block, image, scores)
            weight = jnp.exp(scores - jnp.max(scores, axis=1, keepdims=True))
            weight = weight / jnp.sum(weight, axis=1, keepdims=True)
            value = ex_out[:n, h * (DN + DV) + DN : (h + 1) * (DN + DV)]
            out[at, h * DV : (h + 1) * DV] = mm(weight.astype(BF), value).astype(BF)
    own_out[...] = down_v[pl.ds(pl.multiple_of(place[0] * rows, rows), rows), :]


def attend(place, seq, gain, lgain, wq, wd, wup, cos, sin, heads, rows):
    length = seq.shape[0]
    shapes = [
        jax.ShapeDtypeStruct((length, heads * DV), BF),
        jax.ShapeDtypeStruct((length, D), BF),
        jax.ShapeDtypeStruct((length, wq.shape[1]), BF),
        jax.ShapeDtypeStruct((length, KVR), BF),
        jax.ShapeDtypeStruct((length, 2 * DR), BF),
        jax.ShapeDtypeStruct((length, wup.shape[1]), BF),
        jax.ShapeDtypeStruct((rows, wd.shape[1]), F32),
    ]
    vmem = pl.BlockSpec(memory_space=pltpu.VMEM)
    return pl.pallas_call(
        functools.partial(attend_kernel, heads, rows),
        out_shape=shapes,
        in_specs=[pl.BlockSpec(memory_space=pltpu.SMEM)] + [vmem] * 8,
        out_specs=[vmem] * len(shapes),
        scratch_shapes=[pltpu.VMEM((length, wd.shape[1]), F32)],
        compiler_params=pltpu.CompilerParams(vmem_limit_bytes=56 * 1024 * 1024),
        cost_estimate=pl.CostEstimate(flops=1 << 20, bytes_accessed=1 << 16, transcendentals=0),
    )(place, seq, gain, lgain, wq, wd, wup, cos, sin)


def attend_back_kernel(
    heads, place, grad, flags, first, q, kr, ex, lat, wq, wup, cos, sin,
    gain_out, first_keep, first_send, lat_keep, lat_send, pack_out,
    dk_v, dv_v, dr_v, qg_v, eg_v,
):
    block = PIECE
    nope = heads * DN
    length = first.shape[0]
    half = length // 2
    scale = (DN + DR) ** (-0.5)
    dk_v[...] = jnp.zeros_like(dk_v)
    dv_v[...] = jnp.zeros_like(dv_v)
    dr_v[...] = jnp.zeros_like(dr_v)
    for i in range(length // block):
        at = slice(i * block, (i + 1) * block)
        n = (i + 1) * block
        image = flags[at, :1].astype(F32) > 0
        rope_grad = jnp.zeros((block, 2 * DR), F32)
        for h in range(heads):
            mine = slice(h * (DN + DV), h * (DN + DV) + DN)
            value = ex[:n, h * (DN + DV) + DN : (h + 1) * (DN + DV)]
            q_nope = q[at, h * DN : (h + 1) * DN]
            q_rope = head_part(q[at, nope:], h)
            scores = mm_nt(q_nope, ex[:n, mine]) + mm_nt(q_rope, kr[:n, :])
            scores = score_block(i, block, image, scores)
            weight = jnp.exp(scores - jnp.max(scores, axis=1, keepdims=True))
            weight = weight / jnp.sum(weight, axis=1, keepdims=True)
            upstream = grad[at, h * DV : (h + 1) * DV]
            dprob = mm_nt(upstream, value)
            dv_v[:n, h * DV : (h + 1) * DV] += mm_tn(weight.astype(BF), upstream)
            inner = jnp.sum(weight * dprob, axis=1, keepdims=True)
            back = (weight * (dprob - inner)).astype(BF)
            qg_v[at, h * DN : (h + 1) * DN] = (mm(back, ex[:n, mine]) * scale).astype(BF)
            turned = mm(back, kr[:n, :])
            lane = lax.broadcasted_iota(jnp.int32, turned.shape, 1)
            rope_grad = jnp.where(lane // DR == h, turned * scale, rope_grad)
            dk_v[:n, h * DN : (h + 1) * DN] += mm_tn(back, q_nope)
            dr_v[:n, :] += mm_tn(back, q_rope)
        qg_v[at, nope:] = turn(rope_grad, cos[at, :], -sin[at, :]).astype(BF)
    for h in range(heads):
        mine = slice(h * (DN + DV), h * (DN + DV) + DN)
        eg_v[:, mine] = (dk_v[:, h * DN : (h + 1) * DN] * scale).astype(BF)
        eg_v[:, h * (DN + DV) + DN : (h + 1) * (DN + DV)] = dv_v[:, h * DV : (h + 1) * DV].astype(BF)
    key_rope = dr_v[...]
    key_rope = (key_rope + pltpu.roll(key_rope, DR, 1)) * scale
    dr_v[...] = key_rope
    keep = pl.ds(pl.multiple_of(place[1] * half, half), half)
    send = pl.ds(pl.multiple_of((1 - place[1]) * half, half), half)
    total = jnp.zeros((1, D), F32)
    for at, to_lat, to_first in ((send, lat_send, first_send), (keep, lat_keep, first_keep)):
        to_lat[:, :KVR] = mm_nt(eg_v[at, :], wup[...]).astype(BF)
        to_lat[:, KVR:] = dr_v[at, :].astype(BF)
        part = mm_nt(qg_v[at, :], wq[...])
        to_first[...] = part.astype(BF)
        total = total + jnp.sum(part * first[at, :].astype(F32), axis=0, keepdims=True)
    gain_out[...] = total
    owners, pack_rows, _ = pack_out.shape
    wide = wq.shape[1]
    q_rows = D // owners
    pack_out[:, :q_rows, :wide] = mm_tn(first[...], qg_v[...]).astype(BF).reshape(owners, q_rows, wide)
    pack_out[:, :q_rows, wide:] = jnp.zeros((owners, q_rows, pack_out.shape[2] - wide), BF)
    pack_out[:, q_rows:, :] = mm_tn(lat[...], eg_v[...]).astype(BF).reshape(owners, pack_rows - q_rows, -1)


def attend_back(place, grad, flags, first, q, kr, ex, lat, wq, wup, cos, sin, heads, owners):
    length = first.shape[0]
    half = length // 2
    wide = KVR + 2 * DR
    shapes = [
        jax.ShapeDtypeStruct((1, D), F32),
        jax.ShapeDtypeStruct((half, D), BF),
        jax.ShapeDtypeStruct((half, D), BF),
        jax.ShapeDtypeStruct((half, wide), BF),
        jax.ShapeDtypeStruct((half, wide), BF),
        jax.ShapeDtypeStruct((owners, (D + KVR) // owners, wup.shape[1]), BF),
    ]
    vmem = pl.BlockSpec(memory_space=pltpu.VMEM)
    return pl.pallas_call(
        functools.partial(attend_back_kernel, heads),
        out_shape=shapes,
        in_specs=[pl.BlockSpec(memory_space=pltpu.SMEM)] + [vmem] * 11,
        out_specs=[vmem] * len(shapes),
        scratch_shapes=[
            pltpu.VMEM((length, heads * DN), F32),
            pltpu.VMEM((length, heads * DV), F32),
            pltpu.VMEM((length, 2 * DR), F32),
            pltpu.VMEM((length, q.shape[1]), BF),
            pltpu.VMEM((length, ex.shape[1]), BF),
        ],
        compiler_params=pltpu.CompilerParams(vmem_limit_bytes=56 * 1024 * 1024),
        cost_estimate=pl.CostEstimate(flops=1 << 20, bytes_accessed=1 << 16, transcendentals=0),
    )(place, grad, flags, first, q, kr, ex, lat, wq, wup, cos, sin)


def on_device(
    tokens,
    attention_norm,
    query_weight,
    latent_down,
    latent_norm,
    latent_up,
    output_weight,
    post_norm,
    shared_gate,
    shared_up,
    shared_down,
    router_weight,
    expert_gate,
    expert_up,
    expert_down,
    image_piece_index,
    routes,
    cotangent,
):
    rows = tokens.shape[0]
    c_size, k_size, z_size = (lax.axis_size(a) for a in EVERY)
    c, k, z = (lax.axis_index(a) for a in EVERY)
    column_size = k_size * z_size
    device_count = c_size * column_size
    local_experts = expert_gate.shape[0]
    experts = router_weight.shape[1]
    capacity = rows * TOPK * 4 // (3 * experts)
    length = column_size * rows
    heads = H // column_size
    width = shared_down.shape[0]
    score_scale = (DN + DR) ** (-0.5)
    weight_rows = query_weight.shape[0]
    up_rows = latent_up.shape[0]

    paired = H == 4 * c_size and heads == 2 and column_size == 8

    def by_owner(array, n):
        if paired:
            array = array.reshape(-1, 2, 2, 4, n).transpose(0, 3, 1, 2, 4)
        return array.reshape(-1, column_size, heads * n)

    def by_head(array, n):
        if paired:
            array = array.reshape(-1, 4, 2, 2, n).transpose(0, 2, 3, 1, 4)
        return array.reshape(-1, H * n)

    flag = (image_piece_index > 0).astype(BF)[:, None]
    expert_ids = jnp.arange(experts, dtype=jnp.int32)
    named = jnp.any(routes[:, :, None] == expert_ids[None, None, :], axis=1)

    out_mine = in_order(gather_z(output_weight.astype(BF)), z)
    extra = -(-weight_rows // 8) * 8 + 8 - weight_rows
    down_width = KVR + DR
    small_width = lanes(max(down_width + experts + 8, weight_rows))
    gains = jnp.stack(
        [attention_norm, post_norm, jnp.pad(latent_norm, (0, weight_rows - latent_norm.shape[0]))]
    )
    small = jnp.concatenate([latent_down, router_weight], axis=1).astype(BF)
    small = jnp.pad(small, ((0, 0), (0, small_width - small.shape[1])))
    gains = jnp.pad(gains.astype(BF), ((0, extra - 3), (0, small_width - weight_rows)))
    small = jnp.concatenate([small, gains], axis=0)
    q_width = heads * (DN + DR)
    kv_width = heads * (DN + DV)
    q_out = by_owner(query_weight.astype(BF), DN + DR).transpose(1, 0, 2)
    q_out = q_out.reshape(column_size, weight_rows, heads, DN + DR)
    q_out = jnp.concatenate(
        [q_out[..., :DN].reshape(column_size, weight_rows, -1), q_out[..., DN:].reshape(column_size, weight_rows, -1)],
        axis=2,
    )
    q_out = jnp.pad(q_out, ((0, 0), (0, 0), (0, kv_width - q_width)))
    up_out = by_owner(latent_up.astype(BF), DN + DV).transpose(1, 0, 2)
    head_pack = jnp.concatenate([q_out, up_out], axis=1)
    head_pack = lax.all_to_all(head_pack, COLUMN, split_axis=0, concat_axis=0, tiled=True)
    token_units = gather_z(after(widen(tokens, flag), head_pack))
    cot_units = gather_z(after(widen(cotangent, named), *token_units[1:]))
    head_pack = [head_pack] + [swap(head_pack, "c", d) for d in range(1, c_size)]
    small, small_recv = gather_weight(small)
    mine = in_order(after_all(token_units, *head_pack[1:], *small_recv), z)
    sequence = in_order([mine, swap(mine, "k", 1)], k).reshape(length, -1)
    small = small.reshape(device_count, weight_rows + extra, small_width)
    full_small = small[:, :weight_rows].reshape(D, small_width)
    full_router = full_small[:, down_width : down_width + experts]
    full_gains = small[:, weight_rows : weight_rows + 3, :weight_rows].astype(F32)
    attn_gain = full_gains[:, 0].reshape(D)
    post_gain = full_gains[:, 1].reshape(D)
    latent_gain = full_gains[:, 2, : latent_norm.shape[0]].reshape(KVR)
    out_mine = after(out_mine, *head_pack[1:])
    out_planes = [out_mine] + [swap(out_mine, "c", d) for d in range(1, c_size)]
    head_pack = in_order(head_pack, c)
    head_query = head_pack[:, :, :weight_rows, :q_width].reshape(D, q_width)
    head_up = head_pack[:, :, weight_rows:].reshape(KVR, kv_width)
    shared_pack = jnp.concatenate(
        [
            shared_gate.astype(BF).reshape(weight_rows, device_count, width),
            shared_up.astype(BF).reshape(weight_rows, device_count, width),
        ],
        axis=2,
    ).transpose(1, 0, 2)
    shared_in = lax.all_to_all(after(shared_pack, *token_units[1:]), EVERY, split_axis=0, concat_axis=0, tiled=True)
    shared_low = shared_down.astype(BF)

    places = jnp.arange(length, dtype=F32)
    frequency = ROPE_BASE ** (-2.0 * jnp.arange(DR // 2, dtype=F32) / DR)
    angles = places[:, None] * frequency[None, :]
    cosine, sine = jnp.cos(angles), jnp.sin(angles)
    cosine_wide = jnp.tile(cosine, (1, 4))
    sine_wide = jnp.tile(jnp.concatenate([-sine, sine], axis=1), (1, 2))
    here = k * z_size + z

    def own_rows(array):
        return lax.dynamic_slice_in_dim(array, here * rows, rows, axis=0)

    spot = jnp.stack([here, k]).astype(jnp.int32)
    heads_out, first_low, query_low, latent_low, rope_low, expanded, down_raw = attend(
        spot, sequence, attn_gain[None], latent_gain[None], head_query, full_small, head_up,
        cosine_wide, sine_wide, heads, rows,
    )
    own_values = tokens.astype(F32)
    own_scale = rms_parts(own_values)
    own_first_low = (own_values * own_scale * attn_gain).astype(BF)
    latent_raw = down_raw[:, :KVR]
    latent_scale = rms_parts(latent_raw)

    def heads_to_tokens(array):
        n = array.shape[1]
        moved = lax.all_to_all(
            array.reshape(column_size, rows, n), COLUMN, split_axis=0, concat_axis=0, tiled=True
        )
        return by_head(moved.transpose(1, 0, 2), n // heads)

    def tokens_to_heads(array):
        n = array.shape[1] // H
        moved = lax.all_to_all(
            by_owner(array, n).transpose(1, 0, 2), COLUMN, split_axis=0, concat_axis=0, tiled=True
        )
        return moved.reshape(length, heads * n)

    shared_in, *cot_units = after_all([shared_in, *cot_units], heads_out)
    cot_own = jnp.concatenate(cot_units, axis=0)
    shared_in = shared_in.reshape(D, 2 * width)
    room = ((0, 0), (0, lanes(width) - width))
    shared_in = jnp.concatenate(
        [jnp.pad(shared_in[:, :width], room), jnp.pad(shared_in[:, width:], room)], axis=1
    )
    out_planes = in_order(after_all(out_planes, heads_out, cot_own), c)
    full_out = in_order([out_planes, swap(out_planes, "k", 1)], k)
    full_out = full_out.transpose(1, 0, 2, 3, 4).reshape(D, D)

    def plane_groups(own):
        near = [swap(own, "c", d) for d in range(1, c_size - 1)]
        return [own, *near, swap(after(own, *near), "c", c_size - 1)]

    cot_groups = [cot_own] + [swap(cot_own, "c", d) for d in range(1, c_size)]
    heads_low = after(heads_to_tokens(after(heads_out, cot_own, shared_in)), full_out)
    residual = tokens.astype(F32) + mm(heads_low, full_out)
    second_scale = rms_parts(residual)
    second_low = (residual * second_scale * post_gain).astype(BF)
    router_probs = jax.nn.softmax(mm(second_low, full_router), axis=-1)

    probs_high = router_probs.astype(BF)
    probs_rest = (router_probs - probs_high.astype(F32)).astype(BF)
    second_own = jnp.concatenate(
        gather_z(widen(second_low, jnp.concatenate([probs_high, probs_rest], axis=1))), axis=0
    )
    second_own = after(second_own, *cot_groups[1:])
    second_groups = plane_groups(second_own)
    pair = lambda group: (group, swap(group, "k", 1))
    cot_groups = [pair(g) for g in cot_groups]
    wpad = lanes(width)
    place = jnp.stack([(c * k_size + k) * local_experts, jnp.zeros((), jnp.int32)]).astype(jnp.int32)
    shared_rows = jnp.pad(shared_low, ((0, wpad - width), (0, 0)))
    weights = (
        jnp.swapaxes(expert_gate, 1, 2),
        jnp.swapaxes(expert_up, 1, 2),
        expert_down,
        shared_in,
        shared_rows,
    )
    kept, sg_parts, sd_parts, sums, out_sums, marks = None, [], [], [], [], []
    arrived = []
    for d in range(c_size):
        where = place.at[1].set(d)
        group = second_groups[d]
        if d == 1:
            group, *second_groups[2:-1] = after_all([group, *second_groups[2:-1]], marks[0])
        if d == c_size - 2:
            second_groups[-1] = after(second_groups[-1], marks[d - 1])
            where = after(where, second_groups[-1])
        if d > 1:
            where = after(where, out_sums[d - 2], sums[d - 1])
        results = list(
            expert_group(
                where, pair(group), cot_groups[d], weights, kept, capacity, rows, experts, c_size
            )
        )
        kept = results[:5]
        marks.append(results[10])
        if d == c_size - 1:
            results[7] = after(results[7], *arrived)
        sums.append(core_sum(*results[7:9], d))
        if d:
            arrived.append(swap(sums[d], "c", d))
        if d == c_size - 1:
            kept = after_all(kept, *arrived[:-1], sums[d])
            results[6] = after(results[6], arrived[-1])
        out_sums.append(core_sum(*results[5:7], d))
        sg_parts.append(results[9])
        sd_parts.append(results[10])
    plane = functools.reduce(lambda total, block: total + block.astype(F32), arrived, sums[0])
    expert_in, cot_in, act_weighted, gate_grad, up_grad = kept
    ein = lambda spec, a, b: jnp.einsum(spec, a, b, preferred_element_type=F32)
    expert_down_grad = ein("esf,esd->efd", act_weighted, cot_in)
    expert_gate_grad = jnp.swapaxes(ein("esf,esd->efd", gate_grad, expert_in), 1, 2)
    expert_up_grad = jnp.swapaxes(ein("esf,esd->efd", up_grad, expert_in), 1, 2)
    plane = after(plane, expert_down_grad, expert_gate_grad, expert_up_grad)
    second_sum = scatter_z(z_units(plane, rows))
    out_near = [swap(after(out_sums[d], *arrived), "c", d) for d in range(1, c_size - 1)]
    second_sum = after(second_sum, *out_near, out_sums[-1])
    out_far = swap(after(out_sums[-1], *out_near), "c", c_size - 1)
    probs_grad = second_sum[:, D : D + experts]
    logits_grad = (
        router_probs * (probs_grad - jnp.sum(router_probs * probs_grad, axis=-1, keepdims=True))
    ).astype(BF)
    second_grad = second_sum[:, :D] + mm_nt(logits_grad, full_router)
    norm_part, post_terms = rms_back(residual, second_scale, post_gain, second_grad)
    residual_grad = cotangent.astype(F32) + norm_part
    attn_grad_low = residual_grad.astype(BF)
    heads_grad = tokens_to_heads(mm_nt(attn_grad_low, full_out).astype(BF))
    output_pieces = core_pieces(mm_tn(heads_low, attn_grad_low).astype(BF))

    gain_part, first_keep, first_send, latent_keep, latent_send, head_grad = attend_back(
        after(spot, *output_pieces), heads_grad, sequence[:, D:], first_low, query_low,
        rope_low, expanded, latent_low, head_query, head_up, cosine_wide, sine_wide, heads, device_count,
    )
    def column_sum(keep, send):
        summed = keep.astype(F32) + swap(send, "k", 1).astype(F32)
        summed = summed.reshape(z_size, rows, keep.shape[1])
        return scatter_z([pick(summed, z ^ d) for d in range(z_size)])

    latent_sum = column_sum(latent_keep, after(latent_send, out_far))
    shared_in_grad = sum(sg_parts[1:], sg_parts[0])
    shared_in_grad = jnp.concatenate(
        [shared_in_grad[:width], shared_in_grad[wpad : wpad + width]], axis=0
    ).astype(BF)
    shared_down_grad = sum(sd_parts[1:], sd_parts[0])[:width]
    shared_back = shared_in_grad.reshape(2 * width, c_size, column_size, weight_rows).transpose(2, 1, 3, 0)
    shared_back = lax.all_to_all(
        after(shared_back, latent_keep), COLUMN, split_axis=0, concat_axis=0, tiled=True
    )
    latent_raw_grad, latent_terms = rms_back(
        latent_raw, latent_scale, latent_gain, latent_sum[:, :KVR]
    )
    rope_raw_grad = rotate(
        latent_sum[:, KVR:down_width], own_rows(cosine), own_rows(sine), -1.0
    )
    down_grad_low = jnp.concatenate([latent_raw_grad, rope_raw_grad], axis=-1).astype(BF)
    first_own = mm_nt(down_grad_low, full_small[:, :down_width])
    attn_gain_grad = gain_part[0] / attn_gain + jnp.sum(
        first_own * (own_values * own_scale), axis=0
    )
    gain_grads = jnp.stack(
        [
            attn_gain_grad,
            jnp.sum(post_terms, axis=0),
            jnp.pad(
                jnp.sum(latent_terms, axis=0).reshape(device_count, latent_norm.shape[0]),
                ((0, 0), (0, weight_rows - latent_norm.shape[0])),
            ).reshape(D),
        ]
    )
    first_gain = down_width + experts
    small_right = jnp.zeros((2 * rows + 8, small_width), BF)
    small_right = small_right.at[:rows, :down_width].set(down_grad_low)
    small_right = small_right.at[rows : 2 * rows, down_width:first_gain].set(logits_grad)
    ones = (jnp.arange(8)[:, None] == jnp.arange(small_width)[None, :] - first_gain).astype(BF)
    small_right = small_right.at[2 * rows :].set(ones)
    small_left = jnp.concatenate(
        [own_first_low, second_low, jnp.pad(gain_grads, ((0, 5), (0, 0))).astype(BF)], axis=0
    )
    output_near = [swap(output_pieces[d], "c", d) for d in range(1, c_size - 1)]
    small_pieces = core_pieces(mm_tn(small_left, small_right).astype(BF))
    first_sum = column_sum(first_keep, first_send)
    first_sum, *small_pieces = after_all([first_sum, *small_pieces], *output_near)
    out_plane = functools.reduce(
        lambda total, block: total + block.astype(F32),
        after_all([*out_near, out_far], first_sum),
        out_sums[0],
    )
    out_units = z_units(out_plane, rows)
    out_units = out_units[:1] + [swap(unit.astype(BF), "z", d) for d, unit in enumerate(out_units) if d]
    output_moved = [
        *output_near, swap(after(output_pieces[-1], *output_near), "c", c_size - 1)
    ]
    head_grad = head_grad.reshape(c_size, column_size, weight_rows + up_rows, kv_width)
    head_moved = [swap(pick(head_grad, c ^ d), "c", d) for d in range(1, c_size)]
    small_plane, _ = plane_sum(small_pieces, *head_moved)
    output_plane = functools.reduce(
        lambda total, block: total + block.astype(F32),
        after_all(output_moved, small_plane),
        output_pieces[0],
    )
    shared_back = after(shared_back, small_plane)
    shared_moved = [
        swap(lax.dynamic_index_in_dim(shared_back, c ^ d, axis=1, keepdims=False), "c", d)
        for d in range(1, c_size)
    ]
    first_grad = first_sum + first_own
    out_sum = functools.reduce(
        lambda total, block: total + block.astype(F32), after_all(out_units[1:], first_grad), out_units[0]
    )
    layer_out = (residual + out_sum).astype(BF)
    first_norm_grad, _ = rms_back(own_values, own_scale, attn_gain, first_grad)
    tokens_grad = residual_grad + first_norm_grad
    own_both = z_sum(jnp.concatenate([output_plane, small_plane], axis=1))
    own_output, own_small = own_both[:, :D], own_both[:, D:]
    shared_back = in_order(
        [
            lax.dynamic_index_in_dim(shared_back, c, axis=1, keepdims=False),
            *after_all(shared_moved, own_both),
        ],
        c,
    ).reshape(device_count, weight_rows, 2 * width).transpose(1, 0, 2)
    head_sum = pick(head_grad, c).astype(F32)
    for block in after_all(head_moved, small_plane):
        head_sum = head_sum + block.astype(F32)
    head_sum = lax.all_to_all(head_sum.astype(BF), COLUMN, split_axis=0, concat_axis=0, tiled=True)
    own_query = head_sum[:, :weight_rows, :q_width].transpose(1, 0, 2)
    own_query = jnp.concatenate(
        [
            own_query[..., : heads * DN].reshape(weight_rows, column_size, heads, DN),
            own_query[..., heads * DN :].reshape(weight_rows, column_size, heads, DR),
        ],
        axis=3,
    )
    own_query = by_head(own_query.reshape(weight_rows, column_size, q_width), DN + DR)
    own_up = by_head(head_sum[:, weight_rows:].transpose(1, 0, 2), DN + DV)
    own_gate = shared_back[:, :, :width].reshape(weight_rows, -1)
    own_shared_up = shared_back[:, :, width:].reshape(weight_rows, -1)
    return (
        layer_out,
        tokens_grad,
        own_small[:, first_gain],
        own_query.astype(F32),
        own_small[:, :down_width],
        own_small[: latent_norm.shape[0], first_gain + 2],
        own_up.astype(F32),
        own_output,
        own_small[:, first_gain + 1],
        own_gate.astype(F32),
        own_shared_up.astype(F32),
        shared_down_grad,
        own_small[:, down_width:first_gain],
        expert_gate_grad,
        expert_up_grad,
        expert_down_grad,
    )


def solution(mesh):
    expert_size, z_size = mesh.devices.shape
    fine = Mesh(mesh.devices.reshape(expert_size // 2, 2, z_size), EVERY)
    row, flat = P(EVERY, None), P(EVERY)
    wide, tall = P(("c", "k"), None, "z"), P(("c", "k"), "z", None)
    return jax.shard_map(
        on_device,
        mesh=fine,
        in_specs=(row, flat, row, row, flat, row, row, flat, row, row, row, row)
        + (wide, wide, tall, flat, row, row),
        out_specs=(row, row, flat, row, row, flat, row, row, flat, row, row, row, row)
        + (wide, wide, tall),
        check_vma=False,
    )
```

```python
import functools

import jax
import jax.numpy as jnp
from jax import lax
from jax.experimental import pallas as pl
from jax.experimental.pallas import tpu as pltpu
from jax.sharding import Mesh, PartitionSpec as P

D = 2048
H = 16
DN = 128
DR = 64
DV = 128
KVR = 512
TOPK = 6
PIECE = 256
EPSILON = 1e-06
ROPE_BASE = 10000.0
NEGATIVE = -1e30
BF = jnp.bfloat16
F32 = jnp.float32
EVERY = ("c", "k", "z")
COLUMN = ("k", "z")


def swap(block, axis, distance):
    n = lax.axis_size(axis)
    return lax.ppermute(block, axis, [(i, i ^ distance) for i in range(n)])


def lanes(n):
    return -(-n // 128) * 128


def widen(block, extra):
    room = lanes(extra.shape[1]) - extra.shape[1]
    return jnp.concatenate([block, jnp.pad(extra.astype(BF), ((0, 0), (0, room)))], axis=1)


def dot(a, b, dims):
    return lax.dot_general(a, b, (dims, ((), ())), preferred_element_type=F32)


def mm(a, b):
    return dot(a, b, ((1,), (0,)))


def mm_nt(a, b):
    return dot(a, b, ((1,), (1,)))


def mm_tn(a, b):
    return dot(a, b, ((0,), (0,)))


def after(array, *others):
    return lax.optimization_barrier((array, *others))[0]


def after_all(arrays, *others):
    return lax.optimization_barrier((tuple(arrays), *others))[0]


def put(buffer, block, index):
    return lax.dynamic_update_slice_in_dim(buffer, block[None], index, axis=0)


def gather_z(unit):
    return [unit] + [swap(unit, "z", d) for d in range(1, lax.axis_size("z"))]


def in_order(blocks, index):
    whole = jnp.zeros((len(blocks), *blocks[0].shape), blocks[0].dtype)
    for d, block in enumerate(blocks):
        whole = put(whole, block, index ^ d)
    return whole


def gather_weight(unit):
    c_size, k_size, _ = (lax.axis_size(a) for a in EVERY)
    c, k, z = (lax.axis_index(a) for a in EVERY)
    mine = in_order(gather_z(unit), z)
    planes = [mine] + [swap(mine, "c", d) for d in range(1, c_size)]
    own = in_order(planes, c)
    other = swap(own, "k", 1)
    halves = in_order([own, other], k)
    return halves.transpose(1, 0, 2, 3, 4), planes[1:]


def scatter_z(blocks):
    total = blocks[0]
    for d in range(1, len(blocks)):
        total = total + swap(blocks[d].astype(BF), "z", d).astype(F32)
    return total


def scatter_column(part, rows):
    z_size = lax.axis_size("z")
    k, z = lax.axis_index("k"), lax.axis_index("z")
    grid = part.reshape(2, z_size, rows, part.shape[1])
    summed = pick(grid, k) + swap(pick(grid, k ^ 1).astype(BF), "k", 1).astype(F32)
    return scatter_z([pick(summed, z ^ d) for d in range(z_size)])


def core_sum(own, other, distance):
    summed = own.astype(F32) + swap(other, "k", 1).astype(F32)
    return summed.astype(BF) if distance else summed


def plane_sum(sums, *others):
    moved = [swap(block, "c", d) for d, block in enumerate(sums) if d]
    if others:
        moved = after_all(moved, *others)
    total = sums[0]
    for block in moved:
        total = total + block.astype(F32)
    return total, moved


def z_units(total, rows):
    return [total[d * rows : (d + 1) * rows] for d in range(lax.axis_size("z"))]


def pick(array, index):
    return lax.dynamic_index_in_dim(array, index, axis=0, keepdims=False)


def core_pieces(part):
    c_size, k_size, z_size = (lax.axis_size(a) for a in EVERY)
    c, k = lax.axis_index("c"), lax.axis_index("k")
    grid = part.reshape(c_size, k_size, part.shape[0] // (c_size * k_size), part.shape[1])
    got = swap(lax.dynamic_index_in_dim(grid, k ^ 1, axis=1, keepdims=False), "k", 1)
    kept = lax.dynamic_index_in_dim(grid, k, axis=1, keepdims=False)
    pieces = []
    for d in range(c_size):
        piece = pick(kept, c ^ d).astype(F32) + pick(got, c ^ d).astype(F32)
        pieces.append(piece.astype(BF) if d else piece)
    return pieces


def pieces_sum(pieces, *others):
    total, _ = plane_sum(pieces, *others)
    return z_sum(total)


def z_sum(total):
    z_size, z = lax.axis_size("z"), lax.axis_index("z")
    total = total.reshape(z_size, total.shape[0] // z_size, total.shape[1])
    return scatter_z([pick(total, z ^ d) for d in range(z_size)])


def scatter_weight(part):
    return pieces_sum(core_pieces(part))


def rms_parts(values):
    return lax.rsqrt(jnp.mean(values * values, axis=-1, keepdims=True) + EPSILON)


def rms_back(values, scale, gain, grad):
    weighted = grad * gain
    inner = jnp.mean(weighted * values, axis=-1, keepdims=True)
    return scale * (weighted - values * (scale * scale * inner)), grad * values * scale


def rotate(values, cosine, sine, sign):
    half = values.shape[-1] // 2
    a, b = values[..., :half], values[..., half:]
    return jnp.concatenate([a * cosine - sign * b * sine, b * cosine + sign * a * sine], axis=-1)


def expert_kernel(
    local_experts,
    capacity,
    rows,
    experts,
    first,
    place_ref,
    sec_a,
    sec_b,
    cot_a,
    cot_b,
    gate_hbm,
    up_hbm,
    down_hbm,
    sin_hbm,
    sdn_hbm,
    *rest,
):
    rest = rest if first else rest[5:]
    (x_out, c_out, aw_out, gg_out, ug_out, out_a, out_b, in_a, in_b, sg_out, sd_out) = rest[:11]
    (sec_v, cot_v, gate_v, up_v, down_v, sin_v, sdn_v, x_v, c_v, y_v, z_v, aw_v, gg_v, ug_v) = rest[11:25]
    (choose_v, prob_v, sact_v, slow_v, sgp_v, sdp_v, sem_in, sem_out, sem_block) = rest[25:34]
    half = sec_a.shape[0]
    blocks = 2 * half // rows
    per = blocks * capacity
    wpad = sdn_v.shape[0]
    base = place_ref[1] * per

    def copy(src, dst, sem, i):
        made = pltpu.make_async_copy(src, dst, sem.at[i])
        made.start()
        return made

    near = [
        copy(sec_a, sec_v.at[pl.ds(0, half)], sem_in, 0),
        copy(cot_a, cot_v.at[pl.ds(0, half)], sem_in, 2),
    ]
    first_expert = place_ref[0]
    tail = cot_v.shape[1] - D
    row_i = lax.broadcasted_iota(jnp.int32, (rows, rows), 0)
    col_i = lax.broadcasted_iota(jnp.int32, (rows, rows), 1)
    earlier = (col_i < row_i).astype(BF)
    lane = lax.broadcasted_iota(jnp.int32, (rows, tail), 1)
    slot = lax.broadcasted_iota(jnp.int32, (rows, local_experts * capacity), 1).astype(F32)
    sec_tail = sec_v.shape[1] - D
    tail_lane = lax.broadcasted_iota(jnp.int32, (capacity, sec_tail), 1)

    def gather(b, carry):
        at = pl.ds(pl.multiple_of(b * rows, rows), rows)
        named = cot_v[at, D:]
        rank = mm(earlier, named)
        code = jnp.where((named.astype(F32) > 0) & (rank < capacity), rank, -1e6)
        chosen = jnp.zeros(slot.shape, F32)
        for e in range(local_experts):
            own = jnp.sum(jnp.where(lane == first_expert + e, code, 0.0), axis=1, keepdims=True)
            chosen = jnp.where(own + e * capacity == slot, 1.0, chosen)
        choose = chosen.astype(BF)
        choose_v[at, :] = choose
        picked = mm_tn(choose, sec_v[at, :])
        cots = mm_tn(choose, cot_v[at, :D])
        for e in range(local_experts):
            mine = slice(e * capacity, (e + 1) * capacity)
            to = pl.ds(pl.multiple_of(e * per + b * capacity, capacity), capacity)
            x_v[to, :] = picked[mine, :D].astype(BF)
            c_v[to, :] = cots[mine].astype(BF)
            which = first_expert + e
            hits = (tail_lane == which) | (tail_lane == which + experts)
            prob = jnp.sum(jnp.where(hits, picked[mine, D:], 0.0), axis=1, keepdims=True)
            prob_v[to, :] = jnp.broadcast_to(prob, (capacity, 128))
        return carry

    for one in near:
        one.wait()
    far = [
        copy(sec_b, sec_v.at[pl.ds(half, half)], sem_in, 1),
        copy(cot_b, cot_v.at[pl.ds(half, half)], sem_in, 3),
    ]
    in_sin = copy(sin_hbm, sin_v, sem_in, 7)
    in_sdn = copy(sdn_hbm, sdn_v, sem_in, 8)
    lax.fori_loop(0, blocks // 2, gather, 0, unroll=True)
    for one in far:
        one.wait()
    in_gate = copy(gate_hbm, gate_v, sem_in, 4)
    in_up = copy(up_hbm, up_v, sem_in, 5)
    in_down = copy(down_hbm, down_v, sem_in, 6)
    lax.fori_loop(blocks // 2, blocks, gather, 0, unroll=True)
    outs = []
    for e in range(local_experts):
        mine = pl.ds(e * per, per)
        outs.append(copy(x_v.at[mine], x_out.at[e, pl.ds(base, per)], sem_out, 2 * e))
        outs.append(copy(c_v.at[mine], c_out.at[e, pl.ds(base, per)], sem_out, 2 * e + 1))
    used = 2 * local_experts

    in_sin.wait()
    in_sdn.wait()
    shared = mm(sec_v[:, :D], sin_v[...])
    s_gate, s_up = shared[:, :wpad], shared[:, wpad:]
    s_sigma = jax.nn.sigmoid(s_gate)
    s_silu = s_gate * s_sigma
    s_grad = mm_nt(cot_v[:, :D], sdn_v[...])
    sact_v[...] = (s_silu * s_up).astype(BF)
    slow_v[:, :wpad] = (s_grad * s_up * (s_sigma * (1.0 + s_gate * (1.0 - s_sigma)))).astype(BF)
    slow_v[:, wpad:] = (s_grad * s_silu).astype(BF)
    sgp_v[...] = mm_tn(slow_v[...], sec_v[:, :D])
    sdp_v[...] = mm_tn(sact_v[...], cot_v[:, :D])
    cot_v[:, :D] = mm(sact_v[...], sdn_v[...]).astype(BF)
    sec_v[:, :D] = mm_nt(slow_v[...], sin_v[...]).astype(BF)
    outs.append(copy(sgp_v, sg_out, sem_out, used))
    outs.append(copy(sdp_v, sd_out, sem_out, used + 1))
    used += 2

    in_gate.wait()
    in_up.wait()
    in_down.wait()
    in_tail = z_v.shape[2] - D
    pair_lane = lax.broadcasted_iota(jnp.int32, (per, in_tail), 1)
    for e in range(local_experts):
        mine = pl.ds(e * per, per)
        x_e, c_e = x_v[mine, :], c_v[mine, :]
        gate = mm_nt(x_e, gate_v[e])
        up = mm_nt(x_e, up_v[e])
        pull = mm_nt(c_e, down_v[e])
        prob = prob_v[mine, :1]
        sigma = jax.nn.sigmoid(gate)
        silu = gate * sigma
        act = silu * up
        pair = jnp.sum(pull * act, axis=1, keepdims=True)
        pull = pull * prob
        gg_v[e] = (pull * up * (sigma * (1.0 + gate * (1.0 - sigma)))).astype(BF)
        ug_v[e] = (pull * silu).astype(BF)
        aw_v[e] = (act * prob).astype(BF)
        outs.append(copy(aw_v.at[e], aw_out.at[e, pl.ds(base, per)], sem_out, used))
        outs.append(copy(gg_v.at[e], gg_out.at[e, pl.ds(base, per)], sem_out, used + 1))
        outs.append(copy(ug_v.at[e], ug_out.at[e, pl.ds(base, per)], sem_out, used + 2))
        used += 3
        y = mm(aw_v[e], down_v[e]).astype(BF)
        y_v[:, e * capacity : (e + 1) * capacity, :] = y.reshape(blocks, capacity, D)
        zed = (mm(gg_v[e], gate_v[e]) + mm(ug_v[e], up_v[e])).astype(BF)
        z_v[:, e * capacity : (e + 1) * capacity, :D] = zed.reshape(blocks, capacity, D)
        pairs = jnp.where(pair_lane == first_expert + e, pair, 0.0).astype(BF)
        z_v[:, e * capacity : (e + 1) * capacity, D:] = pairs.reshape(blocks, capacity, in_tail)

    def block_copies(b):
        moves = []
        for i, (to_in, to_out) in enumerate(((in_a, out_a), (in_b, out_b))):
            at = pl.ds(pl.multiple_of(b * rows, rows), rows)
            from_at = pl.ds(pl.multiple_of(i * half + b * rows, rows), rows)
            moves.append(pltpu.make_async_copy(sec_v.at[from_at], to_in.at[at], sem_block.at[i, 0, b]))
            moves.append(
                pltpu.make_async_copy(cot_v.at[from_at, pl.ds(0, D)], to_out.at[at], sem_block.at[i, 1, b])
            )
        return moves

    def scatter(b, carry):
        for i in range(2):
            at = pl.ds(pl.multiple_of(i * half + b * rows, rows), rows)
            choose = choose_v[at, :]
            which = i * (half // rows) + b
            cot_v[at, :D] = (mm(choose, y_v[which]) + cot_v[at, :D].astype(F32)).astype(BF)
            back = mm(choose, z_v[which])
            sec_v[at, :D] = (back[:, :D] + sec_v[at, :D].astype(F32)).astype(BF)
            sec_v[at, D:] = back[:, D:].astype(BF)
        for move in block_copies(b):
            move.start()
        return carry

    lax.fori_loop(0, half // rows, scatter, 0, unroll=True)
    for b in range(half // rows):
        for move in block_copies(b):
            move.wait()
    for one in outs:
        one.wait()


def expert_group(place, sec, cot, weights, kept, capacity, rows, experts, groups):
    gate, up, down, sin, sdn = weights
    local_experts, hidden, _ = gate.shape
    half = sec[0].shape[0]
    tokens = 2 * half
    blocks = tokens // rows
    per = blocks * capacity
    slots = per * groups
    wpad = sdn.shape[0]
    in_width = D + lanes(experts)
    big = (local_experts, slots)
    shapes = [
        jax.ShapeDtypeStruct((*big, D), BF),
        jax.ShapeDtypeStruct((*big, D), BF),
        jax.ShapeDtypeStruct((*big, hidden), BF),
        jax.ShapeDtypeStruct((*big, hidden), BF),
        jax.ShapeDtypeStruct((*big, hidden), BF),
        jax.ShapeDtypeStruct((half, D), BF),
        jax.ShapeDtypeStruct((half, D), BF),
        jax.ShapeDtypeStruct((half, in_width), BF),
        jax.ShapeDtypeStruct((half, in_width), BF),
        jax.ShapeDtypeStruct((2 * wpad, D), F32),
        jax.ShapeDtypeStruct((wpad, D), F32),
    ]
    first = kept is None
    operands = [place, *sec, *cot, gate, up, down, sin, sdn] + ([] if first else list(kept))
    any_space = pl.BlockSpec(memory_space=pl.ANY)
    smem = pl.BlockSpec(memory_space=pltpu.SMEM)
    return pl.pallas_call(
        functools.partial(expert_kernel, local_experts, capacity, rows, experts, first),
        out_shape=shapes,
        in_specs=[smem] + [any_space] * (len(operands) - 1),
        out_specs=[any_space] * len(shapes),
        scratch_shapes=[
            pltpu.VMEM((tokens, sec[0].shape[1]), BF),
            pltpu.VMEM((tokens, cot[0].shape[1]), BF),
            pltpu.VMEM(gate.shape, BF),
            pltpu.VMEM(up.shape, BF),
            pltpu.VMEM(down.shape, BF),
            pltpu.VMEM(sin.shape, BF),
            pltpu.VMEM(sdn.shape, BF),
            pltpu.VMEM((local_experts * per, D), BF),
            pltpu.VMEM((local_experts * per, D), BF),
            pltpu.VMEM((blocks, local_experts * capacity, D), BF),
            pltpu.VMEM((blocks, local_experts * capacity, in_width), BF),
            pltpu.VMEM((local_experts, per, hidden), BF),
            pltpu.VMEM((local_experts, per, hidden), BF),
            pltpu.VMEM((local_experts, per, hidden), BF),
            pltpu.VMEM((tokens, local_experts * capacity), BF),
            pltpu.VMEM((local_experts * per, 128), F32),
            pltpu.VMEM((tokens, wpad), BF),
            pltpu.VMEM((tokens, 2 * wpad), BF),
            pltpu.VMEM((2 * wpad, D), F32),
            pltpu.VMEM((wpad, D), F32),
            pltpu.SemaphoreType.DMA((9,)),
            pltpu.SemaphoreType.DMA((5 * local_experts + 2,)),
            pltpu.SemaphoreType.DMA((2, 2, half // rows)),
        ],
        input_output_aliases={} if first else {10 + i: i for i in range(5)},
        compiler_params=pltpu.CompilerParams(vmem_limit_bytes=63 * 1024 * 1024),
        cost_estimate=pl.CostEstimate(flops=1 << 20, bytes_accessed=1 << 16, transcendentals=0),
    )(*operands)


def turn(values, cosine, sine):
    lane = lax.broadcasted_iota(jnp.int32, values.shape, 1)
    partner = jnp.where(
        lane % DR < DR // 2, pltpu.roll(values, 2 * DR - DR // 2, 1), pltpu.roll(values, DR // 2, 1)
    )
    return values * cosine + partner * sine


def score_block(i, block, image, scores):
    row = lax.broadcasted_iota(jnp.int32, scores.shape, 0) + i * block
    column = lax.broadcasted_iota(jnp.int32, scores.shape, 1)
    allowed = (column <= row) | ((column >= i * block) & image)
    return jnp.where(allowed, scores * ((DN + DR) ** (-0.5)), NEGATIVE)


def head_part(values, h):
    lane = lax.broadcasted_iota(jnp.int32, values.shape, 1)
    return jnp.where(lane // DR == h, values.astype(F32), 0.0).astype(BF)


def attend_kernel(
    heads, rows, place, seq, gain, lgain, wq, wd, wup, cos, sin, out, first, q_out, lat_out, kr_out, ex_out, own_out, down_v
):
    block = PIECE
    nope = heads * DN
    for i in range(seq.shape[0] // block):
        at = slice(i * block, (i + 1) * block)
        values = seq[at, :D].astype(F32)
        low = (values * rms_parts(values) * gain[...]).astype(BF)
        first[at, :] = low
        q = mm(low, wq[...])
        down = mm(low, wd[...])
        down_v[at, :] = down
        latent = down[:, :KVR]
        lat = (latent * rms_parts(latent) * lgain[...]).astype(BF)
        lat_out[at, :] = lat
        ex_out[at, :] = mm(lat, wup[...]).astype(BF)
        turned = turn(down[:, KVR : KVR + 2 * DR], cos[at, :], sin[at, :])
        lane = lax.broadcasted_iota(jnp.int32, turned.shape, 1)
        turned = jnp.where(lane < DR, turned, 0.0)
        kr_out[at, :] = (turned + pltpu.roll(turned, DR, 1)).astype(BF)
        q_rope = turn(q[:, nope:], cos[at, :], sin[at, :]).astype(BF)
        q_out[at, :nope] = q[:, :nope].astype(BF)
        q_out[at, nope:] = q_rope
        image = seq[at, D : D + 128][:, :1].astype(F32) > 0
        n = (i + 1) * block
        for h in range(heads):
            mine = slice(h * (DN + DV), h * (DN + DV) + DN)
            scores = mm_nt(q_out[at, h * DN : (h + 1) * DN], ex_out[:n, mine])
            scores = scores + mm_nt(head_part(q_rope, h), kr_out[:n, :])
            scores = score_block(i, block, image, scores)
            weight = jnp.exp(scores - jnp.max(scores, axis=1, keepdims=True))
            weight = weight / jnp.sum(weight, axis=1, keepdims=True)
            value = ex_out[:n, h * (DN + DV) + DN : (h + 1) * (DN + DV)]
            out[at, h * DV : (h + 1) * DV] = mm(weight.astype(BF), value).astype(BF)
    own_out[...] = down_v[pl.ds(pl.multiple_of(place[0] * rows, rows), rows), :]


def attend(place, seq, gain, lgain, wq, wd, wup, cos, sin, heads, rows):
    length = seq.shape[0]
    shapes = [
        jax.ShapeDtypeStruct((length, heads * DV), BF),
        jax.ShapeDtypeStruct((length, D), BF),
        jax.ShapeDtypeStruct((length, wq.shape[1]), BF),
        jax.ShapeDtypeStruct((length, KVR), BF),
        jax.ShapeDtypeStruct((length, 2 * DR), BF),
        jax.ShapeDtypeStruct((length, wup.shape[1]), BF),
        jax.ShapeDtypeStruct((rows, wd.shape[1]), F32),
    ]
    vmem = pl.BlockSpec(memory_space=pltpu.VMEM)
    return pl.pallas_call(
        functools.partial(attend_kernel, heads, rows),
        out_shape=shapes,
        in_specs=[pl.BlockSpec(memory_space=pltpu.SMEM)] + [vmem] * 8,
        out_specs=[vmem] * len(shapes),
        scratch_shapes=[pltpu.VMEM((length, wd.shape[1]), F32)],
        compiler_params=pltpu.CompilerParams(vmem_limit_bytes=56 * 1024 * 1024),
        cost_estimate=pl.CostEstimate(flops=1 << 20, bytes_accessed=1 << 16, transcendentals=0),
    )(place, seq, gain, lgain, wq, wd, wup, cos, sin)


def attend_back_kernel(
    heads, place, grad, flags, first, q, kr, ex, lat, wq, wup, cos, sin,
    gain_out, first_keep, first_send, lat_keep, lat_send, pack_out,
    dk_v, dv_v, dr_v, qg_v, eg_v,
):
    block = PIECE
    nope = heads * DN
    length = first.shape[0]
    half = length // 2
    scale = (DN + DR) ** (-0.5)
    dk_v[...] = jnp.zeros_like(dk_v)
    dv_v[...] = jnp.zeros_like(dv_v)
    dr_v[...] = jnp.zeros_like(dr_v)
    for i in range(length // block):
        at = slice(i * block, (i + 1) * block)
        n = (i + 1) * block
        image = flags[at, :1].astype(F32) > 0
        rope_grad = jnp.zeros((block, 2 * DR), F32)
        for h in range(heads):
            mine = slice(h * (DN + DV), h * (DN + DV) + DN)
            value = ex[:n, h * (DN + DV) + DN : (h + 1) * (DN + DV)]
            q_nope = q[at, h * DN : (h + 1) * DN]
            q_rope = head_part(q[at, nope:], h)
            scores = mm_nt(q_nope, ex[:n, mine]) + mm_nt(q_rope, kr[:n, :])
            scores = score_block(i, block, image, scores)
            weight = jnp.exp(scores - jnp.max(scores, axis=1, keepdims=True))
            weight = weight / jnp.sum(weight, axis=1, keepdims=True)
            upstream = grad[at, h * DV : (h + 1) * DV]
            dprob = mm_nt(upstream, value)
            dv_v[:n, h * DV : (h + 1) * DV] += mm_tn(weight.astype(BF), upstream)
            inner = jnp.sum(weight * dprob, axis=1, keepdims=True)
            back = (weight * (dprob - inner)).astype(BF)
            qg_v[at, h * DN : (h + 1) * DN] = (mm(back, ex[:n, mine]) * scale).astype(BF)
            turned = mm(back, kr[:n, :])
            lane = lax.broadcasted_iota(jnp.int32, turned.shape, 1)
            rope_grad = jnp.where(lane // DR == h, turned * scale, rope_grad)
            dk_v[:n, h * DN : (h + 1) * DN] += mm_tn(back, q_nope)
            dr_v[:n, :] += mm_tn(back, q_rope)
        qg_v[at, nope:] = turn(rope_grad, cos[at, :], -sin[at, :]).astype(BF)
    for h in range(heads):
        mine = slice(h * (DN + DV), h * (DN + DV) + DN)
        eg_v[:, mine] = (dk_v[:, h * DN : (h + 1) * DN] * scale).astype(BF)
        eg_v[:, h * (DN + DV) + DN : (h + 1) * (DN + DV)] = dv_v[:, h * DV : (h + 1) * DV].astype(BF)
    key_rope = dr_v[...]
    key_rope = (key_rope + pltpu.roll(key_rope, DR, 1)) * scale
    dr_v[...] = key_rope
    keep = pl.ds(pl.multiple_of(place[1] * half, half), half)
    send = pl.ds(pl.multiple_of((1 - place[1]) * half, half), half)
    total = jnp.zeros((1, D), F32)
    for at, to_lat, to_first in ((send, lat_send, first_send), (keep, lat_keep, first_keep)):
        to_lat[:, :KVR] = mm_nt(eg_v[at, :], wup[...]).astype(BF)
        to_lat[:, KVR:] = dr_v[at, :].astype(BF)
        part = mm_nt(qg_v[at, :], wq[...])
        to_first[...] = part.astype(BF)
        total = total + jnp.sum(part * first[at, :].astype(F32), axis=0, keepdims=True)
    gain_out[...] = total
    owners, pack_rows, _ = pack_out.shape
    wide = wq.shape[1]
    q_rows = D // owners
    pack_out[:, :q_rows, :wide] = mm_tn(first[...], qg_v[...]).astype(BF).reshape(owners, q_rows, wide)
    pack_out[:, :q_rows, wide:] = jnp.zeros((owners, q_rows, pack_out.shape[2] - wide), BF)
    pack_out[:, q_rows:, :] = mm_tn(lat[...], eg_v[...]).astype(BF).reshape(owners, pack_rows - q_rows, -1)


def attend_back(place, grad, flags, first, q, kr, ex, lat, wq, wup, cos, sin, heads, owners):
    length = first.shape[0]
    half = length // 2
    wide = KVR + 2 * DR
    shapes = [
        jax.ShapeDtypeStruct((1, D), F32),
        jax.ShapeDtypeStruct((half, D), BF),
        jax.ShapeDtypeStruct((half, D), BF),
        jax.ShapeDtypeStruct((half, wide), BF),
        jax.ShapeDtypeStruct((half, wide), BF),
        jax.ShapeDtypeStruct((owners, (D + KVR) // owners, wup.shape[1]), BF),
    ]
    vmem = pl.BlockSpec(memory_space=pltpu.VMEM)
    return pl.pallas_call(
        functools.partial(attend_back_kernel, heads),
        out_shape=shapes,
        in_specs=[pl.BlockSpec(memory_space=pltpu.SMEM)] + [vmem] * 11,
        out_specs=[vmem] * len(shapes),
        scratch_shapes=[
            pltpu.VMEM((length, heads * DN), F32),
            pltpu.VMEM((length, heads * DV), F32),
            pltpu.VMEM((length, 2 * DR), F32),
            pltpu.VMEM((length, q.shape[1]), BF),
            pltpu.VMEM((length, ex.shape[1]), BF),
        ],
        compiler_params=pltpu.CompilerParams(vmem_limit_bytes=56 * 1024 * 1024),
        cost_estimate=pl.CostEstimate(flops=1 << 20, bytes_accessed=1 << 16, transcendentals=0),
    )(place, grad, flags, first, q, kr, ex, lat, wq, wup, cos, sin)


def on_device(
    tokens,
    attention_norm,
    query_weight,
    latent_down,
    latent_norm,
    latent_up,
    output_weight,
    post_norm,
    shared_gate,
    shared_up,
    shared_down,
    router_weight,
    expert_gate,
    expert_up,
    expert_down,
    image_piece_index,
    routes,
    cotangent,
):
    rows = tokens.shape[0]
    c_size, k_size, z_size = (lax.axis_size(a) for a in EVERY)
    c, k, z = (lax.axis_index(a) for a in EVERY)
    column_size = k_size * z_size
    device_count = c_size * column_size
    local_experts = expert_gate.shape[0]
    experts = router_weight.shape[1]
    capacity = rows * TOPK * 4 // (3 * experts)
    length = column_size * rows
    heads = H // column_size
    width = shared_down.shape[0]
    score_scale = (DN + DR) ** (-0.5)
    weight_rows = query_weight.shape[0]
    up_rows = latent_up.shape[0]

    paired = H == 4 * c_size and heads == 2 and column_size == 8

    def by_owner(array, n):
        if paired:
            array = array.reshape(-1, 2, 2, 4, n).transpose(0, 3, 1, 2, 4)
        return array.reshape(-1, column_size, heads * n)

    def by_head(array, n):
        if paired:
            array = array.reshape(-1, 4, 2, 2, n).transpose(0, 2, 3, 1, 4)
        return array.reshape(-1, H * n)

    flag = (image_piece_index > 0).astype(BF)[:, None]
    expert_ids = jnp.arange(experts, dtype=jnp.int32)
    named = jnp.any(routes[:, :, None] == expert_ids[None, None, :], axis=1)

    out_mine = in_order(gather_z(output_weight.astype(BF)), z)
    extra = -(-weight_rows // 8) * 8 + 8 - weight_rows
    down_width = KVR + DR
    small_width = lanes(max(down_width + experts + 8, weight_rows))
    gains = jnp.stack(
        [attention_norm, post_norm, jnp.pad(latent_norm, (0, weight_rows - latent_norm.shape[0]))]
    )
    small = jnp.concatenate([latent_down, router_weight], axis=1).astype(BF)
    small = jnp.pad(small, ((0, 0), (0, small_width - small.shape[1])))
    gains = jnp.pad(gains.astype(BF), ((0, extra - 3), (0, small_width - weight_rows)))
    small = jnp.concatenate([small, gains], axis=0)
    q_width = heads * (DN + DR)
    kv_width = heads * (DN + DV)
    q_out = by_owner(query_weight.astype(BF), DN + DR).transpose(1, 0, 2)
    q_out = q_out.reshape(column_size, weight_rows, heads, DN + DR)
    q_out = jnp.concatenate(
        [q_out[..., :DN].reshape(column_size, weight_rows, -1), q_out[..., DN:].reshape(column_size, weight_rows, -1)],
        axis=2,
    )
    q_out = jnp.pad(q_out, ((0, 0), (0, 0), (0, kv_width - q_width)))
    up_out = by_owner(latent_up.astype(BF), DN + DV).transpose(1, 0, 2)
    head_pack = jnp.concatenate([q_out, up_out], axis=1)
    head_pack = lax.all_to_all(head_pack, COLUMN, split_axis=0, concat_axis=0, tiled=True)
    token_units = gather_z(after(widen(tokens, flag), head_pack))
    cot_units = gather_z(after(widen(cotangent, named), *token_units[1:]))
    head_pack = [head_pack] + [swap(head_pack, "c", d) for d in range(1, c_size)]
    small, small_recv = gather_weight(small)
    mine = in_order(after_all(token_units, *head_pack[1:], *small_recv), z)
    sequence = in_order([mine, swap(mine, "k", 1)], k).reshape(length, -1)
    small = small.reshape(device_count, weight_rows + extra, small_width)
    full_small = small[:, :weight_rows].reshape(D, small_width)
    full_router = full_small[:, down_width : down_width + experts]
    full_gains = small[:, weight_rows : weight_rows + 3, :weight_rows].astype(F32)
    attn_gain = full_gains[:, 0].reshape(D)
    post_gain = full_gains[:, 1].reshape(D)
    latent_gain = full_gains[:, 2, : latent_norm.shape[0]].reshape(KVR)
    out_mine = after(out_mine, *head_pack[1:])
    out_planes = [out_mine] + [swap(out_mine, "c", d) for d in range(1, c_size)]
    head_pack = in_order(head_pack, c)
    head_query = head_pack[:, :, :weight_rows, :q_width].reshape(D, q_width)
    head_up = head_pack[:, :, weight_rows:].reshape(KVR, kv_width)
    shared_pack = jnp.concatenate(
        [
            shared_gate.astype(BF).reshape(weight_rows, device_count, width),
            shared_up.astype(BF).reshape(weight_rows, device_count, width),
        ],
        axis=2,
    ).transpose(1, 0, 2)
    shared_in = lax.all_to_all(after(shared_pack, *token_units[1:]), EVERY, split_axis=0, concat_axis=0, tiled=True)
    shared_low = shared_down.astype(BF)

    places = jnp.arange(length, dtype=F32)
    frequency = ROPE_BASE ** (-2.0 * jnp.arange(DR // 2, dtype=F32) / DR)
    angles = places[:, None] * frequency[None, :]
    cosine, sine = jnp.cos(angles), jnp.sin(angles)
    cosine_wide = jnp.tile(cosine, (1, 4))
    sine_wide = jnp.tile(jnp.concatenate([-sine, sine], axis=1), (1, 2))
    here = k * z_size + z

    def own_rows(array):
        return lax.dynamic_slice_in_dim(array, here * rows, rows, axis=0)

    spot = jnp.stack([here, k]).astype(jnp.int32)
    heads_out, first_low, query_low, latent_low, rope_low, expanded, down_raw = attend(
        spot, sequence, attn_gain[None], latent_gain[None], head_query, full_small, head_up,
        cosine_wide, sine_wide, heads, rows,
    )
    own_values = tokens.astype(F32)
    own_scale = rms_parts(own_values)
    own_first_low = (own_values * own_scale * attn_gain).astype(BF)
    latent_raw = down_raw[:, :KVR]
    latent_scale = rms_parts(latent_raw)

    def heads_to_tokens(array):
        n = array.shape[1]
        moved = lax.all_to_all(
            array.reshape(column_size, rows, n), COLUMN, split_axis=0, concat_axis=0, tiled=True
        )
        return by_head(moved.transpose(1, 0, 2), n // heads)

    def tokens_to_heads(array):
        n = array.shape[1] // H
        moved = lax.all_to_all(
            by_owner(array, n).transpose(1, 0, 2), COLUMN, split_axis=0, concat_axis=0, tiled=True
        )
        return moved.reshape(length, heads * n)

    shared_in, *cot_units = after_all([shared_in, *cot_units], heads_out)
    cot_own = jnp.concatenate(cot_units, axis=0)
    shared_in = shared_in.reshape(D, 2 * width)
    room = ((0, 0), (0, lanes(width) - width))
    shared_in = jnp.concatenate(
        [jnp.pad(shared_in[:, :width], room), jnp.pad(shared_in[:, width:], room)], axis=1
    )
    out_planes = in_order(after_all(out_planes, heads_out, cot_own), c)
    full_out = in_order([out_planes, swap(out_planes, "k", 1)], k)
    full_out = full_out.transpose(1, 0, 2, 3, 4).reshape(D, D)

    def plane_groups(own):
        near = [swap(own, "c", d) for d in range(1, c_size - 1)]
        return [own, *near, swap(after(own, *near), "c", c_size - 1)]

    cot_groups = [cot_own] + [swap(cot_own, "c", d) for d in range(1, c_size)]
    heads_low = after(heads_to_tokens(after(heads_out, cot_own, shared_in)), full_out)
    residual = tokens.astype(F32) + mm(heads_low, full_out)
    second_scale = rms_parts(residual)
    second_low = (residual * second_scale * post_gain).astype(BF)
    router_probs = jax.nn.softmax(mm(second_low, full_router), axis=-1)

    probs_high = router_probs.astype(BF)
    probs_rest = (router_probs - probs_high.astype(F32)).astype(BF)
    second_own = jnp.concatenate(
        gather_z(widen(second_low, jnp.concatenate([probs_high, probs_rest], axis=1))), axis=0
    )
    second_own = after(second_own, *cot_groups[1:])
    second_groups = plane_groups(second_own)
    pair = lambda group: (group, swap(group, "k", 1))
    cot_groups = [pair(g) for g in cot_groups]
    wpad = lanes(width)
    place = jnp.stack([(c * k_size + k) * local_experts, jnp.zeros((), jnp.int32)]).astype(jnp.int32)
    shared_rows = jnp.pad(shared_low, ((0, wpad - width), (0, 0)))
    weights = (
        jnp.swapaxes(expert_gate, 1, 2),
        jnp.swapaxes(expert_up, 1, 2),
        expert_down,
        shared_in,
        shared_rows,
    )
    kept, sg_parts, sd_parts, sums, out_sums, marks = None, [], [], [], [], []
    arrived = []
    for d in range(c_size):
        where = place.at[1].set(d)
        group = second_groups[d]
        if d == 1:
            group, *second_groups[2:-1] = after_all([group, *second_groups[2:-1]], marks[0])
        if d == c_size - 2:
            second_groups[-1] = after(second_groups[-1], marks[d - 1])
            where = after(where, second_groups[-1])
        if d > 1:
            where = after(where, sums[d - 1])
        results = list(
            expert_group(
                where, pair(group), cot_groups[d], weights, kept, capacity, rows, experts, c_size
            )
        )
        kept = results[:5]
        marks.append(results[10])
        if d == c_size - 1:
            results[7] = after(results[7], *arrived)
        sums.append(core_sum(*results[7:9], d))
        if d:
            arrived.append(swap(sums[d], "c", d))
        if d == c_size - 1:
            kept = after_all(kept, *arrived[:-1], sums[d])
            results[6] = after(results[6], arrived[-1])
        out_sums.append(core_sum(*results[5:7], d))
        sg_parts.append(results[9])
        sd_parts.append(results[10])
    plane = functools.reduce(lambda total, block: total + block.astype(F32), arrived, sums[0])
    expert_in, cot_in, act_weighted, gate_grad, up_grad = kept
    ein = lambda spec, a, b: jnp.einsum(spec, a, b, preferred_element_type=F32)
    expert_down_grad = ein("esf,esd->efd", act_weighted, cot_in)
    expert_gate_grad = jnp.swapaxes(ein("esf,esd->efd", gate_grad, expert_in), 1, 2)
    expert_up_grad = jnp.swapaxes(ein("esf,esd->efd", up_grad, expert_in), 1, 2)
    plane = after(plane, expert_down_grad, expert_gate_grad, expert_up_grad)
    second_sum = scatter_z(z_units(plane, rows))
    out_near = [swap(after(out_sums[d], *arrived), "c", d) for d in range(1, c_size - 1)]
    second_sum = after(second_sum, *out_near, out_sums[-1])
    out_far = swap(after(out_sums[-1], *out_near), "c", c_size - 1)
    probs_grad = second_sum[:, D : D + experts]
    logits_grad = (
        router_probs * (probs_grad - jnp.sum(router_probs * probs_grad, axis=-1, keepdims=True))
    ).astype(BF)
    second_grad = second_sum[:, :D] + mm_nt(logits_grad, full_router)
    norm_part, post_terms = rms_back(residual, second_scale, post_gain, second_grad)
    residual_grad = cotangent.astype(F32) + norm_part
    attn_grad_low = residual_grad.astype(BF)
    heads_grad = tokens_to_heads(mm_nt(attn_grad_low, full_out).astype(BF))
    output_pieces = core_pieces(mm_tn(heads_low, attn_grad_low).astype(BF))

    gain_part, first_keep, first_send, latent_keep, latent_send, head_grad = attend_back(
        after(spot, *output_pieces), heads_grad, sequence[:, D:], first_low, query_low,
        rope_low, expanded, latent_low, head_query, head_up, cosine_wide, sine_wide, heads, device_count,
    )
    def column_sum(keep, send):
        summed = keep.astype(F32) + swap(send, "k", 1).astype(F32)
        summed = summed.reshape(z_size, rows, keep.shape[1])
        return scatter_z([pick(summed, z ^ d) for d in range(z_size)])

    latent_sum = column_sum(latent_keep, after(latent_send, out_far))
    shared_in_grad = sum(sg_parts[1:], sg_parts[0])
    shared_in_grad = jnp.concatenate(
        [shared_in_grad[:width], shared_in_grad[wpad : wpad + width]], axis=0
    ).astype(BF)
    shared_down_grad = sum(sd_parts[1:], sd_parts[0])[:width]
    shared_back = shared_in_grad.reshape(2 * width, c_size, column_size, weight_rows).transpose(2, 1, 3, 0)
    shared_back = lax.all_to_all(
        after(shared_back, latent_keep), COLUMN, split_axis=0, concat_axis=0, tiled=True
    )
    latent_raw_grad, latent_terms = rms_back(
        latent_raw, latent_scale, latent_gain, latent_sum[:, :KVR]
    )
    rope_raw_grad = rotate(
        latent_sum[:, KVR:down_width], own_rows(cosine), own_rows(sine), -1.0
    )
    down_grad_low = jnp.concatenate([latent_raw_grad, rope_raw_grad], axis=-1).astype(BF)
    first_own = mm_nt(down_grad_low, full_small[:, :down_width])
    attn_gain_grad = gain_part[0] / attn_gain + jnp.sum(
        first_own * (own_values * own_scale), axis=0
    )
    gain_grads = jnp.stack(
        [
            attn_gain_grad,
            jnp.sum(post_terms, axis=0),
            jnp.pad(
                jnp.sum(latent_terms, axis=0).reshape(device_count, latent_norm.shape[0]),
                ((0, 0), (0, weight_rows - latent_norm.shape[0])),
            ).reshape(D),
        ]
    )
    first_gain = down_width + experts
    small_right = jnp.zeros((2 * rows + 8, small_width), BF)
    small_right = small_right.at[:rows, :down_width].set(down_grad_low)
    small_right = small_right.at[rows : 2 * rows, down_width:first_gain].set(logits_grad)
    ones = (jnp.arange(8)[:, None] == jnp.arange(small_width)[None, :] - first_gain).astype(BF)
    small_right = small_right.at[2 * rows :].set(ones)
    small_left = jnp.concatenate(
        [own_first_low, second_low, jnp.pad(gain_grads, ((0, 5), (0, 0))).astype(BF)], axis=0
    )
    output_near = [swap(output_pieces[d], "c", d) for d in range(1, c_size - 1)]
    small_pieces = core_pieces(mm_tn(small_left, small_right).astype(BF))
    first_sum = column_sum(first_keep, first_send)
    first_sum, *small_pieces = after_all([first_sum, *small_pieces], *output_near)
    out_plane = functools.reduce(
        lambda total, block: total + block.astype(F32),
        after_all([*out_near, out_far], first_sum),
        out_sums[0],
    )
    out_units = z_units(out_plane, rows)
    out_units = out_units[:1] + [swap(unit.astype(BF), "z", d) for d, unit in enumerate(out_units) if d]
    output_moved = [
        *output_near, swap(after(output_pieces[-1], *output_near), "c", c_size - 1)
    ]
    head_grad = head_grad.reshape(c_size, column_size, weight_rows + up_rows, kv_width)
    head_moved = [swap(pick(head_grad, c ^ d), "c", d) for d in range(1, c_size)]
    small_plane, _ = plane_sum(small_pieces, *head_moved)
    output_plane = functools.reduce(
        lambda total, block: total + block.astype(F32),
        after_all(output_moved, small_plane),
        output_pieces[0],
    )
    shared_back = after(shared_back, small_plane)
    shared_moved = [
        swap(lax.dynamic_index_in_dim(shared_back, c ^ d, axis=1, keepdims=False), "c", d)
        for d in range(1, c_size)
    ]
    first_grad = first_sum + first_own
    out_sum = functools.reduce(
        lambda total, block: total + block.astype(F32), after_all(out_units[1:], first_grad), out_units[0]
    )
    layer_out = (residual + out_sum).astype(BF)
    first_norm_grad, _ = rms_back(own_values, own_scale, attn_gain, first_grad)
    tokens_grad = residual_grad + first_norm_grad
    own_both = z_sum(jnp.concatenate([output_plane, small_plane], axis=1))
    own_output, own_small = own_both[:, :D], own_both[:, D:]
    shared_back = in_order(
        [
            lax.dynamic_index_in_dim(shared_back, c, axis=1, keepdims=False),
            *after_all(shared_moved, own_both),
        ],
        c,
    ).reshape(device_count, weight_rows, 2 * width).transpose(1, 0, 2)
    head_sum = pick(head_grad, c).astype(F32)
    for block in after_all(head_moved, small_plane):
        head_sum = head_sum + block.astype(F32)
    head_sum = lax.all_to_all(head_sum.astype(BF), COLUMN, split_axis=0, concat_axis=0, tiled=True)
    own_query = head_sum[:, :weight_rows, :q_width].transpose(1, 0, 2)
    own_query = jnp.concatenate(
        [
            own_query[..., : heads * DN].reshape(weight_rows, column_size, heads, DN),
            own_query[..., heads * DN :].reshape(weight_rows, column_size, heads, DR),
        ],
        axis=3,
    )
    own_query = by_head(own_query.reshape(weight_rows, column_size, q_width), DN + DR)
    own_up = by_head(head_sum[:, weight_rows:].transpose(1, 0, 2), DN + DV)
    own_gate = shared_back[:, :, :width].reshape(weight_rows, -1)
    own_shared_up = shared_back[:, :, width:].reshape(weight_rows, -1)
    return (
        layer_out,
        tokens_grad,
        own_small[:, first_gain],
        own_query.astype(F32),
        own_small[:, :down_width],
        own_small[: latent_norm.shape[0], first_gain + 2],
        own_up.astype(F32),
        own_output,
        own_small[:, first_gain + 1],
        own_gate.astype(F32),
        own_shared_up.astype(F32),
        shared_down_grad,
        own_small[:, down_width:first_gain],
        expert_gate_grad,
        expert_up_grad,
        expert_down_grad,
    )


def solution(mesh):
    expert_size, z_size = mesh.devices.shape
    fine = Mesh(mesh.devices.reshape(expert_size // 2, 2, z_size), EVERY)
    row, flat = P(EVERY, None), P(EVERY)
    wide, tall = P(("c", "k"), None, "z"), P(("c", "k"), "z", None)
    return jax.shard_map(
        on_device,
        mesh=fine,
        in_specs=(row, flat, row, row, flat, row, row, flat, row, row, row, row)
        + (wide, wide, tall, flat, row, row),
        out_specs=(row, row, flat, row, row, flat, row, row, flat, row, row, row, row)
        + (wide, wide, tall),
        check_vma=False,
    )
```
